128 devices in a mesh: fine: 4 (over y_lo, core), coarse: 32 (over x, y_hi, z).
Axes of the slice: x: 4, y: 4 (y_hi: 2, y_lo: 2; y = y_hi * 2 + y_lo), z: 4, core: 2. Of those that a mesh axis runs over, the one named last changes fastest.
Arguments:
- node_state: bfloat16 [131072, 128], P(('fine', 'coarse')), may hold values from -6 to 6
- fine_edge_state: bfloat16 [524288, 128], P(('fine', 'coarse')), may hold values from -6 to 6
- coarse_edge_state: bfloat16 [81920, 128], P(('fine', 'coarse')), may hold values from -6 to 6
- fine_src: int32 [524288], P(('fine', 'coarse')), may hold values from 0 to 1535
- fine_dst: int32 [524288], P(('fine', 'coarse')), may hold values from 0 to 1023
- halo_rows: int32 [512, 128], P(('fine', 'coarse')), may hold values from 0 to 1023
- block_owner: int32 [8192, 1], P(('fine', 'coarse')), may hold values from 0 to 31; in each aligned block of 64 rows (0 to 63, 64 to 127, ...) at most 5 rows name the same one
- coarse_src: int32 [81920], P(('fine', 'coarse')), may hold values from 0 to 479
- coarse_dst: int32 [81920], P(('fine', 'coarse')), may hold values from 0 to 159
- cotangent: bfloat16 [131072, 128], P(('fine', 'coarse')), may hold values from -6 to 6
- fine_edge_in: bfloat16 [2, 384, 128], replicated, may hold values from -0.3125 to 0.3125
- fine_edge_out: bfloat16 [2, 128, 128], replicated, may hold values from -0.5 to 0.5
- fine_node_in: bfloat16 [2, 256, 128], replicated, may hold values from -0.375 to 0.375
- fine_node_out: bfloat16 [2, 128, 128], replicated, may hold values from -0.5 to 0.5
- coarse_edge_in: bfloat16 [2, 384, 128], replicated, may hold values from -0.3125 to 0.3125
- coarse_edge_out: bfloat16 [2, 128, 128], replicated, may hold values from -0.5 to 0.5
- coarse_node_in: bfloat16 [2, 256, 128], replicated, may hold values from -0.375 to 0.375
- coarse_node_out: bfloat16 [2, 128, 128], replicated, may hold values from -0.5 to 0.5
Outputs:
- new_state: bfloat16 [131072, 128], P(('fine', 'coarse'))
- state_grad: bfloat16 [131072, 128], P(('fine', 'coarse'))
- grad_fine_edge_in: float32 [2, 384, 128], replicated
- grad_fine_edge_out: float32 [2, 128, 128], replicated
- grad_fine_node_in: float32 [2, 256, 128], replicated
- grad_fine_node_out: float32 [2, 128, 128], replicated
- grad_coarse_edge_in: float32 [2, 384, 128], replicated
- grad_coarse_edge_out: float32 [2, 128, 128], replicated
- grad_coarse_node_in: float32 [2, 256, 128], replicated
- grad_coarse_node_out: float32 [2, 128, 128], replicated
The draws below stay inside these ranges and needn't reach their ends.
Inputs may be any that keep to these rules, and one draw needn't show every extreme that they name: `block_owner`: among the 64 blocks of one partition, at most 5 name the same owner, and in every draw some owner is named exactly 5 times.
All inputs are finite; a program needn't handle non-finite values.
Results may differ from the reference program's by a relative error of at most 0.039.
Values may be sent and summed in bfloat16 or wider, within the bound.
A program may use at most 128 MiB of HBM per device.

```python
import math
import jax
import jax.numpy as jnp
import numpy as np
from jax import lax

L = 128
NF = 1024
POOL = 16
EF = 4096
HS = 128
BLK_DEV = 64
CAP = 5
SLOTS = 160
ECD = 640
ROWS = 131072
EDGES = 524288
BLOCKS = 8192
CEDGES = 81920
N_FINE = 4
N_COARSE = 32
DEVICES = 128


def touch_ends(drawn, key, smallest, high):
    longest = drawn.shape.index(max(drawn.shape))
    spots = []
    for shift in (0, 1):
        where = [jax.random.randint(jax.random.fold_in(key, axis), (), 0, length) for axis, length in enumerate(drawn.shape)]
        where[longest] = (where[longest] + shift) % drawn.shape[longest]
        spots.append(tuple(where))
    return drawn.at[spots[0]].set(smallest).at[spots[1]].set(high)


def level_of(key, extent, shards, least, largest):
    def one(axis_at, shards_of):
        draws = jax.random.uniform(jax.random.fold_in(jax.random.fold_in(key, 6), axis_at), (shards_of,), jnp.float32, least / len(shards), largest / len(shards))
        return jnp.repeat(jnp.exp(draws), extent[axis_at] // shards_of).reshape((-1,) + (1,) * (len(extent) - axis_at - 1))

    gain = one(*shards[0])
    for cut in shards[1:]:
        gain = gain * one(*cut)
    return gain


def routed_block(own_key, own, number, rows, number_of, top, limit, slope):
    ranking = jax.random.permutation(own_key, number_of)
    packed, ordinary = shares(number_of, rows * top, limit, slope, True), shares(number_of, rows * top, limit, slope, False)
    places = jnp.arange(number_of)

    def named(tallies, offset_by):
        used = int((tallies > 0).sum())
        fixed = max(1, used // 4)
        passed = fixed + (places - fixed + offset_by * (used - fixed)) % max(1, number_of - fixed)
        return jnp.zeros((number_of,), jnp.int32).at[ranking[jnp.where(places < fixed, places, passed)]].set(jnp.asarray(tallies, jnp.int32))

    tallies = jnp.where(number % 4 == 0, named(packed, number // 4), named(ordinary, number - number // 4 - 1))
    mixed = jax.random.permutation(jax.random.fold_in(own, 3), number_of)
    donor, sink = mixed[0:number_of // 2 * 2:2], mixed[1:number_of // 2 * 2:2]
    margin = jnp.minimum(tallies[donor] - 1, limit - tallies[sink]) // 2
    margin = jnp.where((donor == ranking[0]) | (sink == ranking[0]) | (tallies[sink] == 0), 0, jnp.maximum(margin, 0))
    passed = jax.random.randint(jax.random.fold_in(own, 4), (number_of // 2,), 0, 1 << 20) % (margin + 1)
    tallies = tallies.at[donor].add(-passed).at[sink].add(passed)
    labels = jnp.searchsorted(jnp.cumsum(tallies), jnp.arange(rows * top), side="right").astype(jnp.int32)
    listing = labels.reshape(top, rows).T
    listing = listing[jax.random.permutation(jax.random.fold_in(own, 1), rows)]
    offset_by = jax.random.randint(jax.random.fold_in(own, 2), (rows, 1), 0, top)
    return jnp.take_along_axis(listing, (jnp.arange(top)[None, :] + offset_by) % top, axis=1)


def shares(count, total, bound, lean, full):
    portions = [(1 << 20) // math.isqrt(grade ** lean) + 1 for grade in range(1, count + 1)]
    largest = bound if full else min(bound, max(-(-total // count), total * portions[0] // sum(portions)))
    least = 1 if total - largest >= count - 1 else 0
    holding, surplus = [largest] + [least] * (count - 1), total - largest - least * (count - 1)
    while surplus > 0:
        free = [i for i in range(1, count) if holding[i] < largest] or [i for i in range(1, count) if holding[i] < bound]
        mass, left = sum([portions[i] for i in free]), surplus
        for i in free:
            addition = min(bound - holding[i], max(1, left * portions[i] // mass), surplus)
            holding[i] = holding[i] + addition
            surplus = surplus - addition
    return np.array(holding)


def noise(rng, shape, scale, bound, cuts=(), held_as=jnp.bfloat16):
    result = scale * jax.random.normal(rng, shape, jnp.float32)
    if cuts:
        result = result * level_of(rng, shape, cuts, -0.22, 0.18)
    return jnp.clip(result, -bound, bound).astype(held_as)


def setup_inputs(seed: int = 0) -> dict:
    splits = jax.random.split(jax.random.key(seed), 19)
    node_state = noise(splits[0], (ROWS, L), 1.0, 6.0, ((0, 128),))
    fine_edge_state = noise(splits[1], (EDGES, L), 1.0, 6.0, ((0, 128),))
    coarse_edge_state = noise(splits[2], (CEDGES, L), 1.0, 6.0, ((0, 128),))
    fine_src = touch_ends(jax.random.randint(splits[3], (EDGES,), 0, NF + N_FINE * HS), jax.random.fold_in(splits[3], 1), 0, (NF + N_FINE * HS) - 1).astype(jnp.int32)
    fine_dst = touch_ends(jax.random.randint(splits[4], (EDGES,), 0, NF), jax.random.fold_in(splits[4], 1), 0, NF - 1).astype(jnp.int32)
    halo_rows = touch_ends(jax.random.randint(splits[5], (DEVICES * N_FINE, HS), 0, NF), jax.random.fold_in(splits[5], 1), 0, NF - 1).astype(jnp.int32)
    block_owner_keys = jax.random.split(jax.random.fold_in(splits[6], 1), BLOCKS // BLK_DEV)
    block_owner_turns = jax.random.permutation(jax.random.fold_in(splits[6], 3), BLOCKS // BLK_DEV)
    block_owner = jax.vmap(lambda own, number: routed_block(jax.random.fold_in(splits[6], 2), own, number, BLK_DEV, N_COARSE, 1, CAP, 1))(block_owner_keys, block_owner_turns).reshape((BLOCKS, 1))
    coarse_src = touch_ends(jax.random.randint(splits[7], (CEDGES,), 0, 3 * SLOTS), jax.random.fold_in(splits[7], 1), 0, (3 * SLOTS) - 1).astype(jnp.int32)
    coarse_dst = touch_ends(jax.random.randint(splits[8], (CEDGES,), 0, SLOTS), jax.random.fold_in(splits[8], 1), 0, SLOTS - 1).astype(jnp.int32)
    cotangent = noise(splits[9], (ROWS, L), 1.0, 6.0, ((0, 128),))
    fine_edge_in = noise(splits[10], (2, 3 * L, L), (3 * L) ** -0.5, 0.3125)
    fine_edge_out = noise(splits[11], (2, L, L), L ** -0.5, 0.5)
    fine_node_in = noise(splits[12], (2, 2 * L, L), (2 * L) ** -0.5, 0.375)
    fine_node_out = noise(splits[13], (2, L, L), L ** -0.5, 0.5)
    coarse_edge_in = noise(splits[14], (2, 3 * L, L), (3 * L) ** -0.5, 0.3125)
    coarse_edge_out = noise(splits[15], (2, L, L), L ** -0.5, 0.5)
    coarse_node_in = noise(splits[16], (2, 2 * L, L), (2 * L) ** -0.5, 0.375)
    coarse_node_out = noise(splits[17], (2, L, L), L ** -0.5, 0.5)
    return {"node_state": node_state, "fine_edge_state": fine_edge_state, "coarse_edge_state": coarse_edge_state, "fine_src": fine_src, "fine_dst": fine_dst, "halo_rows": halo_rows, "block_owner": block_owner, "coarse_src": coarse_src, "coarse_dst": coarse_dst, "cotangent": cotangent, "fine_edge_in": fine_edge_in, "fine_edge_out": fine_edge_out, "fine_node_in": fine_node_in, "fine_node_out": fine_node_out, "coarse_edge_in": coarse_edge_in, "coarse_edge_out": coarse_edge_out, "coarse_node_in": coarse_node_in, "coarse_node_out": coarse_node_out}


norm_eps = 1e-05

def normalize(values):
    center = values - lax.optimization_barrier(jnp.mean(values, axis=-1, keepdims=True))
    spread = lax.optimization_barrier(jnp.mean(center * center, axis=-1, keepdims=True))
    return center * lax.rsqrt(spread + norm_eps)

def perceptron(inputs, w_first, w_second):
    hidden = jax.nn.silu(jnp.dot(inputs, w_first, preferred_element_type=jnp.float32)).astype(jnp.bfloat16)
    return normalize(jnp.dot(hidden, w_second, preferred_element_type=jnp.float32))

def graph_layer(state, extra, edges, senders, receivers, live, w_edge_in, w_edge_out, w_node_in, w_node_out):
    table = jnp.concatenate([state, extra], axis=0)
    joined = jnp.concatenate([edges, table[senders], state[receivers]], axis=1)
    new_edges = (edges.astype(jnp.float32) + perceptron(joined, w_edge_in, w_edge_out)).astype(jnp.bfloat16)
    incoming = jax.ops.segment_sum(new_edges.astype(jnp.float32), receivers, num_segments=state.shape[0]).astype(jnp.bfloat16)
    node_input = jnp.concatenate([state, incoming], axis=1)
    updated = state.astype(jnp.float32) + perceptron(node_input, w_node_in, w_node_out)
    if live is not None:
        updated = updated * live
    return (updated.astype(jnp.bfloat16), new_edges)

def slot_table(owners, groups, capacity):
    choose = (owners[:, None] == jnp.arange(groups, dtype=jnp.int32)[None, :]).astype(jnp.int32)
    ranks = lax.optimization_barrier(jnp.sum((jnp.cumsum(choose, axis=0) - 1) * choose, axis=1))
    places = owners * capacity + ranks
    return (places[:, None] == jnp.arange(groups * capacity, dtype=jnp.int32)[None, :]).astype(jnp.bfloat16)

def pool_rows(state, select, pool_size):
    width = state.shape[1]
    pooled = lax.optimization_barrier(jnp.mean(state.astype(jnp.float32).reshape(-1, pool_size, width), axis=1)).astype(jnp.bfloat16)
    placed = lax.dot_general(select, pooled, (((0,), (0,)), ((), ())), preferred_element_type=jnp.float32)
    return placed.astype(jnp.bfloat16)

def prolong(state, back, select, pool_size):
    width = state.shape[1]
    picked = jnp.dot(select, back, preferred_element_type=jnp.float32)
    grown = state.astype(jnp.float32).reshape(-1, pool_size, width) + picked[:, None, :]
    return grown.reshape(state.shape).astype(jnp.bfloat16)

def add_three(first, second, third):
    return (first.astype(jnp.float32) + second.astype(jnp.float32) + third.astype(jnp.float32)).astype(jnp.bfloat16)

def add_two(first, second):
    return (first.astype(jnp.float32) + second.astype(jnp.float32)).astype(jnp.bfloat16)

def reference(node_state, fine_edge_state, coarse_edge_state, fine_src, fine_dst, halo_rows, block_owner, coarse_src, coarse_dst, cotangent, fine_edge_in, fine_edge_out, fine_node_in, fine_node_out, coarse_edge_in, coarse_edge_out, coarse_node_in, coarse_node_out):
    devices = N_FINE * N_COARSE
    width = L
    slots = SLOTS
    state_zero = node_state.reshape(devices, NF, width)
    edges_zero = fine_edge_state.reshape(devices, EF, width)
    cedges_zero = coarse_edge_state.reshape(devices, ECD, width)
    senders = fine_src.reshape(devices, EF)
    receivers = fine_dst.reshape(devices, EF)
    sent_rows = halo_rows.reshape(devices, N_FINE, HS)
    owners = block_owner.reshape(devices, BLK_DEV)
    csenders = coarse_src.reshape(devices, ECD)
    creceivers = coarse_dst.reshape(devices, ECD)
    grad_out = cotangent.reshape(devices, NF, width)

    def fine_weights(layer):
        return (fine_edge_in[layer], fine_edge_out[layer], fine_node_in[layer], fine_node_out[layer])

    def coarse_weights(layer):
        return (coarse_edge_in[layer], coarse_edge_out[layer], coarse_node_in[layer], coarse_node_out[layer])

    def group_swap(values):
        grid = values.reshape((N_FINE, N_COARSE) + values.shape[1:])
        return jnp.swapaxes(grid, 0, 2).reshape(values.shape)

    def owner_swap(values):
        grid = values.reshape((N_FINE, N_COARSE) + values.shape[1:])
        return jnp.swapaxes(grid, 1, 2).reshape(values.shape)

    def roll_owners(values, offset):
        grid = values.reshape((N_FINE, N_COARSE) + values.shape[1:])
        return jnp.roll(grid, offset, axis=1).reshape(values.shape)

    def pick(state, rows):
        return state[rows.reshape(-1)].reshape(N_FINE, HS, width)

    def pick_back(items):
        state, rows, grad = items
        return jax.vjp(lambda value: pick(value, rows), state)[1](grad)[0]

    def fine_forward(layer):

        def run(items):
            state, received, edges, send_ids, recv_ids = items
            return graph_layer(state, received.reshape(-1, width), edges, send_ids, recv_ids, None, *fine_weights(layer))
        return run

    def fine_backward(layer):

        def run(items):
            state, received, edges, send_ids, recv_ids, grad_state, grad_edges = items

            def step(state_in, received_in, edges_in, w_a, w_b, w_c, w_d):
                return graph_layer(state_in, received_in.reshape(-1, width), edges_in, send_ids, recv_ids, None, w_a, w_b, w_c, w_d)
            return jax.vjp(step, state, received, edges, *fine_weights(layer))[1]((grad_state, grad_edges))
        return run

    def coarse_forward(layer):

        def run(items):
            state, extra, edges, send_ids, recv_ids, live = items
            return graph_layer(state, extra, edges, send_ids, recv_ids, live, *coarse_weights(layer))
        return run

    def coarse_backward(layer):

        def run(items):
            state, extra, edges, send_ids, recv_ids, live, grad_state, grad_edges = items

            def step(state_in, extra_in, edges_in, w_a, w_b, w_c, w_d):
                return graph_layer(state_in, extra_in, edges_in, send_ids, recv_ids, live, w_a, w_b, w_c, w_d)
            return jax.vjp(step, state, extra, edges, *coarse_weights(layer))[1]((grad_state, grad_edges))
        return run

    def neighbours(states):
        return jnp.concatenate([roll_owners(states, 1), roll_owners(states, -1)], axis=1)

    def neighbours_back(grad_extra, grad_state):
        return add_three(grad_state, roll_owners(grad_extra[:, slots:], 1), roll_owners(grad_extra[:, :slots], -1))
    select = lax.map(lambda own: slot_table(own, N_COARSE, CAP), owners)
    flags = lax.optimization_barrier(jnp.sum(select, axis=1)).astype(jnp.int32).reshape(devices, N_COARSE, CAP)
    live = owner_swap(flags).reshape(devices, slots, 1).astype(jnp.float32)
    recv_one = group_swap(lax.map(lambda items: pick(items[0], items[1]), (state_zero, sent_rows)))
    state_one, edges_one = lax.map(fine_forward(0), (state_zero, recv_one, edges_zero, senders, receivers))
    placed = lax.map(lambda items: pool_rows(items[0], items[1], POOL), (state_one, select))
    coarse_zero = owner_swap(placed.reshape(devices, N_COARSE, CAP, width)).reshape(devices, slots, width)
    extra_zero = neighbours(coarse_zero)
    coarse_one, cedges_one = lax.map(coarse_forward(0), (coarse_zero, extra_zero, cedges_zero, csenders, creceivers, live))
    extra_one = neighbours(coarse_one)
    coarse_two, cedges_two = lax.map(coarse_forward(1), (coarse_one, extra_one, cedges_one, csenders, creceivers, live))
    back = owner_swap(coarse_two.reshape(devices, N_COARSE, CAP, width)).reshape(devices, slots, width)
    state_two = lax.map(lambda items: prolong(items[0], items[1], items[2], POOL), (state_one, back, select))
    recv_two = group_swap(lax.map(lambda items: pick(items[0], items[1]), (state_two, sent_rows)))
    new_state, edges_two = lax.map(fine_forward(1), (state_two, recv_two, edges_one, senders, receivers))
    grads_late = lax.map(fine_backward(1), (state_two, recv_two, edges_one, senders, receivers, grad_out, jnp.zeros_like(edges_two)))
    halo_back = lax.map(pick_back, (state_two, sent_rows, group_swap(grads_late[1])))
    grad_two = add_two(grads_late[0], halo_back)

    def prolong_back(items):
        state, value, table, grad = items
        return jax.vjp(lambda first, second: prolong(first, second, table, POOL), state, value)[1](grad)
    grad_one_local, grad_back = lax.map(prolong_back, (state_one, back, select, grad_two))
    grad_ctwo = owner_swap(grad_back.reshape(devices, N_COARSE, CAP, width)).reshape(devices, slots, width)
    grads_cb = lax.map(coarse_backward(1), (coarse_one, extra_one, cedges_one, csenders, creceivers, live, grad_ctwo, jnp.zeros_like(cedges_two)))
    grad_cone = neighbours_back(grads_cb[1], grads_cb[0])
    grads_ca = lax.map(coarse_backward(0), (coarse_zero, extra_zero, cedges_zero, csenders, creceivers, live, grad_cone, grads_cb[2]))
    grad_czero = neighbours_back(grads_ca[1], grads_ca[0])
    grad_placed = owner_swap(grad_czero.reshape(devices, N_COARSE, CAP, width)).reshape(devices, N_COARSE * CAP, width)

    def pool_back(items):
        state, table, grad = items
        return jax.vjp(lambda value: pool_rows(value, table, POOL), state)[1](grad)[0]
    grad_pool = lax.map(pool_back, (state_one, select, grad_placed))
    grad_one = add_two(grad_one_local, grad_pool)
    grads_early = lax.map(fine_backward(0), (state_zero, recv_one, edges_zero, senders, receivers, grad_one, grads_late[2]))
    halo_first = lax.map(pick_back, (state_zero, sent_rows, group_swap(grads_early[1])))
    state_grad = add_two(grads_early[0], halo_first)

    def total(first, second):
        return jnp.stack([lax.optimization_barrier(jnp.sum(first.astype(jnp.float32), axis=0)), lax.optimization_barrier(jnp.sum(second.astype(jnp.float32), axis=0))])
    return (new_state.reshape(ROWS, width), state_grad.reshape(ROWS, width), total(grads_early[3], grads_late[3]), total(grads_early[4], grads_late[4]), total(grads_early[5], grads_late[5]), total(grads_early[6], grads_late[6]), total(grads_ca[3], grads_cb[3]), total(grads_ca[4], grads_cb[4]), total(grads_ca[5], grads_cb[5]), total(grads_ca[6], grads_cb[6]))
```

```python
from types import SimpleNamespace

import jax
import jax.numpy as jnp
from jax import lax
from jax.experimental import pallas as pl
from jax.experimental.pallas import tpu as pltpu
from jax.sharding import PartitionSpec as P

BF = jnp.bfloat16
F32 = jnp.float32
I16 = jnp.int16
I32 = jnp.int32
F8 = jnp.float8_e4m3fn
MESH = pl.DeviceIdType.MESH

L = 128
NF, EF, HALO = 1024, 4096, 512
NC, EC = 160, 640
BLOCKS, POOL, CAP = 64, 16, 5
PAD = 16
N_FINE, N_COARSE = 4, 32
WIDE = N_COARSE * PAD
SET = 896
PART = SET // N_FINE
OWNERS = PART // 8
EPS = 1e-05


def dot(a, b):
    return jnp.dot(a, b, preferred_element_type=F32)


def dot_nt(a, b):
    return lax.dot_general(a, b, (((1,), (1,)), ((), ())), preferred_element_type=F32)


def dot_tn(a, b):
    return lax.dot_general(a, b, (((0,), (0,)), ((), ())), preferred_element_type=F32)


def iota(shape, dim):
    return lax.broadcasted_iota(I32, shape, dim)


def ones_where(mask):
    return jnp.where(mask, jnp.asarray(1, BF), jnp.asarray(0, BF))


def lane_sum(x):
    return jnp.sum(x, axis=-1, keepdims=True)


def normed(y):
    center = y - lane_sum(y) * (1.0 / L)
    scale = lax.rsqrt(lane_sum(center * center) * (1.0 / L) + EPS)
    return center * scale, scale


def normed_back(dn, n, scale):
    return scale * (dn - lane_sum(dn) * (1.0 / L) - n * (lane_sum(dn * n) * (1.0 / L)))


def hot_columns(column, base, width, dtype):
    count = column.shape[0]
    lanes = iota((16, 128), 1).astype(I16)
    parts = []
    for start in range(0, width, 128):
        places = jnp.concatenate([lanes + jnp.asarray(base + start, I16)] * (count // 16), axis=0)
        parts.append(ones_where(column == places))
    hot = jnp.concatenate(parts, axis=1) if len(parts) > 1 else parts[0]
    return hot.astype(dtype)


def gather_rows(columns, table):
    total = None
    for column, base, width in columns:
        for k in range(0, width, 256):
            size = min(256, width - k)
            part = dot(hot_columns(column, k, size, table.dtype), table[base + k : base + k + size, :])
            total = part if total is None else total + part
    return total


def scatter_rows(rows_ref, data_ref, first, count, edges):
    down = iota((count, 128), 0).astype(I16)
    shift = jnp.asarray(first, I32).astype(I16)
    total = None
    for k in range(0, edges, 256):
        size = min(256, edges - k)
        parts = []
        for j in range(k // 128, (k + size) // 128):
            row = rows_ref[j] - shift
            parts.append(ones_where(down == jnp.concatenate([row] * (count // 16), axis=0)))
        hot = jnp.concatenate(parts, axis=1) if len(parts) > 1 else parts[0]
        part = dot(hot.astype(data_ref.dtype), data_ref[k : k + size, :])
        total = part if total is None else total + part
    return total


def column_peak(x):
    return jnp.max(jnp.abs(x), axis=0, keepdims=True)


def scale_for(peak):
    return jnp.exp2(7.0 - jnp.floor(jnp.log2(jnp.maximum(peak, 1e-30))))


def halves(x, scale):
    x = x * scale
    high = x.astype(F8)
    low = ((x - high.astype(F32)) * 16.0).astype(F8)
    return jnp.concatenate([high, low], axis=1)


def joined(pair, scale):
    return (pair[:, 0:L] + pair[:, L : 2 * L] * 0.0625) * (1.0 / scale)


def vm(*shape, dtype=F32):
    return pltpu.VMEM(shape, dtype)


def level_shapes(n, tab, own, e):
    def layer():
        return SimpleNamespace(
            tab=vm(tab, L, dtype=BF),
            slope=vm(e, L),
            hid=vm(e, L, dtype=BF),
            n=vm(e, L),
            scale=vm(e, L),
            e=vm(e, L, dtype=BF),
            g=vm(n, L, dtype=BF),
            slope2=vm(n, L),
            hid2=vm(n, L, dtype=BF),
            n2=vm(n, L),
            scale2=vm(n, L),
        )

    return SimpleNamespace(
        cs=vm(e, L, dtype=I16),
        cr=vm(e, L, dtype=I16),
        rs=vm(e // L, 16, L, dtype=I16),
        rr=vm(e // L, 16, L, dtype=I16),
        proj=vm(tab + own, L, dtype=BF),
        wide=vm(tab + own, L),
        proj8=vm(tab + own, 2 * L, dtype=F8),
        dz=vm(e, L, dtype=BF),
        e8=vm(e, 2 * L, dtype=F8),
        dg8=vm(own, 2 * L, dtype=F8),
        de=vm(e, L, dtype=BF),
        dg=vm(own, L, dtype=BF),
        acc=vm(n, L),
        layers=[layer(), layer()],
    )


def shapes():
    dma = pltpu.SemaphoreType.DMA
    return SimpleNamespace(
        f=level_shapes(NF, NF + HALO, NF, EF),
        c=level_shapes(NC, 512, 256, EC),
        state_one=vm(NF, L, dtype=BF),
        live=vm(NC, L),
        acc_b=vm(L, L),
        acc_e=vm(L, L),
        halo_col=vm(HALO, L, dtype=I16),
        halo_row=vm(HALO // L, 16, L, dtype=I16),
        grad_two=vm(NF, L, dtype=BF),
        grad_one=vm(NF, L, dtype=BF),
        grad_c=vm(NC, L, dtype=BF),
        place=[vm(BLOCKS, L, dtype=I32), vm(L, L, dtype=I32)],
        hs=[vm(HALO, L, dtype=BF) for _ in range(4)],
        hr=[vm(HALO, L, dtype=BF) for _ in range(2)],
        ws=[vm(WIDE, L, dtype=BF) for _ in range(4)],
        wr=[vm(WIDE, L, dtype=BF) for _ in range(4)],
        ns=[vm(2 * NC, L, dtype=BF) for _ in range(2)],
        nr=[vm(2 * NC, L, dtype=BF) for _ in range(2)],
        gw=vm(4, SET, L, dtype=BF),
        r1=vm(4, 3, PART, L, dtype=BF),
        p1=vm(4, PART, L),
        r2=vm(4, N_COARSE * 8, L),
        r3=vm(4, PART, L),
        r4=vm(4, SET, L),
        hs_sem=[dma((2, 3)) for _ in range(4)],
        ws_sem=[dma((2,)) for _ in range(4)],
        near_sem=[dma((2, 2)) for _ in range(4)],
        ar1_sem=dma((4, 2, 3)),
        ar2_sem=dma((4, 2)),
        ar3_sem=dma((4, 2)),
        ar4_sem=dma((4, 2, 3)),
    )


def flat(tree):
    if isinstance(tree, SimpleNamespace):
        return [leaf for part in vars(tree).values() for leaf in flat(part)]
    if isinstance(tree, list):
        return [leaf for part in tree for leaf in flat(part)]
    return [tree]


def rebuilt(tree, leaves):
    if isinstance(tree, SimpleNamespace):
        return SimpleNamespace(**{name: rebuilt(part, leaves) for name, part in vars(tree).items()})
    if isinstance(tree, list):
        return [rebuilt(part, leaves) for part in tree]
    return next(leaves)


def operands():
    def weights():
        return SimpleNamespace(ei=None, eo=None, ni=None, no=None)

    inputs = SimpleNamespace(
        node=None, edge=None, cedge=None, src=None, dst=None, halo=None, owner=None, csrc=None, cdst=None, cot=None,
        fw=weights(), cw=weights(),
    )
    outputs = SimpleNamespace(new_state=None, state_grad=None, fg=weights(), cg=weights())
    return inputs, outputs


STEPS = None


def kernel(*args):
    leaves = iter(args)
    I, O = (rebuilt(tree, leaves) for tree in operands())
    R = rebuilt(shapes(), leaves)
    f = lax.axis_index("fine")
    c = lax.axis_index("coarse")

    def fine_at(d):
        return lax.rem(f + d + N_FINE, N_FINE)

    def coarse_at(d):
        return lax.rem(c + d + N_COARSE, N_COARSE)

    def chunk(i, size, align=None):
        return pl.ds(pl.multiple_of(i * size, align or size), size)

    def remote(src, dst, send, recv, where):
        return pltpu.make_async_remote_copy(
            src_ref=src, dst_ref=dst, send_sem=send, recv_sem=recv, device_id=where, device_id_type=MESH
        )

    def wait_for(view, sem):
        pltpu.make_async_copy(view, view, sem).wait()

    barrier = pltpu.get_barrier_semaphore()

    def greet():
        for d in range(1, N_FINE):
            pl.semaphore_signal(barrier, inc=1, device_id=(fine_at(d), c), device_id_type=MESH)

        def one(d, carry):
            pl.semaphore_signal(barrier, inc=1, device_id=(f, coarse_at(d)), device_id_type=MESH)
            return carry

        lax.fori_loop(1, N_COARSE, one, 0)

    def spread(src, columns, rows, count):
        def one(j, carry):
            wide = jnp.broadcast_to(src[pl.ds(j, 1), :], (L, L))
            rows[j] = wide[:16, :].astype(I16)
            columns[chunk(j, L), :] = wide.T.astype(I16)
            return carry

        lax.fori_loop(0, count, one, 0)

    def halo_copies(src, dst, base, sem):
        out, back = [], []
        for d in range(1, N_FINE):
            q, at = fine_at(d), fine_at(-d)
            out.append(
                remote(
                    src.at[chunk(q, L), :],
                    dst.at[pl.ds(pl.multiple_of(base + f * L, L), L), :],
                    sem.at[0, d - 1],
                    sem.at[1, d - 1],
                    (q, c),
                )
            )
            back.append((dst.at[pl.ds(pl.multiple_of(base + at * L, L), L), :], sem.at[1, d - 1]))
        return out, back

    def halo_start(src, dst, base, sem):
        for copy in halo_copies(src, dst, base, sem)[0]:
            copy.start()
        dst[pl.ds(pl.multiple_of(base + f * L, L), L), :] = src[chunk(f, L), :]

    def halo_wait(src, dst, base, sem):
        out, back = halo_copies(src, dst, base, sem)
        for copy in out:
            copy.wait_send()
        for view, at in back:
            wait_for(view, at)

    def wide_start(k):
        src, dst, sem = R.ws[k], R.wr[k], R.ws_sem[k]

        def one(d, carry):
            o = coarse_at(d)
            remote(src.at[chunk(o, PAD), :], dst.at[chunk(c, PAD), :], sem.at[0], sem.at[1], (f, o)).start()
            return carry

        lax.fori_loop(1, N_COARSE, one, 0)
        dst[chunk(c, PAD), :] = src[chunk(c, PAD), :]

    def wide_wait(k):
        src, dst, sem = R.ws[k], R.wr[k], R.ws_sem[k]
        wait_for(src.at[pl.ds(0, WIDE - PAD), :], sem.at[0])
        wait_for(dst.at[pl.ds(0, WIDE - PAD), :], sem.at[1])

    def near_copies(up_src, up_dst, down_src, down_dst, sem):
        return (
            remote(up_src, up_dst, sem.at[0, 0], sem.at[1, 0], (f, coarse_at(1))),
            remote(down_src, down_dst, sem.at[0, 1], sem.at[1, 1], (f, coarse_at(-1))),
        )

    def sum_one_copies(s):
        out = []
        for d in range(1, N_FINE):
            q = fine_at(d)
            out.append(
                remote(
                    R.gw.at[s, chunk(q, PART, 32), :],
                    R.r1.at[s, d - 1],
                    R.ar1_sem.at[s, 0, d - 1],
                    R.ar1_sem.at[s, 1, d - 1],
                    (q, c),
                )
            )
        return out

    def sum_one(s):
        for copy in sum_one_copies(s):
            copy.start()

    def sum_two(s):
        for copy in sum_one_copies(s):
            copy.wait()
        own = R.gw[s, chunk(f, PART, 32), :].astype(F32)
        for d in range(3):
            own = own + R.r1[s, d].astype(F32)
        R.p1[s] = own
        sem = R.ar2_sem

        def one(d, carry):
            o = coarse_at(d)

            @pl.when(o < OWNERS)
            def _():
                remote(
                    R.p1.at[s, chunk(o, 8), :], R.r2.at[s, chunk(c, 8), :], sem.at[s, 0], sem.at[s, 1], (f, o)
                ).start()

            return carry

        lax.fori_loop(1, N_COARSE, one, 0)

    def sum_three(s):
        sem, sem3 = R.ar2_sem, R.ar3_sem

        @pl.when(c < OWNERS)
        def _():
            mine = chunk(c, 8)
            R.r2[s, mine, :] = R.p1[s, mine, :]
            wait_for(R.p1.at[s, pl.ds(0, (OWNERS - 1) * 8), :], sem.at[s, 0])
            wait_for(R.r2.at[s, pl.ds(0, (N_COARSE - 1) * 8), :], sem.at[s, 1])
            parts = [R.r2[s, j * 8 : j * 8 + 8, :] for j in range(N_COARSE)]
            while len(parts) > 1:
                parts = [parts[j] + parts[j + 1] for j in range(0, len(parts), 2)]
            R.r3[s, mine, :] = parts[0]

            def one(d, carry):
                remote(
                    R.r3.at[s, mine, :], R.r3.at[s, mine, :], sem3.at[s, 0], sem3.at[s, 1], (f, coarse_at(d))
                ).start()
                return carry

            lax.fori_loop(1, N_COARSE, one, 0)

        @pl.when(c >= OWNERS)
        def _():
            wait_for(R.p1.at[s], sem.at[s, 0])

    def sum_four_copies(s):
        mine = chunk(f, PART, 32)
        out = []
        for d in range(1, N_FINE):
            out.append(
                remote(
                    R.r3.at[s],
                    R.r4.at[s, mine, :],
                    R.ar4_sem.at[s, 0, d - 1],
                    R.ar4_sem.at[s, 1, d - 1],
                    (fine_at(d), c),
                )
            )
        return out

    def sum_four(s):
        sem = R.ar3_sem

        @pl.when(c < OWNERS)
        def _():
            wait_for(R.r2.at[s, pl.ds(0, (N_COARSE - 1) * 8), :], sem.at[s, 0])
            wait_for(R.r3.at[s, pl.ds(0, (OWNERS - 1) * 8), :], sem.at[s, 1])

        @pl.when(c >= OWNERS)
        def _():
            wait_for(R.r3.at[s], sem.at[s, 1])

        for copy in sum_four_copies(s):
            copy.start()
        R.r4[s, chunk(f, PART, 32), :] = R.r3[s]

    def sum_end(s):
        for copy in sum_four_copies(s):
            copy.wait()
        out, l = (O.fg, s) if s < 2 else (O.cg, s - 2)
        out.ei[l] = R.r4[s, 0:384, :]
        out.eo[l] = R.r4[s, 384:512, :]
        out.ni[l] = R.r4[s, 512:768, :]
        out.no[l] = R.r4[s, 768:896, :]

    fine = SimpleNamespace(
        n=NF, used=NF + HALO, tab=NF + HALO, own=NF, e=EF, tile=1024, block=512, S=R.f, W=I.fw, first=0, masked=False
    )
    coarse = SimpleNamespace(
        n=NC, used=3 * NC, tab=512, own=256, e=EC, tile=EC, block=NC, S=R.c, W=I.cw, first=2, masked=True
    )

    def project_own(v, l):
        w, h = v.W.ei, v.S.layers[l].tab[0 : v.n, :]
        into = v.S.proj if v.masked else v.S.wide
        into[0 : v.n, :] = dot(h, w[l, 128:256, :]).astype(into.dtype)
        into[v.tab : v.tab + v.n, :] = dot(h, w[l, 256:384, :]).astype(into.dtype)

    def project_rest(v, l):
        rest = v.S.layers[l].tab[v.n : v.tab, :]
        into = v.S.proj if v.masked else v.S.wide
        into[v.n : v.tab, :] = dot(rest, v.W.ei[l, 128:256, :]).astype(into.dtype)

    def forward(v, l, edges):
        S, W, A = v.S, v.W, v.S.layers[l]
        if not v.masked:
            scale = scale_for(column_peak(S.wide[...]))
            S.proj8[...] = halves(S.wide[...], scale)

        def one(i, peak):
            rows = chunk(i, v.tile)
            old = edges[rows, :]
            columns = ((S.cs[rows, :], 0, v.tab), (S.cr[rows, :], v.tab, v.own))
            if v.masked:
                z = gather_rows(columns, S.proj)
            else:
                z = joined(gather_rows(columns, S.proj8), scale)
            z = z + dot(old, W.ei[l, 0:128, :])
            gate = jax.nn.sigmoid(z)
            hidden = z * gate
            A.slope[rows, :] = gate * (1.0 + z - hidden)
            hidden = hidden.astype(BF)
            A.hid[rows, :] = hidden
            values, spread_by = normed(dot(hidden, W.eo[l]))
            A.n[rows, :] = values
            A.scale[rows, :] = jnp.broadcast_to(spread_by, values.shape)
            new = (old.astype(F32) + values).astype(BF)
            A.e[rows, :] = new
            return jnp.maximum(peak, column_peak(new.astype(F32)))

        peak = lax.fori_loop(0, v.e // v.tile, one, jnp.zeros((1, L), F32))
        if not v.masked:
            scale = scale_for(peak)

            def split(i, carry):
                rows = chunk(i, v.tile)
                S.e8[rows, :] = halves(A.e[rows, :].astype(F32), scale)
                return carry

            lax.fori_loop(0, v.e // v.tile, split, 0)

        def two(i, carry):
            rows = chunk(i, v.block)
            if v.masked:
                g = scatter_rows(S.rr, A.e, i * v.block, v.block, v.e)
            else:
                g = joined(scatter_rows(S.rr, S.e8, i * v.block, v.block, v.e), scale)
            A.g[rows, :] = g.astype(BF)
            return carry

        lax.fori_loop(0, v.n // v.block, two, 0)
        h = A.tab[0 : v.n, :]
        z = dot(h, W.ni[l, 0:128, :]) + dot(A.g[...], W.ni[l, 128:256, :])
        gate = jax.nn.sigmoid(z)
        hidden = z * gate
        A.slope2[...] = gate * (1.0 + z - hidden)
        hidden = hidden.astype(BF)
        A.hid2[...] = hidden
        values, spread_by = normed(dot(hidden, W.no[l]))
        A.n2[...] = values
        A.scale2[...] = jnp.broadcast_to(spread_by, values.shape)
        new = h.astype(F32) + values
        if v.masked:
            new = new * R.live[...]
        return new.astype(BF)

    def backward(v, l, edges, grad, edge_grad, send_rest, keep_edge, weights_done):
        S, W, A = v.S, v.W, v.S.layers[l]
        s, acc, gw = v.first + l, v.S.acc, R.gw
        dn = grad.astype(F32)
        if v.masked:
            dn = dn * R.live[...]
        dy = normed_back(dn, A.n2[...], A.scale2[...]).astype(BF)
        dz = (dot_nt(dy, W.no[l]) * A.slope2[...]).astype(BF)
        h = A.tab[0 : v.n, :]
        dg = dot_nt(dz, W.ni[l, 128:256, :])
        if v.masked:
            S.dg[0 : v.n, :] = dg.astype(BF)
        else:
            dg_scale = scale_for(column_peak(dg))
            S.dg8[...] = halves(dg, dg_scale)
        acc[...] = dn + dot_nt(dz, W.ni[l, 0:128, :])
        gw[s, 512:640, :] = dot_tn(h, dz).astype(BF)
        gw[s, 640:768, :] = dot_tn(A.g[...], dz).astype(BF)
        gw[s, 768:896, :] = dot_tn(A.hid2[...], dy).astype(BF)
        R.acc_b[...] = jnp.zeros((L, L), F32)
        R.acc_e[...] = jnp.zeros((L, L), F32)

        def one(i, peak):
            rows = chunk(i, v.tile)
            columns = ((S.cr[rows, :], 0, v.own),)
            if v.masked:
                dn = gather_rows(columns, S.dg)
            else:
                dn = joined(gather_rows(columns, S.dg8), dg_scale)
            if edge_grad is not None:
                dn = dn + edge_grad[rows, :].astype(F32)
            dy = normed_back(dn, A.n[rows, :], A.scale[rows, :]).astype(BF)
            dz = (dot_nt(dy, W.eo[l]) * A.slope[rows, :]).astype(BF)
            S.dz[rows, :] = dz
            R.acc_b[...] += dot_tn(A.hid[rows, :], dy)
            R.acc_e[...] += dot_tn(edges[rows, :], dz)
            if keep_edge:
                S.de[rows, :] = (dn + dot_nt(dz, W.ei[l, 0:128, :])).astype(BF)
            return jnp.maximum(peak, column_peak(dz.astype(F32)))

        peak = lax.fori_loop(0, v.e // v.tile, one, jnp.zeros((1, L), F32))
        if v.masked:

            def spread_back(rows_ref, first, count):
                return scatter_rows(rows_ref, S.dz, first, count, v.e).astype(BF)

        else:
            scale = scale_for(peak)

            def split(i, carry):
                rows = chunk(i, v.tile)
                S.e8[rows, :] = halves(S.dz[rows, :].astype(F32), scale)
                return carry

            lax.fori_loop(0, v.e // v.tile, split, 0)

            def spread_back(rows_ref, first, count):
                return joined(scatter_rows(rows_ref, S.e8, first, count, v.e), scale).astype(BF)

        rest = spread_back(S.rs, v.n, v.used - v.n)
        send_rest(dot_nt(rest, W.ei[l, 128:256, :]).astype(BF))
        gw[s, 0:128, :] = R.acc_e[...].astype(BF)
        gw[s, 384:512, :] = R.acc_b[...].astype(BF)
        R.acc_b[...] = dot_tn(A.tab[v.n : v.used, :], rest)
        R.acc_e[...] = jnp.zeros((L, L), F32)

        def two(i, carry):
            rows = chunk(i, v.block)
            h = A.tab[rows, :]
            part = spread_back(S.rs, i * v.block, v.block)
            R.acc_b[...] += dot_tn(h, part)
            other = spread_back(S.rr, i * v.block, v.block)
            R.acc_e[...] += dot_tn(h, other)
            acc[rows, :] += dot_nt(part, W.ei[l, 128:256, :]) + dot_nt(other, W.ei[l, 256:384, :])
            return carry

        lax.fori_loop(0, v.n // v.block, two, 0)
        gw[s, 128:256, :] = R.acc_b[...].astype(BF)
        gw[s, 256:384, :] = R.acc_e[...].astype(BF)
        weights_done(s)

    def place_column():
        return R.place[0][...]

    def place_wide():
        return jnp.broadcast_to(R.place[1][0:1, :], (WIDE, L))

    def pool_hot():
        return ones_where((iota((BLOCKS, NF), 1) >> 4) == iota((BLOCKS, NF), 0))

    def grow_hot():
        return ones_where((iota((NF, L), 0) >> 4) == iota((NF, L), 1))[:, 0:BLOCKS]

    def put_hot():
        return ones_where(iota((WIDE, L), 0) == place_wide())[:, 0:BLOCKS]

    def flag_hot():
        wide = place_wide()
        return ones_where((iota((WIDE, L), 0) == wide + CAP) & (wide >= 0))[:, 0:BLOCKS]

    def take_hot():
        return ones_where(jnp.concatenate([place_column()] * 4, axis=1) == iota((BLOCKS, WIDE), 1))

    def slot_of(index, offset):
        within = (index & (PAD - 1)) - offset
        return jnp.where((within >= 0) & (within < CAP), (index >> 4) * CAP + within, -1)

    def narrow_hot(offset):
        return ones_where(slot_of(iota((NC, WIDE), 1), offset) == iota((NC, WIDE), 0))

    def widen_hot():
        return ones_where(slot_of(iota((WIDE, 256), 0), 0) == iota((WIDE, 256), 1))[:, 0:NC]

    def halo_pick(tab, k):
        def one(j, carry):
            rows = chunk(j, L)
            R.hs[k][rows, :] = gather_rows(((R.halo_col[rows, :], 0, NF),), tab).astype(BF)
            return carry

        lax.fori_loop(0, N_FINE, one, 0)

    def halo_back(k):
        def send(values):
            R.hs[k][...] = values
            halo_start(R.hs[k], R.hr[k - 2], 0, R.hs_sem[k])

        return send

    def halo_add(k):
        halo_wait(R.hs[k], R.hr[k - 2], 0, R.hs_sem[k])

        def one(i, carry):
            rows = chunk(i, 512)
            R.f.acc[rows, :] += scatter_rows(R.halo_row, R.hr[k - 2], i * 512, 512, HALO)
            return carry

        lax.fori_loop(0, NF // 512, one, 0)

    def near_table(l):
        tab = R.c.layers[l].tab
        own = tab.at[pl.ds(0, NC), :]
        return near_copies(own, tab.at[pl.ds(NC, NC), :], own, tab.at[pl.ds(2 * NC, NC), :], R.near_sem[l])

    def near_grad(l):
        src, dst = R.ns[l], R.nr[l]
        low, high = pl.ds(0, NC), pl.ds(NC, NC)
        return near_copies(src.at[high, :], dst.at[low, :], src.at[low, :], dst.at[high, :], R.near_sem[2 + l])

    def start(copies):
        for copy in copies:
            copy.start()

    def wait(copies):
        for copy in copies:
            copy.wait()

    def enter():
        greet()
        spread(I.halo, R.halo_col, R.halo_row, HALO // L)
        halo_pick(I.node, 0)
        pl.semaphore_wait(barrier, N_FINE - 1 + N_COARSE - 1)
        halo_start(R.hs[0], R.f.layers[0].tab, NF, R.hs_sem[0])

    def prepare():
        R.f.layers[0].tab[0:NF, :] = I.node[...]
        project_own(fine, 0)
        spread(I.src, R.f.cs, R.f.rs, EF // L)
        spread(I.dst, R.f.cr, R.f.rr, EF // L)
        spread(I.csrc, R.c.cs, R.c.rs, EC // L)
        spread(I.cdst, R.c.cr, R.c.rr, EC // L)
        for l in (0, 1):
            R.c.layers[l].tab[3 * NC : 512, :] = jnp.zeros((512 - 3 * NC, L), BF)
        R.c.proj[512 + NC : 768, :] = jnp.zeros((256 - NC, L), BF)
        R.c.dg[NC:256, :] = jnp.zeros((256 - NC, L), BF)
        owner = jnp.broadcast_to(I.owner[...], (BLOCKS, L))
        below = jnp.full((L - BLOCKS, L), -1, I32)
        square = jnp.concatenate([owner, below], axis=0).T
        same = (owner == square[0:BLOCKS, :]) & (iota((BLOCKS, L), 1) < iota((BLOCKS, L), 0))
        rank = lane_sum(jnp.where(same, 1.0, 0.0)).astype(I32)
        place = owner * PAD + rank
        R.place[0][...] = place
        R.place[1][...] = jnp.concatenate([place, below], axis=0).T

    def fine_zero():
        halo_wait(R.hs[0], R.f.layers[0].tab, NF, R.hs_sem[0])
        project_rest(fine, 0)
        R.state_one[...] = forward(fine, 0, I.edge)

    def sink():
        pooled = (dot(pool_hot(), R.state_one[...]) * (1.0 / POOL)).astype(BF)
        flags = dot(flag_hot(), jnp.ones((BLOCKS, L), BF))
        R.ws[0][...] = (dot(put_hot(), pooled) + flags).astype(BF)
        wide_start(0)
        wide_wait(0)
        arrived = R.wr[0][...]
        R.live[...] = dot(narrow_hot(CAP), arrived)
        R.c.layers[0].tab[0:NC, :] = dot(narrow_hot(0), arrived).astype(BF)

    def coarse_layer(l):
        def run():
            start(near_table(l))
            project_own(coarse, l)
            wait(near_table(l))
            project_rest(coarse, l)
            new = forward(coarse, l, I.cedge if l == 0 else R.c.layers[0].e)
            if l == 0:
                R.c.layers[1].tab[0:NC, :] = new
            else:
                R.ws[1][...] = dot(widen_hot(), new).astype(BF)
                wide_start(1)

        return run

    def rise():
        wide_wait(1)
        picked = dot(take_hot(), R.wr[1][...]).astype(BF)
        R.f.layers[1].tab[0:NF, :] = (R.state_one[...].astype(F32) + dot(grow_hot(), picked)).astype(BF)
        halo_pick(R.f.layers[1].tab, 1)
        halo_start(R.hs[1], R.f.layers[1].tab, NF, R.hs_sem[1])
        project_own(fine, 1)
        halo_wait(R.hs[1], R.f.layers[1].tab, NF, R.hs_sem[1])
        project_rest(fine, 1)

    def fine_one():
        O.new_state[...] = forward(fine, 1, R.f.layers[0].e)

    def fine_one_back():
        backward(fine, 1, R.f.layers[0].e, I.cot[...], None, halo_back(2), True, sum_one)

    def sink_back():
        halo_add(2)
        grad_two = R.f.acc[...].astype(BF)
        R.grad_two[...] = grad_two
        R.ws[2][...] = dot(put_hot(), dot(pool_hot(), grad_two).astype(BF)).astype(BF)
        wide_start(2)
        sum_two(1)
        wide_wait(2)
        R.grad_c[...] = dot(narrow_hot(0), R.wr[2][...]).astype(BF)

    def coarse_back(l):
        def run():
            def send(values):
                R.ns[l][...] = values
                start(near_grad(l))

            edges, edge_grad = (I.cedge, R.c.de) if l == 0 else (R.c.layers[0].e, None)
            backward(coarse, l, edges, R.grad_c[...], edge_grad, send, l == 1, sum_one)
            if l == 1:
                sum_three(1)
            else:
                sum_two(3)
            wait(near_grad(l))
            dst = R.nr[l]
            total = R.c.acc[...] + dst[0:NC, :].astype(F32) + dst[NC : 2 * NC, :].astype(F32)
            R.grad_c[...] = total.astype(BF)

        return run

    def rise_back():
        R.ws[3][...] = dot(widen_hot(), R.grad_c[...]).astype(BF)
        wide_start(3)
        sum_four(1)
        sum_two(2)
        wide_wait(3)
        sunk = (dot(take_hot(), R.wr[3][...]) * (1.0 / POOL)).astype(BF)
        R.grad_one[...] = (R.grad_two[...].astype(F32) + dot(grow_hot(), sunk)).astype(BF)
        sum_three(3)

    def fine_zero_back():
        def weights_done(s):
            sum_three(2)
            sum_one(0)

        backward(fine, 0, I.edge, R.grad_one[...], R.f.de, halo_back(3), False, weights_done)

    def leave():
        sum_four(3)
        halo_add(3)
        sum_two(0)
        O.state_grad[...] = R.f.acc[...].astype(BF)
        sum_four(2)
        sum_end(1)
        sum_three(0)
        sum_end(3)
        sum_end(2)
        sum_four(0)
        sum_end(0)

    steps = (
        enter, prepare, fine_zero, sink, coarse_layer(0), coarse_layer(1), rise, fine_one, fine_one_back, sink_back,
        coarse_back(1), coarse_back(0), rise_back, fine_zero_back, leave,
    )
    for step in steps[:STEPS]:
        step()


def body(*arrays):
    arrays = list(arrays)
    for i, rows in ((3, EF // L), (4, EF // L), (7, EC // L), (8, EC // L)):
        arrays[i] = arrays[i].reshape(rows, L)
    outs = [jax.ShapeDtypeStruct((NF, L), BF)] * 2
    for _ in range(2):
        outs += [jax.ShapeDtypeStruct((2, rows, L), F32) for rows in (384, 128, 256, 128)]
    vm = pl.BlockSpec(memory_space=pltpu.VMEM)
    return pl.pallas_call(
        kernel,
        out_shape=tuple(outs),
        in_specs=[vm] * len(arrays),
        out_specs=tuple([vm] * len(outs)),
        scratch_shapes=flat(shapes()),
        compiler_params=pltpu.CompilerParams(
            collective_id=0, has_side_effects=True, vmem_limit_bytes=60 * 2**20
        ),
        cost_estimate=pl.CostEstimate(flops=40 * 10**9, bytes_accessed=8 * 2**20, transcendentals=4 * 10**6),
    )(*arrays)


def solution(mesh):
    rows = P(("fine", "coarse"), None)
    flat = P(("fine", "coarse"))
    placed = (rows, rows, rows, flat, flat, rows, rows, flat, flat, rows) + (P(),) * 8
    return jax.shard_map(
        body, mesh=mesh, in_specs=placed, out_specs=(rows, rows) + (P(),) * 8, check_vma=False
    )
```

```python
from types import SimpleNamespace

import jax
import jax.numpy as jnp
from jax import lax
from jax.experimental import pallas as pl
from jax.experimental.pallas import tpu as pltpu
from jax.sharding import PartitionSpec as P

BF = jnp.bfloat16
F32 = jnp.float32
I16 = jnp.int16
I32 = jnp.int32
F8 = jnp.float8_e4m3fn
MESH = pl.DeviceIdType.MESH

L = 128
NF, EF, HALO = 1024, 4096, 512
NC, EC = 160, 640
BLOCKS, POOL, CAP = 64, 16, 5
PAD = 16
N_FINE, N_COARSE = 4, 32
WIDE = N_COARSE * PAD
SET = 896
LATE = 256
OWNED = 32
EPS = 1e-05


def dot(a, b):
    return jnp.dot(a, b, preferred_element_type=F32)


def dot_nt(a, b):
    return lax.dot_general(a, b, (((1,), (1,)), ((), ())), preferred_element_type=F32)


def dot_tn(a, b):
    return lax.dot_general(a, b, (((0,), (0,)), ((), ())), preferred_element_type=F32)


def iota(shape, dim):
    return lax.broadcasted_iota(I32, shape, dim)


def ones_where(mask):
    return jnp.where(mask, jnp.asarray(1, BF), jnp.asarray(0, BF))


def lane_sum(x):
    return jnp.sum(x, axis=-1, keepdims=True)


def normed(y):
    center = y - lane_sum(y) * (1.0 / L)
    scale = lax.rsqrt(lane_sum(center * center) * (1.0 / L) + EPS)
    return center * scale, scale


def normed_back(dn, n, scale):
    return scale * (dn - lane_sum(dn) * (1.0 / L) - n * (lane_sum(dn * n) * (1.0 / L)))


def hot_columns(column, base, width, dtype):
    count = column.shape[0]
    lanes = iota((16, 128), 1).astype(I16)
    parts = []
    for start in range(0, width, 128):
        places = jnp.concatenate([lanes + jnp.asarray(base + start, I16)] * (count // 16), axis=0)
        parts.append(ones_where(column == places))
    hot = jnp.concatenate(parts, axis=1) if len(parts) > 1 else parts[0]
    return hot.astype(dtype)


def gather_rows(columns, table):
    total = None
    for column, base, width in columns:
        for k in range(0, width, 256):
            size = min(256, width - k)
            part = dot(hot_columns(column, k, size, table.dtype), table[base + k : base + k + size, :])
            total = part if total is None else total + part
    return total


def scatter_rows(rows_ref, data_ref, first, count, edges):
    down = iota((count, 128), 0).astype(I16)
    shift = jnp.asarray(first, I32).astype(I16)
    total = None
    for k in range(0, edges, 256):
        size = min(256, edges - k)
        parts = []
        for j in range(k // 128, (k + size) // 128):
            row = rows_ref[j] - shift
            parts.append(ones_where(down == jnp.concatenate([row] * (count // 16), axis=0)))
        hot = jnp.concatenate(parts, axis=1) if len(parts) > 1 else parts[0]
        part = dot(hot.astype(data_ref.dtype), data_ref[k : k + size, :])
        total = part if total is None else total + part
    return total


def column_peak(x):
    return jnp.max(jnp.abs(x), axis=0, keepdims=True)


def scale_for(peak):
    return jnp.exp2(7.0 - jnp.floor(jnp.log2(jnp.maximum(peak, 1e-30))))


def halves(x, scale):
    x = x * scale
    high = x.astype(F8)
    low = ((x - high.astype(F32)) * 16.0).astype(F8)
    return jnp.concatenate([high, low], axis=1)


def joined(pair, scale):
    return (pair[:, 0:L] + pair[:, L : 2 * L] * 0.0625) * (1.0 / scale)


def vm(*shape, dtype=F32):
    return pltpu.VMEM(shape, dtype)


def level_shapes(n, tab, own, e):
    def layer():
        return SimpleNamespace(
            tab=vm(tab, L, dtype=BF),
            slope=vm(e, L),
            hid=vm(e, L, dtype=BF),
            n=vm(e, L),
            scale=vm(e, L),
            e=vm(e, L, dtype=BF),
            g=vm(n, L, dtype=BF),
            slope2=vm(n, L),
            hid2=vm(n, L, dtype=BF),
            n2=vm(n, L),
            scale2=vm(n, L),
        )

    return SimpleNamespace(
        cs=vm(e, L, dtype=I16),
        cr=vm(e, L, dtype=I16),
        rs=vm(e // L, 16, L, dtype=I16),
        rr=vm(e // L, 16, L, dtype=I16),
        proj=vm(tab + own, L, dtype=BF),
        wide=vm(tab + own, L),
        proj8=vm(tab + own, 2 * L, dtype=F8),
        dz=vm(e, L, dtype=BF),
        e8=vm(e, 2 * L, dtype=F8),
        dg8=vm(own, 2 * L, dtype=F8),
        de=vm(e, L, dtype=BF),
        dg=vm(own, L, dtype=BF),
        acc=vm(n, L),
        layers=[layer(), layer()],
    )


def shapes():
    dma = pltpu.SemaphoreType.DMA
    return SimpleNamespace(
        f=level_shapes(NF, NF + HALO, NF, EF),
        c=level_shapes(NC, 512, 256, EC),
        state_one=vm(NF, L, dtype=BF),
        live=vm(NC, L),
        acc_b=vm(L, L),
        acc_e=vm(L, L),
        halo_col=vm(HALO, L, dtype=I16),
        halo_row=vm(HALO // L, 16, L, dtype=I16),
        grad_two=vm(NF, L, dtype=BF),
        grad_one=vm(NF, L, dtype=BF),
        grad_c=vm(NC, L, dtype=BF),
        place=[vm(BLOCKS, L, dtype=I32), vm(L, L, dtype=I32)],
        hs=[vm(HALO, L, dtype=BF) for _ in range(4)],
        hr=[vm(HALO, L, dtype=BF) for _ in range(2)],
        ws=[vm(WIDE, L, dtype=BF) for _ in range(4)],
        wr=[vm(WIDE, L, dtype=BF) for _ in range(4)],
        ns=vm(2 * NC, L, dtype=BF),
        nr=vm(2 * NC, L, dtype=BF),
        parts=vm(512, L, dtype=BF),
        gw=vm(4, SET, L, dtype=BF),
        late=vm(LATE, L),
        late_got=vm(LATE, L),
        late_quad=vm(N_FINE, 8, L),
        late_sum=vm(LATE, L),
        got=vm(4, N_COARSE * OWNED, L, dtype=BF),
        quad=vm(4, N_FINE, OWNED, L),
        sums=vm(4, N_COARSE * OWNED, L),
        one_sem=dma((5, 2)),
        two_sem=dma((5, 2, 3)),
        three_sem=dma((5, 2)),
        hs_sem=[dma((2, 3)) for _ in range(4)],
        ws_sem=[dma((2,)) for _ in range(4)],
        near_sem=[dma((2, 2)) for _ in range(2)],
    )


def flat(tree):
    if isinstance(tree, SimpleNamespace):
        return [leaf for part in vars(tree).values() for leaf in flat(part)]
    if isinstance(tree, list):
        return [leaf for part in tree for leaf in flat(part)]
    return [tree]


def rebuilt(tree, leaves):
    if isinstance(tree, SimpleNamespace):
        return SimpleNamespace(**{name: rebuilt(part, leaves) for name, part in vars(tree).items()})
    if isinstance(tree, list):
        return [rebuilt(part, leaves) for part in tree]
    return next(leaves)


def operands():
    def weights():
        return SimpleNamespace(ei=None, eo=None, ni=None, no=None)

    inputs = SimpleNamespace(
        node=None, edge=None, cedge=None, src=None, dst=None, halo=None, owner=None, csrc=None, cdst=None, cot=None,
        fw=weights(), cw=weights(),
    )
    outputs = SimpleNamespace(new_state=None, state_grad=None, sums=None)
    return inputs, outputs


STEPS = None


def kernel(*args):
    leaves = iter(args)
    I, O = (rebuilt(tree, leaves) for tree in operands())
    R = rebuilt(shapes(), leaves)
    f = lax.axis_index("fine")
    c = lax.axis_index("coarse")

    def fine_at(d):
        return lax.rem(f + d + N_FINE, N_FINE)

    def coarse_at(d):
        return lax.rem(c + d + N_COARSE, N_COARSE)

    def chunk(i, size, align=None):
        return pl.ds(pl.multiple_of(i * size, align or size), size)

    def remote(src, dst, send, recv, where):
        return pltpu.make_async_remote_copy(
            src_ref=src, dst_ref=dst, send_sem=send, recv_sem=recv, device_id=where, device_id_type=MESH
        )

    def wait_for(view, sem):
        pltpu.make_async_copy(view, view, sem).wait()

    barrier = pltpu.get_barrier_semaphore()

    def greet():
        for d in range(1, N_FINE):
            pl.semaphore_signal(barrier, inc=1, device_id=(fine_at(d), c), device_id_type=MESH)

        def one(d, carry):
            pl.semaphore_signal(barrier, inc=1, device_id=(f, coarse_at(d)), device_id_type=MESH)
            return carry

        lax.fori_loop(1, N_COARSE, one, 0)

    def spread(src, columns, rows, count):
        def one(j, carry):
            wide = jnp.broadcast_to(src[pl.ds(j, 1), :], (L, L))
            rows[j] = wide[:16, :].astype(I16)
            columns[chunk(j, L), :] = wide.T.astype(I16)
            return carry

        lax.fori_loop(0, count, one, 0)

    def halo_copies(src, dst, base, sem):
        out, back = [], []
        for d in range(1, N_FINE):
            q, at = fine_at(d), fine_at(-d)
            out.append(
                remote(
                    src.at[chunk(q, L), :],
                    dst.at[pl.ds(pl.multiple_of(base + f * L, L), L), :],
                    sem.at[0, d - 1],
                    sem.at[1, d - 1],
                    (q, c),
                )
            )
            back.append((dst.at[pl.ds(pl.multiple_of(base + at * L, L), L), :], sem.at[1, d - 1]))
        return out, back

    def halo_start(src, dst, base, sem):
        for copy in halo_copies(src, dst, base, sem)[0]:
            copy.start()
        dst[pl.ds(pl.multiple_of(base + f * L, L), L), :] = src[chunk(f, L), :]

    def halo_wait(src, dst, base, sem):
        out, back = halo_copies(src, dst, base, sem)
        for copy in out:
            copy.wait_send()
        for view, at in back:
            wait_for(view, at)

    def wide_start(k):
        src, dst, sem = R.ws[k], R.wr[k], R.ws_sem[k]

        def one(d, carry):
            o = coarse_at(d)
            remote(src.at[chunk(o, PAD), :], dst.at[chunk(c, PAD), :], sem.at[0], sem.at[1], (f, o)).start()
            return carry

        lax.fori_loop(N_COARSE // 2, N_COARSE, one, 0)
        lax.fori_loop(1, N_COARSE // 2, one, 0)
        dst[chunk(c, PAD), :] = src[chunk(c, PAD), :]

    def wide_wait(k):
        dst, sem = R.wr[k], R.ws_sem[k]
        wait_for(dst.at[pl.ds(0, WIDE - PAD), :], sem.at[0])
        wait_for(dst.at[pl.ds(0, WIDE - PAD), :], sem.at[1])

    def near_copies(up_src, up_dst, down_src, down_dst, sem):
        return (
            remote(up_src, up_dst, sem.at[0, 0], sem.at[1, 0], (f, coarse_at(1))),
            remote(down_src, down_dst, sem.at[0, 1], sem.at[1, 1], (f, coarse_at(-1))),
        )

    def summing(k, owners, block, src, got, quad, dst):
        sem, group_sem, last_sem = R.one_sem.at[k], R.two_sem.at[k], R.three_sem.at[k]
        mine = chunk(c, block)

        def owner(run):
            run() if owners == N_COARSE else pl.when(c < owners)(run)

        def other(run):
            if owners < N_COARSE:
                pl.when(c >= owners)(run)

        def group():
            return [
                remote(quad.at[f], quad.at[f], group_sem.at[0, d - 1], group_sem.at[1, d - 1], (fine_at(d), c))
                for d in range(1, N_FINE)
            ]

        def one():
            def send(d, carry):
                o = coarse_at(d)

                def go():
                    remote(src.at[chunk(o, block), :], got.at[mine, :], sem.at[0], sem.at[1], (f, o)).start()

                go() if owners == N_COARSE else pl.when(o < owners)(go)
                return carry

            lax.fori_loop(N_COARSE // 2, N_COARSE, send, 0)
            lax.fori_loop(1, N_COARSE // 2, send, 0)

        def two():
            def run():
                got[mine, :] = src[mine, :]
                wait_for(got.at[pl.ds(0, (owners - 1) * block), :], sem.at[0])
                wait_for(got.at[pl.ds(0, (N_COARSE - 1) * block), :], sem.at[1])
                parts = [got[j * block : (j + 1) * block, :].astype(F32) for j in range(N_COARSE)]
                while len(parts) > 1:
                    parts = [parts[j] + parts[j + 1] for j in range(0, len(parts), 2)]
                quad[f] = parts[0]
                for copy in group():
                    copy.start()

            owner(run)
            other(lambda: wait_for(got.at[pl.ds(0, owners * block), :], sem.at[0]))

        def three():
            def run():
                for copy in group():
                    copy.wait()
                dst[mine, :] = (quad[0] + quad[1]) + (quad[2] + quad[3])

                def send(d, carry):
                    o = coarse_at(d)
                    remote(dst.at[mine, :], dst.at[mine, :], last_sem.at[0], last_sem.at[1], (f, o)).start()
                    return carry

                lax.fori_loop(N_COARSE // 2, N_COARSE, send, 0)
                lax.fori_loop(1, N_COARSE // 2, send, 0)

            owner(run)

        def four():
            def run():
                wait_for(dst.at[pl.ds(0, (N_COARSE - 1) * block), :], last_sem.at[0])
                wait_for(dst.at[pl.ds(0, (owners - 1) * block), :], last_sem.at[1])

            owner(run)
            other(lambda: wait_for(dst.at[pl.ds(0, owners * block), :], last_sem.at[1]))

        return SimpleNamespace(one=one, two=two, three=three, four=four)

    def summing_set(s):
        first = LATE if s == 0 else 0
        count = SET - first
        work = summing(
            s, count // OWNED, OWNED, R.gw.at[s, pl.ds(first, count), :], R.got.at[s], R.quad.at[s], R.sums.at[s]
        )

        def end():
            work.four()
            O.sums[s, first:SET, :] = R.sums[s, 0:count, :]

        work.end = end
        return work

    total = [summing_set(s) for s in range(4)]
    late = summing(4, N_COARSE, 8, R.late, R.late_got, R.late_quad, R.late_sum)

    fine = SimpleNamespace(
        n=NF, used=NF + HALO, tab=NF + HALO, own=NF, e=EF, tile=1024, block=512, S=R.f, W=I.fw, first=0, masked=False
    )
    coarse = SimpleNamespace(
        n=NC, used=3 * NC, tab=512, own=256, e=EC, tile=EC, block=NC, S=R.c, W=I.cw, first=2, masked=True
    )

    def project_own(v, l):
        w, h = v.W.ei, v.S.layers[l].tab[0 : v.n, :]
        into = v.S.proj if v.masked else v.S.wide
        into[0 : v.n, :] = dot(h, w[l, 128:256, :]).astype(into.dtype)
        into[v.tab : v.tab + v.n, :] = dot(h, w[l, 256:384, :]).astype(into.dtype)

    def project_rest(v, l):
        rest = v.S.layers[l].tab[v.n : v.tab, :]
        into = v.S.proj if v.masked else v.S.wide
        into[v.n : v.tab, :] = dot(rest, v.W.ei[l, 128:256, :]).astype(into.dtype)

    def forward(v, l, edges):
        S, W, A = v.S, v.W, v.S.layers[l]
        if not v.masked:
            scale = scale_for(column_peak(S.wide[...]))
            S.proj8[...] = halves(S.wide[...], scale)

        def one(i, peak):
            rows = chunk(i, v.tile)
            old = edges[rows, :]
            columns = ((S.cs[rows, :], 0, v.tab), (S.cr[rows, :], v.tab, v.own))
            if v.masked:
                z = gather_rows(columns, S.proj)
            else:
                z = joined(gather_rows(columns, S.proj8), scale)
            z = z + dot(old, W.ei[l, 0:128, :])
            gate = jax.nn.sigmoid(z)
            hidden = z * gate
            A.slope[rows, :] = gate * (1.0 + z - hidden)
            hidden = hidden.astype(BF)
            A.hid[rows, :] = hidden
            values, spread_by = normed(dot(hidden, W.eo[l]))
            A.n[rows, :] = values
            A.scale[rows, :] = jnp.broadcast_to(spread_by, values.shape)
            new = (old.astype(F32) + values).astype(BF)
            A.e[rows, :] = new
            return jnp.maximum(peak, column_peak(new.astype(F32)))

        peak = lax.fori_loop(0, v.e // v.tile, one, jnp.zeros((1, L), F32))
        if not v.masked:
            scale = scale_for(peak)

            def split(i, carry):
                rows = chunk(i, v.tile)
                S.e8[rows, :] = halves(A.e[rows, :].astype(F32), scale)
                return carry

            lax.fori_loop(0, v.e // v.tile, split, 0)

        def two(i, carry):
            rows = chunk(i, v.block)
            if v.masked:
                g = scatter_rows(S.rr, A.e, i * v.block, v.block, v.e)
            else:
                g = joined(scatter_rows(S.rr, S.e8, i * v.block, v.block, v.e), scale)
            A.g[rows, :] = g.astype(BF)
            return carry

        lax.fori_loop(0, v.n // v.block, two, 0)
        h = A.tab[0 : v.n, :]
        z = dot(h, W.ni[l, 0:128, :]) + dot(A.g[...], W.ni[l, 128:256, :])
        gate = jax.nn.sigmoid(z)
        hidden = z * gate
        A.slope2[...] = gate * (1.0 + z - hidden)
        hidden = hidden.astype(BF)
        A.hid2[...] = hidden
        values, spread_by = normed(dot(hidden, W.no[l]))
        A.n2[...] = values
        A.scale2[...] = jnp.broadcast_to(spread_by, values.shape)
        new = h.astype(F32) + values
        if v.masked:
            new = new * R.live[...]
        return new.astype(BF)

    def backward(v, l, edges, grad, edge_grad, send_rest, keep_edge, edges_done):
        S, W, A = v.S, v.W, v.S.layers[l]
        s, acc, gw = v.first + l, v.S.acc, R.gw
        dn = grad.astype(F32)
        if v.masked:
            dn = dn * R.live[...]
        dy = normed_back(dn, A.n2[...], A.scale2[...]).astype(BF)
        dz = (dot_nt(dy, W.no[l]) * A.slope2[...]).astype(BF)
        h = A.tab[0 : v.n, :]
        dg = dot_nt(dz, W.ni[l, 128:256, :])
        if v.masked:
            S.dg[0 : v.n, :] = dg.astype(BF)
        else:
            dg_scale = scale_for(column_peak(dg))
            S.dg8[...] = halves(dg, dg_scale)
        acc[...] = dn + dot_nt(dz, W.ni[l, 0:128, :])
        gw[s, 512:640, :] = dot_tn(h, dz).astype(BF)
        gw[s, 640:768, :] = dot_tn(A.g[...], dz).astype(BF)
        gw[s, 768:896, :] = dot_tn(A.hid2[...], dy).astype(BF)
        R.acc_b[...] = jnp.zeros((L, L), F32)
        R.acc_e[...] = jnp.zeros((L, L), F32)

        def one(i, peak):
            rows = chunk(i, v.tile)
            columns = ((S.cr[rows, :], 0, v.own),)
            if v.masked:
                dn = gather_rows(columns, S.dg)
            else:
                dn = joined(gather_rows(columns, S.dg8), dg_scale)
            if edge_grad is not None:
                dn = dn + edge_grad[rows, :].astype(F32)
            dy = normed_back(dn, A.n[rows, :], A.scale[rows, :]).astype(BF)
            dz = (dot_nt(dy, W.eo[l]) * A.slope[rows, :]).astype(BF)
            S.dz[rows, :] = dz
            R.acc_b[...] += dot_tn(A.hid[rows, :], dy)
            R.acc_e[...] += dot_tn(edges[rows, :], dz)
            if keep_edge:
                S.de[rows, :] = (dn + dot_nt(dz, W.ei[l, 0:128, :])).astype(BF)
            return jnp.maximum(peak, column_peak(dz.astype(F32)))

        peak = lax.fori_loop(0, v.e // v.tile, one, jnp.zeros((1, L), F32))
        if v.masked:

            def spread_back(rows_ref, first, count):
                return scatter_rows(rows_ref, S.dz, first, count, v.e).astype(BF)

        else:
            scale = scale_for(peak)

            def split(i, carry):
                rows = chunk(i, v.tile)
                S.e8[rows, :] = halves(S.dz[rows, :].astype(F32), scale)
                return carry

            lax.fori_loop(0, v.e // v.tile, split, 0)

            def spread_back(rows_ref, first, count):
                return joined(scatter_rows(rows_ref, S.e8, first, count, v.e), scale).astype(BF)

        gw[s, 256:384, :] = R.acc_e[...].astype(BF)
        gw[s, 384:512, :] = R.acc_b[...].astype(BF)
        edges_done()
        rest = spread_back(S.rs, v.n, v.used - v.n)
        send_rest(dot_nt(rest, W.ei[l, 128:256, :]).astype(BF))
        R.acc_b[...] = dot_tn(A.tab[v.n : v.used, :], rest)
        R.acc_e[...] = jnp.zeros((L, L), F32)

        def two(i, carry):
            rows = chunk(i, v.block)
            h = A.tab[rows, :]
            part = spread_back(S.rs, i * v.block, v.block)
            R.acc_b[...] += dot_tn(h, part)
            other = spread_back(S.rr, i * v.block, v.block)
            R.acc_e[...] += dot_tn(h, other)
            acc[rows, :] += dot_nt(part, W.ei[l, 128:256, :]) + dot_nt(other, W.ei[l, 256:384, :])
            return carry

        lax.fori_loop(0, v.n // v.block, two, 0)
        gw[s, 0:128, :] = R.acc_b[...].astype(BF)
        gw[s, 128:256, :] = R.acc_e[...].astype(BF)

    def place_column():
        return R.place[0][...]

    def place_wide():
        return jnp.broadcast_to(R.place[1][0:1, :], (WIDE, L))

    def pool_hot():
        return ones_where((iota((BLOCKS, NF), 1) >> 4) == iota((BLOCKS, NF), 0))

    def grow_hot():
        return ones_where((iota((NF, L), 0) >> 4) == iota((NF, L), 1))[:, 0:BLOCKS]

    def put_hot():
        return ones_where(iota((WIDE, L), 0) == place_wide())[:, 0:BLOCKS]

    def three_places(owner, rank):
        places = []
        for part, shift in ((0, 0), (1, 1), (2, N_COARSE - 1)):
            places.append(((owner + shift) & (N_COARSE - 1)) * PAD + part * CAP + rank)
        return places

    def put_three():
        wide = place_wide()
        down = iota((WIDE, L), 0)
        a, b, d = three_places(wide >> 4, wide & (PAD - 1))
        return ones_where((down == a) | (down == b) | (down == d))[:, 0:BLOCKS]

    def put_flags():
        row = ones_where(iota((WIDE, L), 0) == (place_wide() | (PAD - 1)))[:, 0:BLOCKS]
        lane = ones_where(iota((BLOCKS, L), 1) == (place_column() & (PAD - 1)))
        return dot(row, lane)

    def take_hot():
        return ones_where(jnp.concatenate([place_column()] * 4, axis=1) == iota((BLOCKS, WIDE), 1))

    def take_three():
        place = place_column()
        across = iota((BLOCKS, WIDE), 1)
        a, b, d = (jnp.concatenate([at] * 4, axis=1) for at in three_places(place >> 4, place & (PAD - 1)))
        return ones_where((across == a) | (across == b) | (across == d))

    def slot_of(index):
        within = index & (PAD - 1)
        return jnp.where(within < CAP, (index >> 4) * CAP + within, -1)

    def three_of(index):
        within = index & (PAD - 1)
        part = jnp.where(within >= 2 * CAP, 2, jnp.where(within >= CAP, 1, 0))
        return jnp.where(within < 3 * CAP, part * (NC - CAP) + (index >> 4) * CAP + within, -1)

    def across_hot(rows, places):
        down = iota((rows, 128), 0).astype(I16)
        parts = []
        for k in range(0, WIDE, 128):
            at = places(iota((16, 128), 1) + k).astype(I16)
            parts.append(ones_where(down == jnp.concatenate([at] * (rows // 16), axis=0)))
        return jnp.concatenate(parts, axis=1)

    def apart_hot(places, width):
        at = places(iota((WIDE, 128), 0)).astype(I16)
        lanes = iota((16, 128), 1).astype(I16)
        parts = []
        for k in range(0, width, 128):
            here = jnp.concatenate([lanes + jnp.asarray(k, I16)] * (WIDE // 16), axis=0)
            parts.append(ones_where(at == here))
        return jnp.concatenate(parts, axis=1)

    def live_rows(arrived):
        slot = iota((NC, WIDE), 0)
        first = (iota((NC, WIDE), 1) >> 4) * CAP
        last_row = (iota((NC, WIDE), 1) & (PAD - 1)) == PAD - 1
        row = dot(ones_where(last_row & (slot >= first) & (slot < first + CAP)), arrived)
        count = iota((NC, L), 0).astype(F32)
        within = iota((NC, L), 0) - jnp.floor((count + 0.5) * (1.0 / CAP)).astype(I32) * CAP
        return jnp.broadcast_to(lane_sum(jnp.where(iota((NC, L), 1) == within, row, 0.0)), (NC, L))

    def halo_pick(tab, k):
        R.hs[k][...] = gather_rows(((R.halo_col[...], 0, NF),), tab).astype(BF)

    def halo_back(k):
        def send(values):
            R.hs[k][...] = values
            halo_start(R.hs[k], R.hr[k - 2], 0, R.hs_sem[k])

        return send

    def halo_add(k):
        halo_wait(R.hs[k], R.hr[k - 2], 0, R.hs_sem[k])

        def one(i, carry):
            rows = chunk(i, 512)
            R.f.acc[rows, :] += scatter_rows(R.halo_row, R.hr[k - 2], i * 512, 512, HALO)
            return carry

        lax.fori_loop(0, NF // 512, one, 0)

    def near_table():
        tab = R.c.layers[1].tab
        own = tab.at[pl.ds(0, NC), :]
        return near_copies(own, tab.at[pl.ds(NC, NC), :], own, tab.at[pl.ds(2 * NC, NC), :], R.near_sem[0])

    def near_grad():
        low, high = pl.ds(0, NC), pl.ds(NC, NC)
        return near_copies(
            R.ns.at[high, :], R.nr.at[low, :], R.ns.at[low, :], R.nr.at[high, :], R.near_sem[1]
        )

    def start(copies):
        for copy in copies:
            copy.start()

    def wait(copies):
        for copy in copies:
            copy.wait()

    def nothing():
        pass

    def enter():
        greet()
        spread(I.halo, R.halo_col, R.halo_row, HALO // L)
        halo_pick(I.node, 0)
        spread(I.src, R.f.cs, R.f.rs, EF // L)
        spread(I.dst, R.f.cr, R.f.rr, EF // L)
        pl.semaphore_wait(barrier, N_FINE - 1 + N_COARSE - 1)
        halo_start(R.hs[0], R.f.layers[0].tab, NF, R.hs_sem[0])

    def prepare():
        R.f.layers[0].tab[0:NF, :] = I.node[...]
        project_own(fine, 0)
        spread(I.csrc, R.c.cs, R.c.rs, EC // L)
        spread(I.cdst, R.c.cr, R.c.rr, EC // L)
        R.c.layers[1].tab[3 * NC : 512, :] = jnp.zeros((512 - 3 * NC, L), BF)
        R.parts[3 * NC : 512, :] = jnp.zeros((512 - 3 * NC, L), BF)
        R.c.proj[512 + NC : 768, :] = jnp.zeros((256 - NC, L), BF)
        R.c.dg[NC:256, :] = jnp.zeros((256 - NC, L), BF)
        owner = jnp.broadcast_to(I.owner[...], (BLOCKS, L))
        below = jnp.full((L - BLOCKS, L), -1, I32)
        square = jnp.concatenate([owner, below], axis=0).T
        same = (owner == square[0:BLOCKS, :]) & (iota((BLOCKS, L), 1) < iota((BLOCKS, L), 0))
        rank = lane_sum(jnp.where(same, 1.0, 0.0)).astype(I32)
        place = owner * PAD + rank
        R.place[0][...] = place
        R.place[1][...] = jnp.concatenate([place, below], axis=0).T

    def fine_zero():
        halo_wait(R.hs[0], R.f.layers[0].tab, NF, R.hs_sem[0])
        project_rest(fine, 0)
        R.state_one[...] = forward(fine, 0, I.edge)

    def sink():
        pooled = (dot(pool_hot(), R.state_one[...]) * (1.0 / POOL)).astype(BF)
        R.ws[0][...] = (dot(put_three(), pooled) + put_flags()).astype(BF)
        wide_start(0)
        wide_wait(0)
        arrived = R.wr[0][...]
        R.c.layers[0].tab[...] = dot(across_hot(512, three_of), arrived).astype(BF)
        R.live[...] = live_rows(arrived)

    def coarse_layer(l):
        def run():
            if l == 1:
                start(near_table())
            project_own(coarse, l)
            if l == 1:
                wait(near_table())
            project_rest(coarse, l)
            new = forward(coarse, l, I.cedge if l == 0 else R.c.layers[0].e)
            if l == 0:
                R.c.layers[1].tab[0:NC, :] = new
            else:
                R.ws[1][...] = dot(apart_hot(slot_of, 256)[:, 0:NC], new).astype(BF)
                wide_start(1)

        return run

    def rise():
        wide_wait(1)
        picked = dot(take_hot(), R.wr[1][...]).astype(BF)
        R.f.layers[1].tab[0:NF, :] = (R.state_one[...].astype(F32) + dot(grow_hot(), picked)).astype(BF)
        halo_pick(R.f.layers[1].tab, 1)
        halo_start(R.hs[1], R.f.layers[1].tab, NF, R.hs_sem[1])
        project_own(fine, 1)
        halo_wait(R.hs[1], R.f.layers[1].tab, NF, R.hs_sem[1])
        project_rest(fine, 1)

    def fine_one():
        O.new_state[...] = forward(fine, 1, R.f.layers[0].e)

    def fine_one_back():
        backward(fine, 1, R.f.layers[0].e, I.cot[...], None, halo_back(2), True, nothing)

    def sink_back():
        halo_add(2)
        grad_two = R.f.acc[...].astype(BF)
        R.grad_two[...] = grad_two
        R.ws[2][...] = dot(put_hot(), dot(pool_hot(), grad_two).astype(BF)).astype(BF)
        wide_start(2)
        total[1].one()
        wide_wait(2)
        R.grad_c[...] = dot(across_hot(NC, slot_of), R.wr[2][...]).astype(BF)

    def coarse_back(l):
        def run():
            def send(values):
                if l == 1:
                    R.ns[...] = values
                    start(near_grad())
                else:
                    R.parts[NC : 3 * NC, :] = values

            edges, edge_grad = (I.cedge, R.c.de) if l == 0 else (R.c.layers[0].e, None)
            backward(coarse, l, edges, R.grad_c[...], edge_grad, send, l == 1, nothing)
            if l == 1:
                total[3].one()
                total[1].two()
                wait(near_grad())
                grad = R.c.acc[...] + R.nr[0:NC, :].astype(F32) + R.nr[NC : 2 * NC, :].astype(F32)
                R.grad_c[...] = grad.astype(BF)
            else:
                R.parts[0:NC, :] = R.c.acc[...].astype(BF)
                R.ws[3][...] = dot(apart_hot(three_of, 512), R.parts[...]).astype(BF)
                wide_start(3)

        return run

    def rise_back():
        total[2].one()
        total[1].three()
        total[3].two()
        wide_wait(3)
        sunk = (dot(take_three(), R.wr[3][...]).astype(BF).astype(F32) * (1.0 / POOL)).astype(BF)
        R.grad_one[...] = (R.grad_two[...].astype(F32) + dot(grow_hot(), sunk)).astype(BF)

    def fine_zero_back():
        def edges_done():
            total[0].one()
            total[2].two()
            total[3].three()

        backward(fine, 0, I.edge, R.grad_one[...], R.f.de, halo_back(3), False, edges_done)
        R.late[...] = R.gw[0, 0:LATE, :].astype(F32)
        late.one()

    def leave():
        total[0].two()
        total[2].three()
        halo_add(3)
        O.state_grad[...] = R.f.acc[...].astype(BF)
        late.two()
        total[0].three()
        total[1].end()
        late.three()
        total[3].end()
        total[2].end()
        total[0].end()
        late.four()
        O.sums[0, 0:LATE, :] = R.late_sum[...]

    steps = (
        enter, prepare, fine_zero, sink, coarse_layer(0), coarse_layer(1), rise, fine_one, fine_one_back, sink_back,
        coarse_back(1), coarse_back(0), rise_back, fine_zero_back, leave,
    )
    for step in steps[:STEPS]:
        step()


def spread_out(state, grad, sums, *refs):
    outs, sem = refs[:-1], refs[-1]
    pairs = [(state, outs[0]), (grad, outs[1])]
    for s in range(4):
        ei, eo, ni, no = outs[2 + 4 * (s // 2) : 6 + 4 * (s // 2)]
        l = s % 2
        for out, there, here, rows in (
            (ei, 0, 256, 128), (ei, 128, 0, 256), (eo, 0, 384, 128), (ni, 0, 512, 256), (no, 0, 768, 128)
        ):
            pairs.append((sums.at[s, pl.ds(here, rows), :], out.at[l, pl.ds(there, rows), :]))
    copies = [pltpu.make_async_copy(src, dst, sem.at[k]) for k, (src, dst) in enumerate(pairs)]
    for copy in copies:
        copy.start()
    for copy in copies:
        copy.wait()


def body(*arrays):
    arrays = list(arrays)
    for i, rows in ((3, EF // L), (4, EF // L), (7, EC // L), (8, EC // L)):
        arrays[i] = arrays[i].reshape(rows, L)
    states = [jax.ShapeDtypeStruct((NF, L), BF)] * 2
    vm_spec = pl.BlockSpec(memory_space=pltpu.VMEM)
    any_spec = pl.BlockSpec(memory_space=pl.ANY)
    results = pl.pallas_call(
        kernel,
        out_shape=tuple(states + [jax.ShapeDtypeStruct((4, SET, L), F32)]),
        in_specs=[vm_spec] * len(arrays),
        out_specs=(vm_spec,) * 3,
        scratch_shapes=flat(shapes()),
        compiler_params=pltpu.CompilerParams(
            collective_id=0, has_side_effects=True, vmem_limit_bytes=60 * 2**20
        ),
        cost_estimate=pl.CostEstimate(flops=40 * 10**9, bytes_accessed=8 * 2**20, transcendentals=4 * 10**6),
    )(*arrays)
    outs = list(states)
    for _ in range(2):
        outs += [jax.ShapeDtypeStruct((2, rows, L), F32) for rows in (384, 128, 256, 128)]
    return pl.pallas_call(
        spread_out,
        out_shape=tuple(outs),
        in_specs=[vm_spec] * 3,
        out_specs=(any_spec,) * len(outs),
        scratch_shapes=[pltpu.SemaphoreType.DMA((22,))],
    )(*results)


def solution(mesh):
    rows = P(("fine", "coarse"), None)
    flat = P(("fine", "coarse"))
    placed = (rows, rows, rows, flat, flat, rows, rows, flat, flat, rows) + (P(),) * 8
    return jax.shard_map(
        body, mesh=mesh, in_specs=placed, out_specs=(rows, rows) + (P(),) * 8, check_vma=False
    )
```

```python
from types import SimpleNamespace

import jax
import jax.numpy as jnp
from jax import lax
from jax.experimental import pallas as pl
from jax.experimental.pallas import tpu as pltpu
from jax.sharding import PartitionSpec as P

BF = jnp.bfloat16
F32 = jnp.float32
I16 = jnp.int16
I32 = jnp.int32
F8 = jnp.float8_e4m3fn
MESH = pl.DeviceIdType.MESH

L = 128
NF, EF, HALO = 1024, 4096, 512
NC, EC = 160, 640
BLOCKS, POOL, CAP = 64, 16, 5
PAD = 16
N_FINE, N_COARSE = 4, 32
WIDE = N_COARSE * PAD
SET = 896
LATE = 256
OWNED = 32
EPS = 1e-05


def dot(a, b):
    return jnp.dot(a, b, preferred_element_type=F32)


def dot_nt(a, b):
    return lax.dot_general(a, b, (((1,), (1,)), ((), ())), preferred_element_type=F32)


def dot_tn(a, b):
    return lax.dot_general(a, b, (((0,), (0,)), ((), ())), preferred_element_type=F32)


def iota(shape, dim):
    return lax.broadcasted_iota(I32, shape, dim)


def ones_where(mask):
    return jnp.where(mask, jnp.asarray(1, BF), jnp.asarray(0, BF))


def lane_sum(x):
    return jnp.sum(x, axis=-1, keepdims=True)


def normed(y):
    center = y - lane_sum(y) * (1.0 / L)
    scale = lax.rsqrt(lane_sum(center * center) * (1.0 / L) + EPS)
    return center * scale, scale


def normed_back(dn, n, scale):
    return scale * (dn - lane_sum(dn) * (1.0 / L) - n * (lane_sum(dn * n) * (1.0 / L)))


def hot_columns(column, base, width, dtype):
    count = column.shape[0]
    lanes = iota((16, 128), 1).astype(I16)
    parts = []
    for start in range(0, width, 128):
        places = jnp.concatenate([lanes + jnp.asarray(base + start, I16)] * (count // 16), axis=0)
        parts.append(ones_where(column == places))
    hot = jnp.concatenate(parts, axis=1) if len(parts) > 1 else parts[0]
    return hot.astype(dtype)


def gather_rows(columns, table):
    total = None
    for column, first, base, width in columns:
        for k in range(0, width, 256):
            size = min(256, width - k)
            part = dot(hot_columns(column, first + k, size, table.dtype), table[base + k : base + k + size, :])
            total = part if total is None else total + part
    return total


def scatter_rows(rows_ref, data_ref, first, count, edges):
    down = iota((count, 128), 0).astype(I16)
    shift = jnp.asarray(first, I32).astype(I16)
    total = None
    for k in range(0, edges, 256):
        size = min(256, edges - k)
        parts = []
        for j in range(k // 128, (k + size) // 128):
            row = rows_ref[j] - shift
            parts.append(ones_where(down == jnp.concatenate([row] * (count // 16), axis=0)))
        hot = jnp.concatenate(parts, axis=1) if len(parts) > 1 else parts[0]
        part = dot(hot.astype(data_ref.dtype), data_ref[k : k + size, :])
        total = part if total is None else total + part
    return total


def column_peak(x):
    return jnp.max(jnp.abs(x), axis=0, keepdims=True)


def scale_for(peak):
    return jnp.exp2(7.0 - jnp.floor(jnp.log2(jnp.maximum(peak, 1e-30))))


def halves(x, scale):
    x = x * scale
    high = x.astype(F8)
    low = ((x - high.astype(F32)) * 16.0).astype(F8)
    return jnp.concatenate([high, low], axis=1)


def joined(pair, scale):
    return (pair[:, 0:L] + pair[:, L : 2 * L] * 0.0625) * (1.0 / scale)


def vm(*shape, dtype=F32):
    return pltpu.VMEM(shape, dtype)


def level_shapes(n, tab, own, e):
    def layer():
        return SimpleNamespace(
            tab=vm(tab, L, dtype=BF),
            slope=vm(e, L),
            hid=vm(e, L, dtype=BF),
            n=vm(e, L),
            scale=vm(e, L),
            e=vm(e, L, dtype=BF),
            g=vm(n, L, dtype=BF),
            slope2=vm(n, L),
            hid2=vm(n, L, dtype=BF),
            n2=vm(n, L),
            scale2=vm(n, L),
        )

    return SimpleNamespace(
        cs=vm(e, L, dtype=I16),
        cr=vm(e, L, dtype=I16),
        rs=vm(e // L, 16, L, dtype=I16),
        rr=vm(e // L, 16, L, dtype=I16),
        proj=vm(tab + own, L, dtype=BF),
        wide=vm(tab + own, L),
        proj8=vm(tab + own, 2 * L, dtype=F8),
        dz=vm(e, L, dtype=BF),
        e8=vm(e, 2 * L, dtype=F8),
        dg8=vm(own, 2 * L, dtype=F8),
        de=vm(e, L, dtype=BF),
        dg=vm(own, L, dtype=BF),
        dy=vm(e, L, dtype=BF),
        ndy=vm(n, L, dtype=BF),
        ndz=vm(n, L, dtype=BF),
        part=vm(tab, L, dtype=BF),
        other=vm(n, L, dtype=BF),
        acc=vm(n, L),
        layers=[layer(), layer()],
    )


def shapes():
    dma = pltpu.SemaphoreType.DMA
    return SimpleNamespace(
        f=level_shapes(NF, NF + HALO, NF, EF),
        c=level_shapes(NC, 512, 256, EC),
        state_one=vm(NF, L, dtype=BF),
        live=vm(NC, L),
        acc_b=vm(L, L),
        acc_e=vm(L, L),
        block_s=vm(EF, L, dtype=I16),
        block_r=vm(EF, L, dtype=I16),
        delta=vm(2 * BLOCKS + HALO, L),
        halo_col=vm(HALO, L, dtype=I16),
        halo_row=vm(HALO // L, 16, L, dtype=I16),
        grad_two=vm(NF, L, dtype=BF),
        grad_one=vm(NF, L, dtype=BF),
        grad_c=vm(NC, L, dtype=BF),
        place=[vm(BLOCKS, L, dtype=I32), vm(L, L, dtype=I32)],
        hs=[vm(HALO, L, dtype=BF) for _ in range(4)],
        hr=[vm(HALO, L, dtype=BF) for _ in range(2)],
        ws=[vm(WIDE, L, dtype=BF) for _ in range(4)],
        wr=[vm(WIDE, L, dtype=BF) for _ in range(4)],
        ns=vm(2 * NC, L, dtype=BF),
        nr=vm(2 * NC, L, dtype=BF),
        parts=vm(512, L, dtype=BF),
        gw=vm(4, SET, L, dtype=BF),
        late=vm(LATE, L),
        late_got=vm(LATE, L),
        late_quad=vm(N_FINE, 8, L),
        late_sum=vm(LATE, L),
        got=vm(4, N_COARSE * OWNED, L, dtype=BF),
        quad=vm(4, N_FINE, OWNED, L),
        sums=vm(4, N_COARSE * OWNED, L),
        one_sem=dma((5, 2)),
        two_sem=dma((5, 2, 3)),
        three_sem=dma((5, 2)),
        hs_sem=[dma((2, 3)) for _ in range(4)],
        ws_sem=[dma((2,)) for _ in range(4)],
        near_sem=[dma((2, 2)) for _ in range(2)],
    )


def flat(tree):
    if isinstance(tree, SimpleNamespace):
        return [leaf for part in vars(tree).values() for leaf in flat(part)]
    if isinstance(tree, list):
        return [leaf for part in tree for leaf in flat(part)]
    return [tree]


def rebuilt(tree, leaves):
    if isinstance(tree, SimpleNamespace):
        return SimpleNamespace(**{name: rebuilt(part, leaves) for name, part in vars(tree).items()})
    if isinstance(tree, list):
        return [rebuilt(part, leaves) for part in tree]
    return next(leaves)


def operands():
    def weights():
        return SimpleNamespace(ei=None, eo=None, ni=None, no=None)

    inputs = SimpleNamespace(
        node=None, edge=None, cedge=None, src=None, dst=None, halo=None, owner=None, csrc=None, cdst=None, cot=None,
        fw=weights(), cw=weights(),
    )
    outputs = SimpleNamespace(new_state=None, state_grad=None, sums=None)
    return inputs, outputs


STEPS = None


def kernel(*args):
    leaves = iter(args)
    I, O = (rebuilt(tree, leaves) for tree in operands())
    R = rebuilt(shapes(), leaves)
    f = lax.axis_index("fine")
    c = lax.axis_index("coarse")

    def fine_at(d):
        return lax.rem(f + d + N_FINE, N_FINE)

    def coarse_at(d):
        return lax.rem(c + d + N_COARSE, N_COARSE)

    def chunk(i, size, align=None):
        return pl.ds(pl.multiple_of(i * size, align or size), size)

    def remote(src, dst, send, recv, where):
        return pltpu.make_async_remote_copy(
            src_ref=src, dst_ref=dst, send_sem=send, recv_sem=recv, device_id=where, device_id_type=MESH
        )

    def wait_for(view, sem):
        pltpu.make_async_copy(view, view, sem).wait()

    barrier = pltpu.get_barrier_semaphore()

    def greet():
        for d in range(1, N_FINE):
            pl.semaphore_signal(barrier, inc=1, device_id=(fine_at(d), c), device_id_type=MESH)

        def one(d, carry):
            pl.semaphore_signal(barrier, inc=1, device_id=(f, coarse_at(d)), device_id_type=MESH)
            return carry

        lax.fori_loop(1, N_COARSE, one, 0)

    def spread(src, columns, rows, count, blocks=None, shift=0):
        def one(j, carry):
            wide = jnp.broadcast_to(src[pl.ds(j, 1), :], (L, L))
            rows[j] = wide[:16, :].astype(I16)
            tall = wide.T
            columns[chunk(j, L), :] = tall.astype(I16)
            if blocks is not None:
                blocks[chunk(j, L), :] = jnp.where(tall < NF, (tall >> 4) + shift, -1).astype(I16)
            return carry

        lax.fori_loop(0, count, one, 0)

    def halo_copies(src, dst, base, sem):
        out, back = [], []
        for d in range(1, N_FINE):
            q, at = fine_at(d), fine_at(-d)
            out.append(
                remote(
                    src.at[chunk(q, L), :],
                    dst.at[pl.ds(pl.multiple_of(base + f * L, L), L), :],
                    sem.at[0, d - 1],
                    sem.at[1, d - 1],
                    (q, c),
                )
            )
            back.append((dst.at[pl.ds(pl.multiple_of(base + at * L, L), L), :], sem.at[1, d - 1]))
        return out, back

    def halo_start(src, dst, base, sem):
        for copy in halo_copies(src, dst, base, sem)[0]:
            copy.start()
        dst[pl.ds(pl.multiple_of(base + f * L, L), L), :] = src[chunk(f, L), :]

    def halo_wait(src, dst, base, sem):
        out, back = halo_copies(src, dst, base, sem)
        for copy in out:
            copy.wait_send()
        for view, at in back:
            wait_for(view, at)

    def wide_start(k):
        src, dst, sem = R.ws[k], R.wr[k], R.ws_sem[k]

        def one(d, carry):
            o = coarse_at(d)
            remote(src.at[chunk(o, PAD), :], dst.at[chunk(c, PAD), :], sem.at[0], sem.at[1], (f, o)).start()
            return carry

        lax.fori_loop(N_COARSE // 2, N_COARSE, one, 0)
        lax.fori_loop(1, N_COARSE // 2, one, 0)
        dst[chunk(c, PAD), :] = src[chunk(c, PAD), :]

    def wide_wait(k):
        dst, sem = R.wr[k], R.ws_sem[k]
        wait_for(dst.at[pl.ds(0, WIDE - PAD), :], sem.at[0])
        wait_for(dst.at[pl.ds(0, WIDE - PAD), :], sem.at[1])

    def near_copies(up_src, up_dst, down_src, down_dst, sem):
        return (
            remote(up_src, up_dst, sem.at[0, 0], sem.at[1, 0], (f, coarse_at(1))),
            remote(down_src, down_dst, sem.at[0, 1], sem.at[1, 1], (f, coarse_at(-1))),
        )

    def summing(k, owners, block, src, got, quad, dst):
        sem, group_sem, last_sem = R.one_sem.at[k], R.two_sem.at[k], R.three_sem.at[k]
        mine = chunk(c, block)

        def owner(run):
            run() if owners == N_COARSE else pl.when(c < owners)(run)

        def other(run):
            if owners < N_COARSE:
                pl.when(c >= owners)(run)

        def group():
            return [
                remote(quad.at[f], quad.at[f], group_sem.at[0, d - 1], group_sem.at[1, d - 1], (fine_at(d), c))
                for d in range(1, N_FINE)
            ]

        def one():
            def send(d, carry):
                o = coarse_at(d)

                def go():
                    remote(src.at[chunk(o, block), :], got.at[mine, :], sem.at[0], sem.at[1], (f, o)).start()

                go() if owners == N_COARSE else pl.when(o < owners)(go)
                return carry

            lax.fori_loop(N_COARSE // 2, N_COARSE, send, 0)
            lax.fori_loop(1, N_COARSE // 2, send, 0)

        def two():
            def run():
                got[mine, :] = src[mine, :]
                wait_for(got.at[pl.ds(0, (owners - 1) * block), :], sem.at[0])
                wait_for(got.at[pl.ds(0, (N_COARSE - 1) * block), :], sem.at[1])
                parts = [got[j * block : (j + 1) * block, :].astype(F32) for j in range(N_COARSE)]
                while len(parts) > 1:
                    parts = [parts[j] + parts[j + 1] for j in range(0, len(parts), 2)]
                quad[f] = parts[0]
                for copy in group():
                    copy.start()

            owner(run)
            other(lambda: wait_for(got.at[pl.ds(0, owners * block), :], sem.at[0]))

        def three():
            def run():
                for copy in group():
                    copy.wait()
                dst[mine, :] = (quad[0] + quad[1]) + (quad[2] + quad[3])

                def send(d, carry):
                    o = coarse_at(d)
                    remote(dst.at[mine, :], dst.at[mine, :], last_sem.at[0], last_sem.at[1], (f, o)).start()
                    return carry

                lax.fori_loop(N_COARSE // 2, N_COARSE, send, 0)
                lax.fori_loop(1, N_COARSE // 2, send, 0)

            owner(run)

        def four():
            def run():
                wait_for(dst.at[pl.ds(0, (N_COARSE - 1) * block), :], last_sem.at[0])
                wait_for(dst.at[pl.ds(0, (owners - 1) * block), :], last_sem.at[1])

            owner(run)
            other(lambda: wait_for(dst.at[pl.ds(0, owners * block), :], last_sem.at[1]))

        return SimpleNamespace(one=one, two=two, three=three, four=four)

    def summing_set(s):
        first = LATE if s == 0 else 0
        count = SET - first
        work = summing(
            s, count // OWNED, OWNED, R.gw.at[s, pl.ds(first, count), :], R.got.at[s], R.quad.at[s], R.sums.at[s]
        )

        def end():
            work.four()
            O.sums[s, first:SET, :] = R.sums[s, 0:count, :]

        work.end = end
        return work

    total = [summing_set(s) for s in range(4)]
    late = summing(4, N_COARSE, 8, R.late, R.late_got, R.late_quad, R.late_sum)

    fine = SimpleNamespace(
        n=NF, used=NF + HALO, tab=NF + HALO, own=NF, e=EF, tile=1024, block=512, S=R.f, W=I.fw, first=0, masked=False
    )
    coarse = SimpleNamespace(
        n=NC, used=3 * NC, tab=512, own=256, e=EC, tile=EC, block=NC, S=R.c, W=I.cw, first=2, masked=True
    )

    def project_own(v, l):
        w, h = v.W.ei, v.S.layers[l].tab[0 : v.n, :]
        into = v.S.proj if v.masked else v.S.wide
        into[0 : v.n, :] = dot(h, w[l, 128:256, :]).astype(into.dtype)
        into[v.tab : v.tab + v.n, :] = dot(h, w[l, 256:384, :]).astype(into.dtype)

    def project_rest(v, l):
        rest = v.S.layers[l].tab[v.n : v.tab, :]
        into = v.S.proj if v.masked else v.S.wide
        into[v.n : v.tab, :] = dot(rest, v.W.ei[l, 128:256, :]).astype(into.dtype)

    def edge_base():
        S, w, h = R.f, I.fw.ei, R.state_one[...]
        S.wide[0:NF, :] = dot(h, w[1, 128:256, :])
        S.wide[NF : 2 * NF, :] = dot(h, w[1, 256:384, :])
        values = S.wide[0 : 2 * NF, :]
        scale = scale_for(column_peak(values))
        S.proj8[0 : 2 * NF, :] = halves(values, scale)

        def one(i, carry):
            rows = chunk(i, fine.tile)
            columns = ((S.cs[rows, :], 0, 0, NF), (S.cr[rows, :], 0, NF, NF))
            z = joined(gather_rows(columns, S.proj8), scale) + dot(S.layers[0].e[rows, :], w[1, 0:128, :])
            S.layers[1].slope[rows, :] = z
            return carry

        lax.fori_loop(0, EF // fine.tile, one, 0)

    def edge_delta(rows):
        S = R.f
        lanes = iota((16, L), 1).astype(I16)
        lanes = jnp.concatenate([lanes] * (fine.tile // 16), axis=0)
        hot = ones_where((R.block_s[rows, :] == lanes) | (R.block_r[rows, :] == lanes)).astype(F8)
        return dot(hot, S.proj8[0 : 2 * BLOCKS, :]) + gather_rows(((S.cs[rows, :], NF, 2 * BLOCKS, HALO),), S.proj8)

    def forward(v, l, edges):
        S, W, A = v.S, v.W, v.S.layers[l]
        based = l == 1 and not v.masked
        if based:
            scale = scale_for(column_peak(R.delta[...]))
            S.proj8[0 : 2 * BLOCKS + HALO, :] = halves(R.delta[...], scale)
        elif not v.masked:
            scale = scale_for(column_peak(S.wide[...]))
            S.proj8[...] = halves(S.wide[...], scale)

        def one(i, peak):
            rows = chunk(i, v.tile)
            old = edges[rows, :]
            columns = ((S.cs[rows, :], 0, 0, v.tab), (S.cr[rows, :], 0, v.tab, v.own))
            if based:
                z = A.slope[rows, :] + joined(edge_delta(rows), scale)
            elif v.masked:
                z = gather_rows(columns, S.proj) + dot(old, W.ei[l, 0:128, :])
            else:
                z = joined(gather_rows(columns, S.proj8), scale) + dot(old, W.ei[l, 0:128, :])
            gate = jax.nn.sigmoid(z)
            hidden = z * gate
            A.slope[rows, :] = gate * (1.0 + z - hidden)
            hidden = hidden.astype(BF)
            A.hid[rows, :] = hidden
            values, spread_by = normed(dot(hidden, W.eo[l]))
            A.n[rows, :] = values
            A.scale[rows, :] = jnp.broadcast_to(spread_by, values.shape)
            new = (old.astype(F32) + values).astype(BF)
            A.e[rows, :] = new
            return jnp.maximum(peak, column_peak(new.astype(F32)))

        peak = lax.fori_loop(0, v.e // v.tile, one, jnp.zeros((1, L), F32))
        if not v.masked:
            scale = scale_for(peak)

            def split(i, carry):
                rows = chunk(i, v.tile)
                S.e8[rows, :] = halves(A.e[rows, :].astype(F32), scale)
                return carry

            lax.fori_loop(0, v.e // v.tile, split, 0)

        def two(i, carry):
            rows = chunk(i, v.block)
            if v.masked:
                g = scatter_rows(S.rr, A.e, i * v.block, v.block, v.e)
            else:
                g = joined(scatter_rows(S.rr, S.e8, i * v.block, v.block, v.e), scale)
            A.g[rows, :] = g.astype(BF)
            return carry

        lax.fori_loop(0, v.n // v.block, two, 0)
        h = A.tab[0 : v.n, :]
        z = dot(h, W.ni[l, 0:128, :]) + dot(A.g[...], W.ni[l, 128:256, :])
        gate = jax.nn.sigmoid(z)
        hidden = z * gate
        A.slope2[...] = gate * (1.0 + z - hidden)
        hidden = hidden.astype(BF)
        A.hid2[...] = hidden
        values, spread_by = normed(dot(hidden, W.no[l]))
        A.n2[...] = values
        A.scale2[...] = jnp.broadcast_to(spread_by, values.shape)
        new = h.astype(F32) + values
        if v.masked:
            new = new * R.live[...]
        return new.astype(BF)

    def backward(v, l, edges, grad, edge_grad, send_rest, keep_edge, edges_done, parts_done):
        S, W, A = v.S, v.W, v.S.layers[l]
        s, acc, gw = v.first + l, v.S.acc, R.gw
        dn = grad.astype(F32)
        if v.masked:
            dn = dn * R.live[...]
        dy = normed_back(dn, A.n2[...], A.scale2[...]).astype(BF)
        dz = (dot_nt(dy, W.no[l]) * A.slope2[...]).astype(BF)
        S.ndy[...] = dy
        S.ndz[...] = dz
        dg = dot_nt(dz, W.ni[l, 128:256, :])
        if v.masked:
            S.dg[0 : v.n, :] = dg.astype(BF)
        else:
            dg_scale = scale_for(column_peak(dg))
            S.dg8[...] = halves(dg, dg_scale)
        acc[...] = dn + dot_nt(dz, W.ni[l, 0:128, :])

        def one(i, peak):
            rows = chunk(i, v.tile)
            columns = ((S.cr[rows, :], 0, 0, v.own),)
            if v.masked:
                dn = gather_rows(columns, S.dg)
            else:
                dn = joined(gather_rows(columns, S.dg8), dg_scale)
            if edge_grad is not None:
                dn = dn + edge_grad[rows, :].astype(F32)
            dy = normed_back(dn, A.n[rows, :], A.scale[rows, :]).astype(BF)
            dz = (dot_nt(dy, W.eo[l]) * A.slope[rows, :]).astype(BF)
            S.dy[rows, :] = dy
            S.dz[rows, :] = dz
            if keep_edge:
                S.de[rows, :] = dn.astype(BF)
            return jnp.maximum(peak, column_peak(dz.astype(F32)))

        peak = lax.fori_loop(0, v.e // v.tile, one, jnp.zeros((1, L), F32))

        def edge_weights():
            gw[s, 512:640, :] = dot_tn(A.tab[0 : v.n, :], S.ndz[...]).astype(BF)
            gw[s, 640:768, :] = dot_tn(A.g[...], S.ndz[...]).astype(BF)
            gw[s, 768:896, :] = dot_tn(A.hid2[...], S.ndy[...]).astype(BF)
            R.acc_b[...] = jnp.zeros((L, L), F32)
            R.acc_e[...] = jnp.zeros((L, L), F32)

            def add(i, carry):
                rows = chunk(i, v.tile)
                dz = S.dz[rows, :]
                R.acc_b[...] += dot_tn(A.hid[rows, :], S.dy[rows, :])
                R.acc_e[...] += dot_tn(edges[rows, :], dz)
                if keep_edge:
                    S.de[rows, :] = (S.de[rows, :].astype(F32) + dot_nt(dz, W.ei[l, 0:128, :])).astype(BF)
                return carry

            lax.fori_loop(0, v.e // v.tile, add, 0)
            gw[s, 256:384, :] = R.acc_e[...].astype(BF)
            gw[s, 384:512, :] = R.acc_b[...].astype(BF)

        def node_weights():
            gw[s, 0:128, :] = dot_tn(A.tab[0 : v.used, :], S.part[0 : v.used, :]).astype(BF)
            gw[s, 128:256, :] = dot_tn(A.tab[0 : v.n, :], S.other[...]).astype(BF)

        edges_done(edge_weights)
        if v.masked:

            def spread_back(rows_ref, first, count):
                return scatter_rows(rows_ref, S.dz, first, count, v.e).astype(BF)

        else:
            scale = scale_for(peak)

            def split(i, carry):
                rows = chunk(i, v.tile)
                S.e8[rows, :] = halves(S.dz[rows, :].astype(F32), scale)
                return carry

            lax.fori_loop(0, v.e // v.tile, split, 0)

            def spread_back(rows_ref, first, count):
                return joined(scatter_rows(rows_ref, S.e8, first, count, v.e), scale).astype(BF)

        rest = spread_back(S.rs, v.n, v.used - v.n)
        S.part[v.n : v.used, :] = rest
        send_rest(dot_nt(rest, W.ei[l, 128:256, :]).astype(BF))

        def two(i, carry):
            rows = chunk(i, v.block)
            S.part[rows, :] = spread_back(S.rs, i * v.block, v.block)
            S.other[rows, :] = spread_back(S.rr, i * v.block, v.block)
            return carry

        lax.fori_loop(0, v.n // v.block, two, 0)
        parts_done(node_weights)
        acc[...] += dot_nt(S.part[0 : v.n, :], W.ei[l, 128:256, :]) + dot_nt(S.other[...], W.ei[l, 256:384, :])
        return edge_weights, node_weights

    def place_column():
        return R.place[0][...]

    def place_wide():
        return jnp.broadcast_to(R.place[1][0:1, :], (WIDE, L))

    def pool_hot():
        return ones_where((iota((BLOCKS, NF), 1) >> 4) == iota((BLOCKS, NF), 0))

    def grow_hot():
        return ones_where((iota((NF, L), 0) >> 4) == iota((NF, L), 1))[:, 0:BLOCKS]

    def put_hot():
        return ones_where(iota((WIDE, L), 0) == place_wide())[:, 0:BLOCKS]

    def three_places(owner, rank):
        places = []
        for part, shift in ((0, 0), (1, 1), (2, N_COARSE - 1)):
            places.append(((owner + shift) & (N_COARSE - 1)) * PAD + part * CAP + rank)
        return places

    def put_three():
        wide = place_wide()
        down = iota((WIDE, L), 0)
        a, b, d = three_places(wide >> 4, wide & (PAD - 1))
        return ones_where((down == a) | (down == b) | (down == d))[:, 0:BLOCKS]

    def put_flags():
        row = ones_where(iota((WIDE, L), 0) == (place_wide() | (PAD - 1)))[:, 0:BLOCKS]
        lane = ones_where(iota((BLOCKS, L), 1) == (place_column() & (PAD - 1)))
        return dot(row, lane)

    def take_hot():
        return ones_where(jnp.concatenate([place_column()] * 4, axis=1) == iota((BLOCKS, WIDE), 1))

    def take_three():
        place = place_column()
        across = iota((BLOCKS, WIDE), 1)
        a, b, d = (jnp.concatenate([at] * 4, axis=1) for at in three_places(place >> 4, place & (PAD - 1)))
        return ones_where((across == a) | (across == b) | (across == d))

    def slot_of(index):
        within = index & (PAD - 1)
        return jnp.where(within < CAP, (index >> 4) * CAP + within, -1)

    def three_of(index):
        within = index & (PAD - 1)
        part = jnp.where(within >= 2 * CAP, 2, jnp.where(within >= CAP, 1, 0))
        return jnp.where(within < 3 * CAP, part * (NC - CAP) + (index >> 4) * CAP + within, -1)

    def across_hot(rows, places):
        down = iota((rows, 128), 0).astype(I16)
        parts = []
        for k in range(0, WIDE, 128):
            at = places(iota((16, 128), 1) + k).astype(I16)
            parts.append(ones_where(down == jnp.concatenate([at] * (rows // 16), axis=0)))
        return jnp.concatenate(parts, axis=1)

    def apart_hot(places, width):
        at = places(iota((WIDE, 128), 0)).astype(I16)
        lanes = iota((16, 128), 1).astype(I16)
        parts = []
        for k in range(0, width, 128):
            here = jnp.concatenate([lanes + jnp.asarray(k, I16)] * (WIDE // 16), axis=0)
            parts.append(ones_where(at == here))
        return jnp.concatenate(parts, axis=1)

    def live_rows(arrived):
        slot = iota((NC, WIDE), 0)
        first = (iota((NC, WIDE), 1) >> 4) * CAP
        last_row = (iota((NC, WIDE), 1) & (PAD - 1)) == PAD - 1
        row = dot(ones_where(last_row & (slot >= first) & (slot < first + CAP)), arrived)
        count = iota((NC, L), 0).astype(F32)
        within = iota((NC, L), 0) - jnp.floor((count + 0.5) * (1.0 / CAP)).astype(I32) * CAP
        return jnp.broadcast_to(lane_sum(jnp.where(iota((NC, L), 1) == within, row, 0.0)), (NC, L))

    def halo_pick(tab, k):
        R.hs[k][...] = gather_rows(((R.halo_col[...], 0, 0, NF),), tab).astype(BF)

    def halo_back(k):
        def send(values):
            R.hs[k][...] = values
            halo_start(R.hs[k], R.hr[k - 2], 0, R.hs_sem[k])

        return send

    def halo_add(k):
        halo_wait(R.hs[k], R.hr[k - 2], 0, R.hs_sem[k])

        def one(i, carry):
            rows = chunk(i, 512)
            R.f.acc[rows, :] += scatter_rows(R.halo_row, R.hr[k - 2], i * 512, 512, HALO)
            return carry

        lax.fori_loop(0, NF // 512, one, 0)

    def near_table():
        tab = R.c.layers[1].tab
        own = tab.at[pl.ds(0, NC), :]
        return near_copies(own, tab.at[pl.ds(NC, NC), :], own, tab.at[pl.ds(2 * NC, NC), :], R.near_sem[0])

    def near_grad():
        low, high = pl.ds(0, NC), pl.ds(NC, NC)
        return near_copies(
            R.ns.at[high, :], R.nr.at[low, :], R.ns.at[low, :], R.nr.at[high, :], R.near_sem[1]
        )

    def start(copies):
        for copy in copies:
            copy.start()

    def wait(copies):
        for copy in copies:
            copy.wait()

    later = []

    def nothing(run):
        pass

    def enter():
        greet()
        spread(I.halo, R.halo_col, R.halo_row, HALO // L)
        halo_pick(I.node, 0)
        spread(I.src, R.f.cs, R.f.rs, EF // L, R.block_s)
        spread(I.dst, R.f.cr, R.f.rr, EF // L, R.block_r, BLOCKS)
        pl.semaphore_wait(barrier, N_FINE - 1 + N_COARSE - 1)
        halo_start(R.hs[0], R.f.layers[0].tab, NF, R.hs_sem[0])

    def prepare():
        R.f.layers[0].tab[0:NF, :] = I.node[...]
        project_own(fine, 0)
        spread(I.csrc, R.c.cs, R.c.rs, EC // L)
        spread(I.cdst, R.c.cr, R.c.rr, EC // L)
        R.c.layers[1].tab[3 * NC : 512, :] = jnp.zeros((512 - 3 * NC, L), BF)
        R.parts[3 * NC : 512, :] = jnp.zeros((512 - 3 * NC, L), BF)
        R.c.proj[512 + NC : 768, :] = jnp.zeros((256 - NC, L), BF)
        R.c.dg[NC:256, :] = jnp.zeros((256 - NC, L), BF)
        owner = jnp.broadcast_to(I.owner[...], (L, BLOCKS)).T
        below = jnp.full((L - BLOCKS, L), -1, I32)
        square = jnp.concatenate([owner, below], axis=0).T
        same = (owner == square[0:BLOCKS, :]) & (iota((BLOCKS, L), 1) < iota((BLOCKS, L), 0))
        rank = lane_sum(jnp.where(same, 1.0, 0.0)).astype(I32)
        place = owner * PAD + rank
        R.place[0][...] = place
        R.place[1][...] = jnp.concatenate([place, below], axis=0).T

    def fine_zero():
        halo_wait(R.hs[0], R.f.layers[0].tab, NF, R.hs_sem[0])
        project_rest(fine, 0)
        R.state_one[...] = forward(fine, 0, I.edge)

    def sink():
        pooled = (dot(pool_hot(), R.state_one[...]) * (1.0 / POOL)).astype(BF)
        R.ws[0][...] = (dot(put_three(), pooled) + put_flags()).astype(BF)
        wide_start(0)
        edge_base()
        wide_wait(0)
        arrived = R.wr[0][...]
        R.c.layers[0].tab[...] = dot(across_hot(512, three_of), arrived).astype(BF)
        R.live[...] = live_rows(arrived)

    def coarse_layer(l):
        def run():
            if l == 1:
                start(near_table())
            project_own(coarse, l)
            if l == 1:
                wait(near_table())
            project_rest(coarse, l)
            new = forward(coarse, l, I.cedge if l == 0 else R.c.layers[0].e)
            if l == 0:
                R.c.layers[1].tab[0:NC, :] = new
            else:
                R.ws[1][...] = dot(apart_hot(slot_of, 256)[:, 0:NC], new).astype(BF)
                wide_start(1)

        return run

    def rise():
        wide_wait(1)
        picked = dot(take_hot(), R.wr[1][...]).astype(BF)
        R.f.layers[1].tab[0:NF, :] = (R.state_one[...].astype(F32) + dot(grow_hot(), picked)).astype(BF)
        halo_pick(R.f.layers[1].tab, 1)
        halo_start(R.hs[1], R.f.layers[1].tab, NF, R.hs_sem[1])
        w = I.fw.ei
        R.delta[0:BLOCKS, :] = dot(picked, w[1, 128:256, :])
        R.delta[BLOCKS : 2 * BLOCKS, :] = dot(picked, w[1, 256:384, :])
        halo_wait(R.hs[1], R.f.layers[1].tab, NF, R.hs_sem[1])
        R.delta[2 * BLOCKS :, :] = dot(R.f.layers[1].tab[NF : NF + HALO, :], w[1, 128:256, :])

    def fine_one():
        O.new_state[...] = forward(fine, 1, R.f.layers[0].e)

    def fine_one_back():
        later[:] = backward(
            fine, 1, R.f.layers[0].e, I.cot[...], None, halo_back(2), True, nothing, nothing
        )

    def sink_back():
        halo_add(2)
        grad_two = R.f.acc[...].astype(BF)
        R.grad_two[...] = grad_two
        R.ws[2][...] = dot(put_hot(), dot(pool_hot(), grad_two).astype(BF)).astype(BF)
        wide_start(2)
        for run in later:
            run()
        total[1].one()
        wide_wait(2)
        R.grad_c[...] = dot(across_hot(NC, slot_of), R.wr[2][...]).astype(BF)

    def coarse_back(l):
        def run():
            def send(values):
                if l == 1:
                    R.ns[...] = values
                    start(near_grad())
                else:
                    R.parts[NC : 3 * NC, :] = values

            edges, edge_grad = (I.cedge, R.c.de) if l == 0 else (R.c.layers[0].e, None)
            weights = backward(
                coarse, l, edges, R.grad_c[...], edge_grad, send, l == 1, nothing, nothing
            )
            if l == 1:
                for run in weights:
                    run()
                total[3].one()
                wait(near_grad())
                total[1].two()
                grad = R.c.acc[...] + R.nr[0:NC, :].astype(F32) + R.nr[NC : 2 * NC, :].astype(F32)
                R.grad_c[...] = grad.astype(BF)
            else:
                R.parts[0:NC, :] = R.c.acc[...].astype(BF)
                R.ws[3][...] = dot(apart_hot(three_of, 512), R.parts[...]).astype(BF)
                wide_start(3)
                for run in weights:
                    run()

        return run

    def rise_back():
        total[2].one()
        total[1].three()
        total[3].two()
        wide_wait(3)
        sunk = (dot(take_three(), R.wr[3][...]).astype(BF).astype(F32) * (1.0 / POOL)).astype(BF)
        R.grad_one[...] = (R.grad_two[...].astype(F32) + dot(grow_hot(), sunk)).astype(BF)

    def fine_zero_back():
        def edges_done(edge_weights):
            edge_weights()
            total[0].one()
            total[2].two()
            total[3].three()

        def parts_done(node_weights):
            node_weights()
            R.late[...] = R.gw[0, 0:LATE, :].astype(F32)
            late.one()

        backward(fine, 0, I.edge, R.grad_one[...], R.f.de, halo_back(3), False, edges_done, parts_done)

    def leave():
        total[0].two()
        total[2].three()
        halo_add(3)
        O.state_grad[...] = R.f.acc[...].astype(BF)
        late.two()
        total[0].three()
        total[1].end()
        late.three()
        total[3].end()
        total[2].end()
        total[0].end()
        late.four()
        O.sums[0, 0:LATE, :] = R.late_sum[...]

    steps = (
        enter, prepare, fine_zero, sink, coarse_layer(0), coarse_layer(1), rise, fine_one, fine_one_back, sink_back,
        coarse_back(1), coarse_back(0), rise_back, fine_zero_back, leave,
    )
    for step in steps[:STEPS]:
        step()


def spread_out(state, grad, sums, *refs):
    outs, sem = refs[:-1], refs[-1]
    pairs = [(state, outs[0]), (grad, outs[1])]
    for s in range(4):
        ei, eo, ni, no = outs[2 + 4 * (s // 2) : 6 + 4 * (s // 2)]
        l = s % 2
        for out, there, here, rows in (
            (ei, 0, 256, 128), (ei, 128, 0, 256), (eo, 0, 384, 128), (ni, 0, 512, 256), (no, 0, 768, 128)
        ):
            pairs.append((sums.at[s, pl.ds(here, rows), :], out.at[l, pl.ds(there, rows), :]))
    copies = [pltpu.make_async_copy(src, dst, sem.at[k]) for k, (src, dst) in enumerate(pairs)]
    for copy in copies:
        copy.start()
    for copy in copies:
        copy.wait()


def body(*arrays):
    arrays = list(arrays)
    for i, rows in ((3, EF // L), (4, EF // L), (7, EC // L), (8, EC // L)):
        arrays[i] = arrays[i].reshape(rows, L)
    arrays[6] = arrays[6].reshape(1, BLOCKS)
    states = [jax.ShapeDtypeStruct((NF, L), BF)] * 2
    vm_spec = pl.BlockSpec(memory_space=pltpu.VMEM)
    any_spec = pl.BlockSpec(memory_space=pl.ANY)
    results = pl.pallas_call(
        kernel,
        out_shape=tuple(states + [jax.ShapeDtypeStruct((4, SET, L), F32)]),
        in_specs=[vm_spec] * len(arrays),
        out_specs=(vm_spec,) * 3,
        scratch_shapes=flat(shapes()),
        compiler_params=pltpu.CompilerParams(
            collective_id=0, has_side_effects=True, vmem_limit_bytes=60 * 2**20
        ),
        cost_estimate=pl.CostEstimate(flops=40 * 10**9, bytes_accessed=8 * 2**20, transcendentals=4 * 10**6),
    )(*arrays)
    outs = list(states)
    for _ in range(2):
        outs += [jax.ShapeDtypeStruct((2, rows, L), F32) for rows in (384, 128, 256, 128)]
    return pl.pallas_call(
        spread_out,
        out_shape=tuple(outs),
        in_specs=[vm_spec] * 3,
        out_specs=(any_spec,) * len(outs),
        scratch_shapes=[pltpu.SemaphoreType.DMA((22,))],
    )(*results)


def solution(mesh):
    rows = P(("fine", "coarse"), None)
    flat = P(("fine", "coarse"))
    placed = (rows, rows, rows, flat, flat, rows, rows, flat, flat, rows) + (P(),) * 8
    return jax.shard_map(
        body, mesh=mesh, in_specs=placed, out_specs=(rows, rows) + (P(),) * 8, check_vma=False
    )
```

```python
from types import SimpleNamespace

import jax
import jax.numpy as jnp
from jax import lax
from jax.experimental import pallas as pl
from jax.experimental.pallas import tpu as pltpu
from jax.sharding import PartitionSpec as P

BF = jnp.bfloat16
F32 = jnp.float32
I16 = jnp.int16
I32 = jnp.int32
F8 = jnp.float8_e4m3fn
MESH = pl.DeviceIdType.MESH

L = 128
NF, EF, HALO = 1024, 4096, 512
NC, EC = 160, 640
BLOCKS, POOL, CAP = 64, 16, 5
PAD = 16
N_FINE, N_COARSE = 4, 32
WIDE = N_COARSE * PAD
SET = 896
LATE = 256
OWNED = 32
EPS = 1e-05


def dot(a, b):
    return jnp.dot(a, b, preferred_element_type=F32)


def dot_nt(a, b):
    return lax.dot_general(a, b, (((1,), (1,)), ((), ())), preferred_element_type=F32)


def dot_tn(a, b):
    return lax.dot_general(a, b, (((0,), (0,)), ((), ())), preferred_element_type=F32)


def iota(shape, dim):
    return lax.broadcasted_iota(I32, shape, dim)


def ones_where(mask):
    return jnp.where(mask, jnp.asarray(1, BF), jnp.asarray(0, BF))


def lane_sum(x):
    return jnp.sum(x, axis=-1, keepdims=True)


def normed(y):
    center = y - lane_sum(y) * (1.0 / L)
    scale = lax.rsqrt(lane_sum(center * center) * (1.0 / L) + EPS)
    return center * scale, scale


def normed_back(dn, n, scale):
    return scale * (dn - lane_sum(dn) * (1.0 / L) - n * (lane_sum(dn * n) * (1.0 / L)))


def hot_columns(column, base, width, dtype):
    count = column.shape[0]
    lanes = iota((16, 128), 1).astype(I16)
    parts = []
    for start in range(0, width, 128):
        places = jnp.concatenate([lanes + jnp.asarray(base + start, I16)] * (count // 16), axis=0)
        parts.append(ones_where(column == places))
    hot = jnp.concatenate(parts, axis=1) if len(parts) > 1 else parts[0]
    return hot.astype(dtype)


def gather_rows(columns, table):
    total = None
    for column, first, base, width in columns:
        for k in range(0, width, 256):
            size = min(256, width - k)
            part = dot(hot_columns(column, first + k, size, table.dtype), table[base + k : base + k + size, :])
            total = part if total is None else total + part
    return total


def scatter_rows(rows_ref, data_ref, first, count, edges):
    down = iota((count, 128), 0).astype(I16)
    shift = jnp.asarray(first, I32).astype(I16)
    total = None
    for k in range(0, edges, 256):
        size = min(256, edges - k)
        parts = []
        for j in range(k // 128, (k + size) // 128):
            row = rows_ref[j] - shift
            parts.append(ones_where(down == jnp.concatenate([row] * (count // 16), axis=0)))
        hot = jnp.concatenate(parts, axis=1) if len(parts) > 1 else parts[0]
        part = dot(hot.astype(data_ref.dtype), data_ref[k : k + size, :])
        total = part if total is None else total + part
    return total


def column_peak(x):
    return jnp.max(jnp.abs(x), axis=0, keepdims=True)


def scale_for(peak):
    return jnp.exp2(7.0 - jnp.floor(jnp.log2(jnp.maximum(peak, 1e-30))))


def halves(x, scale):
    x = x * scale
    high = x.astype(F8)
    low = ((x - high.astype(F32)) * 16.0).astype(F8)
    return jnp.concatenate([high, low], axis=1)


def joined(pair, scale):
    return (pair[:, 0:L] + pair[:, L : 2 * L] * 0.0625) * (1.0 / scale)


def vm(*shape, dtype=F32):
    return pltpu.VMEM(shape, dtype)


def level_shapes(n, tab, own, e):
    def layer():
        return SimpleNamespace(
            tab=vm(tab, L, dtype=BF),
            slope=vm(e, L),
            hid=vm(e, L, dtype=BF),
            n=vm(e, L),
            scale=vm(e, L),
            e=vm(e, L, dtype=BF),
            g=vm(n, L, dtype=BF),
            slope2=vm(n, L),
            hid2=vm(n, L, dtype=BF),
            n2=vm(n, L),
            scale2=vm(n, L),
        )

    return SimpleNamespace(
        cs=vm(e, L, dtype=I16),
        cr=vm(e, L, dtype=I16),
        rs=vm(e // L, 16, L, dtype=I16),
        rr=vm(e // L, 16, L, dtype=I16),
        proj=vm(tab + own, L, dtype=BF),
        wide=vm(2 * n, L),
        proj8=vm(tab + own, 2 * L, dtype=F8),
        dz=vm(e, L, dtype=BF),
        e8=vm(e, 2 * L, dtype=F8),
        dg8=vm(own, 2 * L, dtype=F8),
        de=vm(e, L, dtype=BF),
        dg=vm(own, L, dtype=BF),
        dy=vm(e, L, dtype=BF),
        ndy=vm(n, L, dtype=BF),
        ndz=vm(n, L, dtype=BF),
        part=vm(tab, L, dtype=BF),
        other=vm(n, L, dtype=BF),
        acc=vm(n, L),
        layers=[layer(), layer()],
    )


def shapes():
    dma = pltpu.SemaphoreType.DMA
    return SimpleNamespace(
        f=level_shapes(NF, NF + HALO, NF, EF),
        c=level_shapes(NC, 512, 256, EC),
        state_one=vm(NF, L, dtype=BF),
        live=vm(NC, L),
        acc_b=vm(L, L),
        acc_e=vm(L, L),
        block_s=vm(EF, L, dtype=I16),
        block_r=vm(EF, L, dtype=I16),
        delta=vm(2 * BLOCKS + HALO, L),
        halo_col=vm(HALO, L, dtype=I16),
        halo_row=vm(HALO // L, 16, L, dtype=I16),
        grad_two=vm(NF, L, dtype=BF),
        grad_one=vm(NF, L, dtype=BF),
        grad_c=vm(NC, L, dtype=BF),
        place=[vm(BLOCKS, L, dtype=I32), vm(L, L, dtype=I32)],
        hs=[vm(HALO, L, dtype=BF) for _ in range(4)],
        hr=[vm(HALO, L, dtype=BF) for _ in range(2)],
        ws=[vm(WIDE, L, dtype=BF) for _ in range(4)],
        wr=[vm(WIDE, L, dtype=BF) for _ in range(4)],
        ns=vm(2 * NC, L, dtype=BF),
        nr=vm(2 * NC, L, dtype=BF),
        parts=vm(512, L, dtype=BF),
        gw=vm(4, SET, L, dtype=BF),
        late=vm(LATE, L),
        late_got=vm(LATE, L),
        late_quad=vm(N_FINE, 8, L),
        late_sum=vm(LATE, L),
        got=vm(4, N_COARSE * OWNED, L, dtype=BF),
        quad=vm(4, N_FINE, OWNED, L),
        sums=vm(4, N_COARSE * OWNED, L),
        one_sem=dma((5, 2)),
        two_sem=dma((5, 2, 3)),
        three_sem=dma((5, 2)),
        hs_sem=[dma((2, 3)) for _ in range(4)],
        ws_sem=[dma((2,)) for _ in range(4)],
        near_sem=[dma((2, 2)) for _ in range(2)],
    )


def flat(tree):
    if isinstance(tree, SimpleNamespace):
        return [leaf for part in vars(tree).values() for leaf in flat(part)]
    if isinstance(tree, list):
        return [leaf for part in tree for leaf in flat(part)]
    return [tree]


def rebuilt(tree, leaves):
    if isinstance(tree, SimpleNamespace):
        return SimpleNamespace(**{name: rebuilt(part, leaves) for name, part in vars(tree).items()})
    if isinstance(tree, list):
        return [rebuilt(part, leaves) for part in tree]
    return next(leaves)


def operands():
    def weights():
        return SimpleNamespace(ei=None, eo=None, ni=None, no=None)

    inputs = SimpleNamespace(
        node=None, edge=None, cedge=None, src=None, dst=None, halo=None, owner=None, csrc=None, cdst=None, cot=None,
        fw=weights(), cw=weights(),
    )
    outputs = SimpleNamespace(new_state=None, state_grad=None, sums=None)
    return inputs, outputs


STEPS = None


def kernel(*args):
    leaves = iter(args)
    I, O = (rebuilt(tree, leaves) for tree in operands())
    R = rebuilt(shapes(), leaves)
    f = lax.axis_index("fine")
    c = lax.axis_index("coarse")

    def fine_at(d):
        return lax.rem(f + d + N_FINE, N_FINE)

    def coarse_at(d):
        return lax.rem(c + d + N_COARSE, N_COARSE)

    def chunk(i, size, align=None):
        return pl.ds(pl.multiple_of(i * size, align or size), size)

    def remote(src, dst, send, recv, where):
        return pltpu.make_async_remote_copy(
            src_ref=src, dst_ref=dst, send_sem=send, recv_sem=recv, device_id=where, device_id_type=MESH
        )

    def wait_for(view, sem):
        pltpu.make_async_copy(view, view, sem).wait()

    barrier = pltpu.get_barrier_semaphore()

    def greet():
        for d in range(1, N_FINE):
            pl.semaphore_signal(barrier, inc=1, device_id=(fine_at(d), c), device_id_type=MESH)

        def one(d, carry):
            pl.semaphore_signal(barrier, inc=1, device_id=(f, coarse_at(d)), device_id_type=MESH)
            return carry

        lax.fori_loop(1, N_COARSE, one, 0)

    def spread(src, columns, rows, count, blocks=None, shift=0):
        def one(j, carry):
            wide = jnp.broadcast_to(src[pl.ds(j, 1), :], (L, L))
            rows[j] = wide[:16, :].astype(I16)
            tall = wide.T
            columns[chunk(j, L), :] = tall.astype(I16)
            if blocks is not None:
                blocks[chunk(j, L), :] = jnp.where(tall < NF, (tall >> 4) + shift, -1).astype(I16)
            return carry

        lax.fori_loop(0, count, one, 0, unroll=next(u for u in (8, 5, 4) if count % u == 0))

    def halo_copies(src, dst, base, sem):
        out, back = [], []
        for d in range(1, N_FINE):
            q, at = fine_at(d), fine_at(-d)
            out.append(
                remote(
                    src.at[chunk(q, L), :],
                    dst.at[pl.ds(pl.multiple_of(base + f * L, L), L), :],
                    sem.at[0, d - 1],
                    sem.at[1, d - 1],
                    (q, c),
                )
            )
            back.append((dst.at[pl.ds(pl.multiple_of(base + at * L, L), L), :], sem.at[1, d - 1]))
        return out, back

    def halo_start(src, dst, base, sem):
        for copy in halo_copies(src, dst, base, sem)[0]:
            copy.start()
        dst[pl.ds(pl.multiple_of(base + f * L, L), L), :] = src[chunk(f, L), :]

    def halo_wait(src, dst, base, sem):
        out, back = halo_copies(src, dst, base, sem)
        for copy in out:
            copy.wait_send()
        for view, at in back:
            wait_for(view, at)

    def wide_start(k):
        src, dst, sem = R.ws[k], R.wr[k], R.ws_sem[k]

        def one(d, carry):
            o = coarse_at(d)
            remote(src.at[chunk(o, PAD), :], dst.at[chunk(c, PAD), :], sem.at[0], sem.at[1], (f, o)).start()
            return carry

        lax.fori_loop(N_COARSE // 2, N_COARSE, one, 0)
        lax.fori_loop(1, N_COARSE // 2, one, 0)
        dst[chunk(c, PAD), :] = src[chunk(c, PAD), :]

    def wide_wait(k):
        dst, sem = R.wr[k], R.ws_sem[k]
        wait_for(dst.at[pl.ds(0, WIDE - PAD), :], sem.at[0])
        wait_for(dst.at[pl.ds(0, WIDE - PAD), :], sem.at[1])

    def near_copies(up_src, up_dst, down_src, down_dst, sem):
        return (
            remote(up_src, up_dst, sem.at[0, 0], sem.at[1, 0], (f, coarse_at(1))),
            remote(down_src, down_dst, sem.at[0, 1], sem.at[1, 1], (f, coarse_at(-1))),
        )

    def summing(k, owners, block, src, got, quad, dst):
        sem, group_sem, last_sem = R.one_sem.at[k], R.two_sem.at[k], R.three_sem.at[k]
        mine = chunk(c, block)

        def owner(run):
            run() if owners == N_COARSE else pl.when(c < owners)(run)

        def other(run):
            if owners < N_COARSE:
                pl.when(c >= owners)(run)

        def group():
            return [
                remote(quad.at[f], quad.at[f], group_sem.at[0, d - 1], group_sem.at[1, d - 1], (fine_at(d), c))
                for d in range(1, N_FINE)
            ]

        def one():
            def send(d, carry):
                o = coarse_at(d)

                def go():
                    remote(src.at[chunk(o, block), :], got.at[mine, :], sem.at[0], sem.at[1], (f, o)).start()

                go() if owners == N_COARSE else pl.when(o < owners)(go)
                return carry

            lax.fori_loop(N_COARSE // 2, N_COARSE, send, 0)
            lax.fori_loop(1, N_COARSE // 2, send, 0)

        def two():
            def run():
                got[mine, :] = src[mine, :]
                wait_for(got.at[pl.ds(0, (owners - 1) * block), :], sem.at[0])
                wait_for(got.at[pl.ds(0, (N_COARSE - 1) * block), :], sem.at[1])
                parts = [got[j * block : (j + 1) * block, :].astype(F32) for j in range(N_COARSE)]
                while len(parts) > 1:
                    parts = [parts[j] + parts[j + 1] for j in range(0, len(parts), 2)]
                quad[f] = parts[0]
                for copy in group():
                    copy.start()

            owner(run)
            other(lambda: wait_for(got.at[pl.ds(0, owners * block), :], sem.at[0]))

        def three():
            def run():
                for copy in group():
                    copy.wait()
                dst[mine, :] = (quad[0] + quad[1]) + (quad[2] + quad[3])

                def send(d, carry):
                    o = coarse_at(d)
                    remote(dst.at[mine, :], dst.at[mine, :], last_sem.at[0], last_sem.at[1], (f, o)).start()
                    return carry

                lax.fori_loop(N_COARSE // 2, N_COARSE, send, 0)
                lax.fori_loop(1, N_COARSE // 2, send, 0)

            owner(run)

        def four():
            def run():
                wait_for(dst.at[pl.ds(0, (N_COARSE - 1) * block), :], last_sem.at[0])
                wait_for(dst.at[pl.ds(0, (owners - 1) * block), :], last_sem.at[1])

            owner(run)
            other(lambda: wait_for(dst.at[pl.ds(0, owners * block), :], last_sem.at[1]))

        return SimpleNamespace(one=one, two=two, three=three, four=four)

    def summing_set(s):
        first = LATE if s == 0 else 0
        count = SET - first
        work = summing(
            s, count // OWNED, OWNED, R.gw.at[s, pl.ds(first, count), :], R.got.at[s], R.quad.at[s], R.sums.at[s]
        )

        def end():
            work.four()
            O.sums[s, first:SET, :] = R.sums[s, 0:count, :]

        work.end = end
        return work

    total = [summing_set(s) for s in range(4)]
    late = summing(4, N_COARSE, 8, R.late, R.late_got, R.late_quad, R.late_sum)

    fine = SimpleNamespace(
        n=NF, used=NF + HALO, tab=NF + HALO, own=NF, e=EF, tile=1024, block=512, S=R.f, W=I.fw, first=0, masked=False
    )
    coarse = SimpleNamespace(
        n=NC, used=3 * NC, tab=512, own=256, e=EC, tile=EC, block=NC, S=R.c, W=I.cw, first=2, masked=True
    )

    def project_own(v, l):
        w, h = v.W.ei, v.S.layers[l].tab[0 : v.n, :]
        v.S.proj[0 : v.n, :] = dot(h, w[l, 128:256, :]).astype(BF)
        v.S.proj[v.tab : v.tab + v.n, :] = dot(h, w[l, 256:384, :]).astype(BF)

    def project_rest(v, l):
        rest = v.S.layers[l].tab[v.n : v.tab, :]
        v.S.proj[v.n : v.tab, :] = dot(rest, v.W.ei[l, 128:256, :]).astype(BF)

    def edge_base(l, h, edges):
        S, w = R.f, I.fw.ei
        S.wide[0:NF, :] = dot(h, w[l, 128:256, :])
        S.wide[NF : 2 * NF, :] = dot(h, w[l, 256:384, :])
        values = S.wide[0 : 2 * NF, :]
        scale = scale_for(column_peak(values))
        S.proj8[0 : 2 * NF, :] = halves(values, scale)

        def one(i, carry):
            rows = chunk(i, fine.tile)
            columns = ((S.cs[rows, :], 0, 0, NF), (S.cr[rows, :], 0, NF, NF))
            z = joined(gather_rows(columns, S.proj8), scale) + dot(edges[rows, :], w[l, 0:128, :])
            S.layers[l].slope[rows, :] = z
            return carry

        lax.fori_loop(0, EF // fine.tile, one, 0)

    def edge_delta(l, rows):
        S = R.f
        received = gather_rows(((S.cs[rows, :], NF, 2 * BLOCKS, HALO),), S.proj8)
        if l == 0:
            return received
        lanes = iota((16, L), 1).astype(I16)
        lanes = jnp.concatenate([lanes] * (fine.tile // 16), axis=0)
        hot = ones_where((R.block_s[rows, :] == lanes) | (R.block_r[rows, :] == lanes)).astype(F8)
        return dot(hot, S.proj8[0 : 2 * BLOCKS, :]) + received

    def forward(v, l, edges):
        S, W, A = v.S, v.W, v.S.layers[l]
        if not v.masked:
            scale = scale_for(column_peak(R.delta[...]))
            S.proj8[0 : 2 * BLOCKS + HALO, :] = halves(R.delta[...], scale)

        def one(i, peak):
            rows = chunk(i, v.tile)
            old = edges[rows, :]
            if v.masked:
                columns = ((S.cs[rows, :], 0, 0, v.tab), (S.cr[rows, :], 0, v.tab, v.own))
                z = gather_rows(columns, S.proj) + dot(old, W.ei[l, 0:128, :])
            else:
                z = A.slope[rows, :] + joined(edge_delta(l, rows), scale)
            gate = jax.nn.sigmoid(z)
            hidden = z * gate
            A.slope[rows, :] = gate * (1.0 + z - hidden)
            hidden = hidden.astype(BF)
            A.hid[rows, :] = hidden
            values, spread_by = normed(dot(hidden, W.eo[l]))
            A.n[rows, :] = values
            A.scale[rows, :] = jnp.broadcast_to(spread_by, values.shape)
            new = (old.astype(F32) + values).astype(BF)
            A.e[rows, :] = new
            return jnp.maximum(peak, column_peak(new.astype(F32)))

        peak = lax.fori_loop(0, v.e // v.tile, one, jnp.zeros((1, L), F32))
        if not v.masked:
            scale = scale_for(peak)

            def split(i, carry):
                rows = chunk(i, v.tile)
                S.e8[rows, :] = halves(A.e[rows, :].astype(F32), scale)
                return carry

            lax.fori_loop(0, v.e // v.tile, split, 0)

        def two(i, carry):
            rows = chunk(i, v.block)
            if v.masked:
                g = scatter_rows(S.rr, A.e, i * v.block, v.block, v.e)
            else:
                g = joined(scatter_rows(S.rr, S.e8, i * v.block, v.block, v.e), scale)
            A.g[rows, :] = g.astype(BF)
            return carry

        lax.fori_loop(0, v.n // v.block, two, 0)
        h = A.tab[0 : v.n, :]
        z = dot(h, W.ni[l, 0:128, :]) + dot(A.g[...], W.ni[l, 128:256, :])
        gate = jax.nn.sigmoid(z)
        hidden = z * gate
        A.slope2[...] = gate * (1.0 + z - hidden)
        hidden = hidden.astype(BF)
        A.hid2[...] = hidden
        values, spread_by = normed(dot(hidden, W.no[l]))
        A.n2[...] = values
        A.scale2[...] = jnp.broadcast_to(spread_by, values.shape)
        new = h.astype(F32) + values
        if v.masked:
            new = new * R.live[...]
        return new.astype(BF)

    def backward(v, l, edges, grad, edge_grad, send_rest, keep_edge, edges_done, parts_done):
        S, W, A = v.S, v.W, v.S.layers[l]
        s, acc, gw = v.first + l, v.S.acc, R.gw
        dn = grad.astype(F32)
        if v.masked:
            dn = dn * R.live[...]
        dy = normed_back(dn, A.n2[...], A.scale2[...]).astype(BF)
        dz = (dot_nt(dy, W.no[l]) * A.slope2[...]).astype(BF)
        S.ndy[...] = dy
        S.ndz[...] = dz
        dg = dot_nt(dz, W.ni[l, 128:256, :])
        if v.masked:
            S.dg[0 : v.n, :] = dg.astype(BF)
        else:
            dg_scale = scale_for(column_peak(dg))
            S.dg8[...] = halves(dg, dg_scale)
        acc[...] = dn + dot_nt(dz, W.ni[l, 0:128, :])

        def one(i, peak):
            rows = chunk(i, v.tile)
            columns = ((S.cr[rows, :], 0, 0, v.own),)
            if v.masked:
                dn = gather_rows(columns, S.dg)
            else:
                dn = joined(gather_rows(columns, S.dg8), dg_scale)
            if edge_grad is not None:
                dn = dn + edge_grad[rows, :].astype(F32)
            dy = normed_back(dn, A.n[rows, :], A.scale[rows, :]).astype(BF)
            dz = (dot_nt(dy, W.eo[l]) * A.slope[rows, :]).astype(BF)
            S.dy[rows, :] = dy
            S.dz[rows, :] = dz
            if keep_edge:
                S.de[rows, :] = dn.astype(BF)
            return jnp.maximum(peak, column_peak(dz.astype(F32)))

        peak = lax.fori_loop(0, v.e // v.tile, one, jnp.zeros((1, L), F32))

        def edge_weights():
            gw[s, 512:640, :] = dot_tn(A.tab[0 : v.n, :], S.ndz[...]).astype(BF)
            gw[s, 640:768, :] = dot_tn(A.g[...], S.ndz[...]).astype(BF)
            gw[s, 768:896, :] = dot_tn(A.hid2[...], S.ndy[...]).astype(BF)
            R.acc_b[...] = jnp.zeros((L, L), F32)
            R.acc_e[...] = jnp.zeros((L, L), F32)

            def add(i, carry):
                rows = chunk(i, v.tile)
                dz = S.dz[rows, :]
                R.acc_b[...] += dot_tn(A.hid[rows, :], S.dy[rows, :])
                R.acc_e[...] += dot_tn(edges[rows, :], dz)
                if keep_edge:
                    S.de[rows, :] = (S.de[rows, :].astype(F32) + dot_nt(dz, W.ei[l, 0:128, :])).astype(BF)
                return carry

            lax.fori_loop(0, v.e // v.tile, add, 0)
            gw[s, 256:384, :] = R.acc_e[...].astype(BF)
            gw[s, 384:512, :] = R.acc_b[...].astype(BF)

        def node_weights():
            gw[s, 0:128, :] = dot_tn(A.tab[0 : v.used, :], S.part[0 : v.used, :]).astype(BF)
            gw[s, 128:256, :] = dot_tn(A.tab[0 : v.n, :], S.other[...]).astype(BF)

        edges_done(edge_weights)
        if v.masked:

            def spread_back(rows_ref, first, count):
                return scatter_rows(rows_ref, S.dz, first, count, v.e).astype(BF)

        else:
            scale = scale_for(peak)

            def split(i, carry):
                rows = chunk(i, v.tile)
                S.e8[rows, :] = halves(S.dz[rows, :].astype(F32), scale)
                return carry

            lax.fori_loop(0, v.e // v.tile, split, 0)

            def spread_back(rows_ref, first, count):
                return joined(scatter_rows(rows_ref, S.e8, first, count, v.e), scale).astype(BF)

        rest = spread_back(S.rs, v.n, v.used - v.n)
        S.part[v.n : v.used, :] = rest
        send_rest(dot_nt(rest, W.ei[l, 128:256, :]).astype(BF))

        def two(i, carry):
            rows = chunk(i, v.block)
            S.part[rows, :] = spread_back(S.rs, i * v.block, v.block)
            S.other[rows, :] = spread_back(S.rr, i * v.block, v.block)
            return carry

        lax.fori_loop(0, v.n // v.block, two, 0)
        parts_done(node_weights)
        acc[...] += dot_nt(S.part[0 : v.n, :], W.ei[l, 128:256, :]) + dot_nt(S.other[...], W.ei[l, 256:384, :])
        return edge_weights, node_weights

    def place_column():
        return R.place[0][...]

    def place_wide():
        return jnp.broadcast_to(R.place[1][0:1, :], (WIDE, L))

    def pool_hot():
        return ones_where((iota((BLOCKS, NF), 1) >> 4) == iota((BLOCKS, NF), 0))

    def grow_hot():
        return ones_where((iota((NF, L), 0) >> 4) == iota((NF, L), 1))[:, 0:BLOCKS]

    def put_hot():
        return ones_where(iota((WIDE, L), 0) == place_wide())[:, 0:BLOCKS]

    def three_places(owner, rank):
        places = []
        for part, shift in ((0, 0), (1, 1), (2, N_COARSE - 1)):
            places.append(((owner + shift) & (N_COARSE - 1)) * PAD + part * CAP + rank)
        return places

    def put_three():
        wide = place_wide()
        down = iota((WIDE, L), 0)
        a, b, d = three_places(wide >> 4, wide & (PAD - 1))
        return ones_where((down == a) | (down == b) | (down == d))[:, 0:BLOCKS]

    def put_flags():
        row = ones_where(iota((WIDE, L), 0) == (place_wide() | (PAD - 1)))[:, 0:BLOCKS]
        lane = ones_where(iota((BLOCKS, L), 1) == (place_column() & (PAD - 1)))
        return dot(row, lane)

    def take_hot():
        return ones_where(jnp.concatenate([place_column()] * 4, axis=1) == iota((BLOCKS, WIDE), 1))

    def take_three():
        place = place_column()
        across = iota((BLOCKS, WIDE), 1)
        a, b, d = (jnp.concatenate([at] * 4, axis=1) for at in three_places(place >> 4, place & (PAD - 1)))
        return ones_where((across == a) | (across == b) | (across == d))

    def slot_of(index):
        within = index & (PAD - 1)
        return jnp.where(within < CAP, (index >> 4) * CAP + within, -1)

    def three_of(index):
        within = index & (PAD - 1)
        part = jnp.where(within >= 2 * CAP, 2, jnp.where(within >= CAP, 1, 0))
        return jnp.where(within < 3 * CAP, part * (NC - CAP) + (index >> 4) * CAP + within, -1)

    def across_hot(rows, places):
        down = iota((rows, 128), 0).astype(I16)
        parts = []
        for k in range(0, WIDE, 128):
            at = places(iota((16, 128), 1) + k).astype(I16)
            parts.append(ones_where(down == jnp.concatenate([at] * (rows // 16), axis=0)))
        return jnp.concatenate(parts, axis=1)

    def apart_hot(places, width):
        at = places(iota((WIDE, 128), 0)).astype(I16)
        lanes = iota((16, 128), 1).astype(I16)
        parts = []
        for k in range(0, width, 128):
            here = jnp.concatenate([lanes + jnp.asarray(k, I16)] * (WIDE // 16), axis=0)
            parts.append(ones_where(at == here))
        return jnp.concatenate(parts, axis=1)

    def live_rows(arrived):
        slot = iota((NC, WIDE), 0)
        first = (iota((NC, WIDE), 1) >> 4) * CAP
        last_row = (iota((NC, WIDE), 1) & (PAD - 1)) == PAD - 1
        row = dot(ones_where(last_row & (slot >= first) & (slot < first + CAP)), arrived)
        count = iota((NC, L), 0).astype(F32)
        within = iota((NC, L), 0) - jnp.floor((count + 0.5) * (1.0 / CAP)).astype(I32) * CAP
        return jnp.broadcast_to(lane_sum(jnp.where(iota((NC, L), 1) == within, row, 0.0)), (NC, L))

    def halo_pick(tab, k):
        R.hs[k][...] = gather_rows(((R.halo_col[...], 0, 0, NF),), tab).astype(BF)

    def halo_back(k):
        def send(values):
            R.hs[k][...] = values
            halo_start(R.hs[k], R.hr[k - 2], 0, R.hs_sem[k])

        return send

    def halo_add(k):
        halo_wait(R.hs[k], R.hr[k - 2], 0, R.hs_sem[k])

        def one(i, carry):
            rows = chunk(i, 512)
            R.f.acc[rows, :] += scatter_rows(R.halo_row, R.hr[k - 2], i * 512, 512, HALO)
            return carry

        lax.fori_loop(0, NF // 512, one, 0)

    def near_table():
        tab = R.c.layers[1].tab
        own = tab.at[pl.ds(0, NC), :]
        return near_copies(own, tab.at[pl.ds(NC, NC), :], own, tab.at[pl.ds(2 * NC, NC), :], R.near_sem[0])

    def near_grad():
        low, high = pl.ds(0, NC), pl.ds(NC, NC)
        return near_copies(
            R.ns.at[high, :], R.nr.at[low, :], R.ns.at[low, :], R.nr.at[high, :], R.near_sem[1]
        )

    def start(copies):
        for copy in copies:
            copy.start()

    def wait(copies):
        for copy in copies:
            copy.wait()

    later = []

    def nothing(run):
        pass

    def enter():
        greet()
        spread(I.halo, R.halo_col, R.halo_row, HALO // L)
        halo_pick(I.node, 0)
        spread(I.src, R.f.cs, R.f.rs, EF // L, R.block_s)
        spread(I.dst, R.f.cr, R.f.rr, EF // L, R.block_r, BLOCKS)
        edge_base(0, I.node[...], I.edge)
        pl.semaphore_wait(barrier, N_FINE - 1 + N_COARSE - 1)
        halo_start(R.hs[0], R.f.layers[0].tab, NF, R.hs_sem[0])

    def prepare():
        R.f.layers[0].tab[0:NF, :] = I.node[...]
        spread(I.csrc, R.c.cs, R.c.rs, EC // L)
        spread(I.cdst, R.c.cr, R.c.rr, EC // L)
        R.c.layers[1].tab[3 * NC : 512, :] = jnp.zeros((512 - 3 * NC, L), BF)
        R.parts[3 * NC : 512, :] = jnp.zeros((512 - 3 * NC, L), BF)
        R.c.proj[512 + NC : 768, :] = jnp.zeros((256 - NC, L), BF)
        R.c.dg[NC:256, :] = jnp.zeros((256 - NC, L), BF)
        R.delta[0 : 2 * BLOCKS, :] = jnp.zeros((2 * BLOCKS, L), F32)
        owner = jnp.broadcast_to(I.owner[...], (L, BLOCKS)).T
        below = jnp.full((L - BLOCKS, L), -1, I32)
        square = jnp.concatenate([owner, below], axis=0).T
        same = (owner == square[0:BLOCKS, :]) & (iota((BLOCKS, L), 1) < iota((BLOCKS, L), 0))
        rank = lane_sum(jnp.where(same, 1.0, 0.0)).astype(I32)
        place = owner * PAD + rank
        R.place[0][...] = place
        R.place[1][...] = jnp.concatenate([place, below], axis=0).T

    def received(l):
        rows = R.f.layers[l].tab[NF : NF + HALO, :]
        R.delta[2 * BLOCKS :, :] = dot(rows, I.fw.ei[l, 128:256, :])

    def fine_zero():
        halo_wait(R.hs[0], R.f.layers[0].tab, NF, R.hs_sem[0])
        received(0)
        R.state_one[...] = forward(fine, 0, I.edge)

    def sink():
        pooled = (dot(pool_hot(), R.state_one[...]) * (1.0 / POOL)).astype(BF)
        R.ws[0][...] = (dot(put_three(), pooled) + put_flags()).astype(BF)
        wide_start(0)
        edge_base(1, R.state_one[...], R.f.layers[0].e)
        wide_wait(0)
        arrived = R.wr[0][...]
        R.c.layers[0].tab[...] = dot(across_hot(512, three_of), arrived).astype(BF)
        R.live[...] = live_rows(arrived)

    def coarse_layer(l):
        def run():
            if l == 1:
                start(near_table())
            project_own(coarse, l)
            if l == 1:
                wait(near_table())
            project_rest(coarse, l)
            new = forward(coarse, l, I.cedge if l == 0 else R.c.layers[0].e)
            if l == 0:
                R.c.layers[1].tab[0:NC, :] = new
            else:
                R.ws[1][...] = dot(apart_hot(slot_of, 256)[:, 0:NC], new).astype(BF)
                wide_start(1)

        return run

    def rise():
        wide_wait(1)
        picked = dot(take_hot(), R.wr[1][...]).astype(BF)
        R.f.layers[1].tab[0:NF, :] = (R.state_one[...].astype(F32) + dot(grow_hot(), picked)).astype(BF)
        halo_pick(R.f.layers[1].tab, 1)
        halo_start(R.hs[1], R.f.layers[1].tab, NF, R.hs_sem[1])
        w = I.fw.ei
        R.delta[0:BLOCKS, :] = dot(picked, w[1, 128:256, :])
        R.delta[BLOCKS : 2 * BLOCKS, :] = dot(picked, w[1, 256:384, :])
        halo_wait(R.hs[1], R.f.layers[1].tab, NF, R.hs_sem[1])
        received(1)

    def fine_one():
        O.new_state[...] = forward(fine, 1, R.f.layers[0].e)

    def fine_one_back():
        later[:] = backward(
            fine, 1, R.f.layers[0].e, I.cot[...], None, halo_back(2), True, nothing, nothing
        )

    def sink_back():
        halo_add(2)
        grad_two = R.f.acc[...].astype(BF)
        R.grad_two[...] = grad_two
        R.ws[2][...] = dot(put_hot(), dot(pool_hot(), grad_two).astype(BF)).astype(BF)
        wide_start(2)
        for run in later:
            run()
        total[1].one()
        wide_wait(2)
        R.grad_c[...] = dot(across_hot(NC, slot_of), R.wr[2][...]).astype(BF)

    def coarse_back(l):
        def run():
            def send(values):
                if l == 1:
                    R.ns[...] = values
                    start(near_grad())
                else:
                    R.parts[NC : 3 * NC, :] = values

            edges, edge_grad = (I.cedge, R.c.de) if l == 0 else (R.c.layers[0].e, None)
            weights = backward(
                coarse, l, edges, R.grad_c[...], edge_grad, send, l == 1, nothing, nothing
            )
            if l == 1:
                for run in weights:
                    run()
                total[3].one()
                wait(near_grad())
                total[1].two()
                grad = R.c.acc[...] + R.nr[0:NC, :].astype(F32) + R.nr[NC : 2 * NC, :].astype(F32)
                R.grad_c[...] = grad.astype(BF)
            else:
                R.parts[0:NC, :] = R.c.acc[...].astype(BF)
                R.ws[3][...] = dot(apart_hot(three_of, 512), R.parts[...]).astype(BF)
                wide_start(3)
                for run in weights:
                    run()

        return run

    def rise_back():
        total[2].one()
        total[1].three()
        total[3].two()
        wide_wait(3)
        sunk = (dot(take_three(), R.wr[3][...]).astype(BF).astype(F32) * (1.0 / POOL)).astype(BF)
        R.grad_one[...] = (R.grad_two[...].astype(F32) + dot(grow_hot(), sunk)).astype(BF)

    def fine_zero_back():
        def edges_done(edge_weights):
            edge_weights()
            total[0].one()
            total[2].two()
            total[3].three()

        def parts_done(node_weights):
            node_weights()
            R.late[...] = R.gw[0, 0:LATE, :].astype(F32)
            late.one()

        backward(fine, 0, I.edge, R.grad_one[...], R.f.de, halo_back(3), False, edges_done, parts_done)

    def leave():
        total[0].two()
        total[2].three()
        halo_add(3)
        O.state_grad[...] = R.f.acc[...].astype(BF)
        late.two()
        total[0].three()
        total[1].end()
        late.three()
        total[3].end()
        total[2].end()
        total[0].end()
        late.four()
        O.sums[0, 0:LATE, :] = R.late_sum[...]

    steps = (
        enter, prepare, fine_zero, sink, coarse_layer(0), coarse_layer(1), rise, fine_one, fine_one_back, sink_back,
        coarse_back(1), coarse_back(0), rise_back, fine_zero_back, leave,
    )
    for step in steps[:STEPS]:
        step()


def spread_out(state, grad, sums, *refs):
    outs, sem = refs[:-1], refs[-1]
    pairs = [(state, outs[0]), (grad, outs[1])]
    for s in range(4):
        ei, eo, ni, no = outs[2 + 4 * (s // 2) : 6 + 4 * (s // 2)]
        l = s % 2
        for out, there, here, rows in (
            (ei, 0, 256, 128), (ei, 128, 0, 256), (eo, 0, 384, 128), (ni, 0, 512, 256), (no, 0, 768, 128)
        ):
            pairs.append((sums.at[s, pl.ds(here, rows), :], out.at[l, pl.ds(there, rows), :]))
    copies = [pltpu.make_async_copy(src, dst, sem.at[k]) for k, (src, dst) in enumerate(pairs)]
    for copy in copies:
        copy.start()
    for copy in copies:
        copy.wait()


def body(*arrays):
    arrays = list(arrays)
    for i, rows in ((3, EF // L), (4, EF // L), (7, EC // L), (8, EC // L)):
        arrays[i] = arrays[i].reshape(rows, L)
    arrays[6] = arrays[6].reshape(1, BLOCKS)
    states = [jax.ShapeDtypeStruct((NF, L), BF)] * 2
    vm_spec = pl.BlockSpec(memory_space=pltpu.VMEM)
    any_spec = pl.BlockSpec(memory_space=pl.ANY)
    results = pl.pallas_call(
        kernel,
        out_shape=tuple(states + [jax.ShapeDtypeStruct((4, SET, L), F32)]),
        in_specs=[vm_spec] * len(arrays),
        out_specs=(vm_spec,) * 3,
        scratch_shapes=flat(shapes()),
        compiler_params=pltpu.CompilerParams(
            collective_id=0, has_side_effects=True, vmem_limit_bytes=60 * 2**20
        ),
        cost_estimate=pl.CostEstimate(flops=40 * 10**9, bytes_accessed=8 * 2**20, transcendentals=4 * 10**6),
    )(*arrays)
    outs = list(states)
    for _ in range(2):
        outs += [jax.ShapeDtypeStruct((2, rows, L), F32) for rows in (384, 128, 256, 128)]
    return pl.pallas_call(
        spread_out,
        out_shape=tuple(outs),
        in_specs=[vm_spec] * 3,
        out_specs=(any_spec,) * len(outs),
        scratch_shapes=[pltpu.SemaphoreType.DMA((22,))],
    )(*results)


def solution(mesh):
    rows = P(("fine", "coarse"), None)
    flat = P(("fine", "coarse"))
    placed = (rows, rows, rows, flat, flat, rows, rows, flat, flat, rows) + (P(),) * 8
    return jax.shard_map(
        body, mesh=mesh, in_specs=placed, out_specs=(rows, rows) + (P(),) * 8, check_vma=False
    )
```

```python
from types import SimpleNamespace

import jax
import jax.numpy as jnp
from jax import lax
from jax.experimental import pallas as pl
from jax.experimental.pallas import tpu as pltpu
from jax.sharding import PartitionSpec as P

BF = jnp.bfloat16
F32 = jnp.float32
I16 = jnp.int16
I32 = jnp.int32
F8 = jnp.float8_e4m3fn
MESH = pl.DeviceIdType.MESH

L = 128
NF, EF, HALO = 1024, 4096, 512
NC, EC = 160, 640
BLOCKS, POOL, CAP = 64, 16, 5
PAD = 16
N_FINE, N_COARSE = 4, 32
WIDE = N_COARSE * PAD
SET = 896
LATE = 256
OWNED = 32
EPS = 1e-05


def dot(a, b):
    return jnp.dot(a, b, preferred_element_type=F32)


def dot_nt(a, b):
    return lax.dot_general(a, b, (((1,), (1,)), ((), ())), preferred_element_type=F32)


def dot_tn(a, b):
    return lax.dot_general(a, b, (((0,), (0,)), ((), ())), preferred_element_type=F32)


def iota(shape, dim):
    return lax.broadcasted_iota(I32, shape, dim)


def ones_where(mask):
    return jnp.where(mask, jnp.asarray(1, BF), jnp.asarray(0, BF))


def lane_sum(x):
    return jnp.sum(x, axis=-1, keepdims=True)


def normed(y):
    center = y - lane_sum(y) * (1.0 / L)
    scale = lax.rsqrt(lane_sum(center * center) * (1.0 / L) + EPS)
    return center * scale, scale


def normed_back(dn, n, scale):
    return scale * (dn - lane_sum(dn) * (1.0 / L) - n * (lane_sum(dn * n) * (1.0 / L)))


def hot_columns(column, base, width, dtype):
    count = column.shape[0]
    lanes = iota((16, 128), 1).astype(I16)
    parts = []
    for start in range(0, width, 128):
        places = jnp.concatenate([lanes + jnp.asarray(base + start, I16)] * (count // 16), axis=0)
        parts.append(ones_where(column == places))
    hot = jnp.concatenate(parts, axis=1) if len(parts) > 1 else parts[0]
    return hot.astype(dtype)


def gather_rows(columns, table):
    total = None
    for column, first, base, width in columns:
        for k in range(0, width, 256):
            size = min(256, width - k)
            part = dot(hot_columns(column, first + k, size, table.dtype), table[base + k : base + k + size, :])
            total = part if total is None else total + part
    return total


def scatter_rows(rows_ref, data_ref, first, count, edges):
    down = iota((count, 128), 0).astype(I16)
    shift = jnp.asarray(first, I32).astype(I16)
    total = None
    for k in range(0, edges, 256):
        size = min(256, edges - k)
        parts = []
        for j in range(k // 128, (k + size) // 128):
            row = rows_ref[j] - shift
            parts.append(ones_where(down == jnp.concatenate([row] * (count // 16), axis=0)))
        hot = jnp.concatenate(parts, axis=1) if len(parts) > 1 else parts[0]
        part = dot(hot.astype(data_ref.dtype), data_ref[k : k + size, :])
        total = part if total is None else total + part
    return total


def column_peak(x):
    return jnp.max(jnp.abs(x), axis=0, keepdims=True)


def scale_for(peak):
    return jnp.exp2(7.0 - jnp.floor(jnp.log2(jnp.maximum(peak, 1e-30))))


def halves(x, scale):
    x = x * scale
    high = x.astype(F8)
    low = ((x - high.astype(F32)) * 16.0).astype(F8)
    return jnp.concatenate([high, low], axis=1)


def joined(pair, scale):
    return (pair[:, 0:L] + pair[:, L : 2 * L] * 0.0625) * (1.0 / scale)


def vm(*shape, dtype=F32):
    return pltpu.VMEM(shape, dtype)


def level_shapes(n, tab, own, e):
    def layer():
        return SimpleNamespace(
            tab=vm(tab, L, dtype=BF),
            slope=vm(e, L),
            hid=vm(e, L, dtype=BF),
            n=vm(e, L),
            scale=vm(e, L),
            e=vm(e, L, dtype=BF),
            g=vm(n, L, dtype=BF),
            slope2=vm(n, L),
            hid2=vm(n, L, dtype=BF),
            n2=vm(n, L),
            scale2=vm(n, L),
        )

    return SimpleNamespace(
        cs=vm(e, L, dtype=I16),
        cr=vm(e, L, dtype=I16),
        rs=vm(e // L, 16, L, dtype=I16),
        rr=vm(e // L, 16, L, dtype=I16),
        proj=vm(tab + own, L, dtype=BF),
        wide=vm(2 * n, L),
        proj8=vm(tab + own, 2 * L, dtype=F8),
        dz=vm(e, L, dtype=BF),
        e8=vm(e, 2 * L, dtype=F8),
        dg8=vm(own, 2 * L, dtype=F8),
        de=vm(e, L, dtype=BF),
        dg=vm(own, L, dtype=BF),
        dy=vm(e, L, dtype=BF),
        ndy=vm(n, L, dtype=BF),
        ndz=vm(n, L, dtype=BF),
        part=vm(tab, L, dtype=BF),
        other=vm(n, L, dtype=BF),
        acc=vm(n, L),
        layers=[layer(), layer()],
    )


def shapes():
    dma = pltpu.SemaphoreType.DMA
    return SimpleNamespace(
        f=level_shapes(NF, NF + HALO, NF, EF),
        c=level_shapes(NC, 512, 256, EC),
        state_one=vm(NF, L, dtype=BF),
        live=vm(NC, L),
        acc_b=vm(L, L),
        acc_e=vm(L, L),
        block_s=vm(EF, L, dtype=I16),
        block_r=vm(EF, L, dtype=I16),
        delta=vm(2 * BLOCKS + HALO, L),
        hot=SimpleNamespace(
            pool=vm(BLOCKS, NF, dtype=BF),
            grow=vm(NF, BLOCKS, dtype=BF),
            three=vm(WIDE, BLOCKS, dtype=BF),
            flags=vm(WIDE, L),
            put=vm(WIDE, BLOCKS, dtype=BF),
            take=vm(BLOCKS, WIDE, dtype=BF),
            take_three=vm(BLOCKS, WIDE, dtype=BF),
            across=vm(512, WIDE, dtype=BF),
            narrow=vm(NC, WIDE, dtype=BF),
            widen=vm(WIDE, 256, dtype=BF),
            apart=vm(WIDE, 512, dtype=BF),
            flag_row=vm(NC, WIDE, dtype=BF),
            flag_lane=vm(NC, L),
        ),
        halo_col=vm(HALO, L, dtype=I16),
        halo_row=vm(HALO // L, 16, L, dtype=I16),
        grad_two=vm(NF, L, dtype=BF),
        grad_one=vm(NF, L, dtype=BF),
        grad_c=vm(NC, L, dtype=BF),
        place=[vm(BLOCKS, L, dtype=I32), vm(L, L, dtype=I32)],
        hs=[vm(HALO, L, dtype=BF) for _ in range(4)],
        hr=[vm(HALO, L, dtype=BF) for _ in range(2)],
        ws=[vm(WIDE, L, dtype=BF) for _ in range(4)],
        wr=[vm(WIDE, L, dtype=BF) for _ in range(4)],
        ns=vm(2 * NC, L, dtype=BF),
        nr=vm(2 * NC, L, dtype=BF),
        parts=vm(512, L, dtype=BF),
        gw=vm(4, SET, L, dtype=BF),
        late=vm(LATE, L),
        late_got=vm(LATE, L),
        late_quad=vm(N_FINE, 8, L),
        late_sum=vm(LATE, L),
        got=vm(4, N_COARSE * OWNED, L, dtype=BF),
        quad=vm(4, N_FINE, OWNED, L),
        sums=vm(4, N_COARSE * OWNED, L),
        one_sem=dma((5, 2)),
        two_sem=dma((5, 2, 3)),
        three_sem=dma((5, 2)),
        hs_sem=[dma((2, 3)) for _ in range(4)],
        ws_sem=[dma((2,)) for _ in range(4)],
        near_sem=[dma((2, 2)) for _ in range(2)],
    )


def flat(tree):
    if isinstance(tree, SimpleNamespace):
        return [leaf for part in vars(tree).values() for leaf in flat(part)]
    if isinstance(tree, list):
        return [leaf for part in tree for leaf in flat(part)]
    return [tree]


def rebuilt(tree, leaves):
    if isinstance(tree, SimpleNamespace):
        return SimpleNamespace(**{name: rebuilt(part, leaves) for name, part in vars(tree).items()})
    if isinstance(tree, list):
        return [rebuilt(part, leaves) for part in tree]
    return next(leaves)


def operands():
    def weights():
        return SimpleNamespace(ei=None, eo=None, ni=None, no=None)

    inputs = SimpleNamespace(
        node=None, edge=None, cedge=None, src=None, dst=None, halo=None, owner=None, csrc=None, cdst=None, cot=None,
        fw=weights(), cw=weights(),
    )
    outputs = SimpleNamespace(new_state=None, state_grad=None, sums=None)
    return inputs, outputs


STEPS = None


def kernel(*args):
    leaves = iter(args)
    I, O = (rebuilt(tree, leaves) for tree in operands())
    R = rebuilt(shapes(), leaves)
    f = lax.axis_index("fine")
    c = lax.axis_index("coarse")

    def fine_at(d):
        return lax.rem(f + d + N_FINE, N_FINE)

    def coarse_at(d):
        return lax.rem(c + d + N_COARSE, N_COARSE)

    def chunk(i, size, align=None):
        return pl.ds(pl.multiple_of(i * size, align or size), size)

    def remote(src, dst, send, recv, where):
        return pltpu.make_async_remote_copy(
            src_ref=src, dst_ref=dst, send_sem=send, recv_sem=recv, device_id=where, device_id_type=MESH
        )

    def wait_for(view, sem):
        pltpu.make_async_copy(view, view, sem).wait()

    barrier = pltpu.get_barrier_semaphore()

    def greet():
        for d in range(1, N_FINE):
            pl.semaphore_signal(barrier, inc=1, device_id=(fine_at(d), c), device_id_type=MESH)

        def one(d, carry):
            pl.semaphore_signal(barrier, inc=1, device_id=(f, coarse_at(d)), device_id_type=MESH)
            return carry

        lax.fori_loop(N_COARSE // 2, N_COARSE, one, 0)
        lax.fori_loop(1, N_COARSE // 2, one, 0)

    def spread(src, columns, rows, count, blocks=None, shift=0):
        def one(j, carry):
            wide = jnp.broadcast_to(src[pl.ds(j, 1), :], (L, L))
            rows[j] = wide[:16, :].astype(I16)
            tall = wide.T
            columns[chunk(j, L), :] = tall.astype(I16)
            if blocks is not None:
                blocks[chunk(j, L), :] = jnp.where(tall < NF, (tall >> 4) + shift, -1).astype(I16)
            return carry

        lax.fori_loop(0, count, one, 0, unroll=next(u for u in (8, 5, 4) if count % u == 0))

    def halo_copies(src, dst, base, sem):
        out, back = [], []
        for d in range(1, N_FINE):
            q, at = fine_at(d), fine_at(-d)
            out.append(
                remote(
                    src.at[chunk(q, L), :],
                    dst.at[pl.ds(pl.multiple_of(base + f * L, L), L), :],
                    sem.at[0, d - 1],
                    sem.at[1, d - 1],
                    (q, c),
                )
            )
            back.append((dst.at[pl.ds(pl.multiple_of(base + at * L, L), L), :], sem.at[1, d - 1]))
        return out, back

    def halo_start(src, dst, base, sem):
        for copy in halo_copies(src, dst, base, sem)[0]:
            copy.start()
        dst[pl.ds(pl.multiple_of(base + f * L, L), L), :] = src[chunk(f, L), :]

    def halo_wait(src, dst, base, sem):
        out, back = halo_copies(src, dst, base, sem)
        for copy in out:
            copy.wait_send()
        for view, at in back:
            wait_for(view, at)

    def wide_start(k):
        src, dst, sem = R.ws[k], R.wr[k], R.ws_sem[k]

        def one(d, carry):
            o = coarse_at(d)
            remote(src.at[chunk(o, PAD), :], dst.at[chunk(c, PAD), :], sem.at[0], sem.at[1], (f, o)).start()
            return carry

        lax.fori_loop(N_COARSE // 2, N_COARSE, one, 0)
        lax.fori_loop(1, N_COARSE // 2, one, 0)
        dst[chunk(c, PAD), :] = src[chunk(c, PAD), :]

    def wide_wait(k):
        dst, sem = R.wr[k], R.ws_sem[k]
        wait_for(dst.at[pl.ds(0, WIDE - PAD), :], sem.at[0])
        wait_for(dst.at[pl.ds(0, WIDE - PAD), :], sem.at[1])

    def near_copies(up_src, up_dst, down_src, down_dst, sem):
        return (
            remote(up_src, up_dst, sem.at[0, 0], sem.at[1, 0], (f, coarse_at(1))),
            remote(down_src, down_dst, sem.at[0, 1], sem.at[1, 1], (f, coarse_at(-1))),
        )

    def summing(k, owners, block, src, got, quad, dst):
        sem, group_sem, last_sem = R.one_sem.at[k], R.two_sem.at[k], R.three_sem.at[k]
        mine = chunk(c, block)

        def owner(run):
            run() if owners == N_COARSE else pl.when(c < owners)(run)

        def other(run):
            if owners < N_COARSE:
                pl.when(c >= owners)(run)

        def group():
            return [
                remote(quad.at[f], quad.at[f], group_sem.at[0, d - 1], group_sem.at[1, d - 1], (fine_at(d), c))
                for d in range(1, N_FINE)
            ]

        def one():
            def send(d, carry):
                o = coarse_at(d)

                def go():
                    remote(src.at[chunk(o, block), :], got.at[mine, :], sem.at[0], sem.at[1], (f, o)).start()

                go() if owners == N_COARSE else pl.when(o < owners)(go)
                return carry

            lax.fori_loop(N_COARSE // 2, N_COARSE, send, 0)
            lax.fori_loop(1, N_COARSE // 2, send, 0)

        def two():
            def run():
                got[mine, :] = src[mine, :]
                wait_for(got.at[pl.ds(0, (owners - 1) * block), :], sem.at[0])
                wait_for(got.at[pl.ds(0, (N_COARSE - 1) * block), :], sem.at[1])
                parts = [got[j * block : (j + 1) * block, :].astype(F32) for j in range(N_COARSE)]
                while len(parts) > 1:
                    parts = [parts[j] + parts[j + 1] for j in range(0, len(parts), 2)]
                quad[f] = parts[0]
                for copy in group():
                    copy.start()

            owner(run)
            other(lambda: wait_for(got.at[pl.ds(0, owners * block), :], sem.at[0]))

        def three():
            def run():
                for copy in group():
                    copy.wait()
                dst[mine, :] = (quad[0] + quad[1]) + (quad[2] + quad[3])

                def send(d, carry):
                    o = coarse_at(d)
                    remote(dst.at[mine, :], dst.at[mine, :], last_sem.at[0], last_sem.at[1], (f, o)).start()
                    return carry

                lax.fori_loop(N_COARSE // 2, N_COARSE, send, 0)
                lax.fori_loop(1, N_COARSE // 2, send, 0)

            owner(run)

        def four():
            def run():
                wait_for(dst.at[pl.ds(0, (N_COARSE - 1) * block), :], last_sem.at[0])
                wait_for(dst.at[pl.ds(0, (owners - 1) * block), :], last_sem.at[1])

            owner(run)
            other(lambda: wait_for(dst.at[pl.ds(0, owners * block), :], last_sem.at[1]))

        return SimpleNamespace(one=one, two=two, three=three, four=four)

    def summing_set(s):
        first = LATE if s == 0 else 0
        count = SET - first
        work = summing(
            s, count // OWNED, OWNED, R.gw.at[s, pl.ds(first, count), :], R.got.at[s], R.quad.at[s], R.sums.at[s]
        )

        def end():
            work.four()
            O.sums[s, first:SET, :] = R.sums[s, 0:count, :]

        work.end = end
        return work

    total = [summing_set(s) for s in range(4)]
    late = summing(4, N_COARSE, 8, R.late, R.late_got, R.late_quad, R.late_sum)

    fine = SimpleNamespace(
        n=NF, used=NF + HALO, tab=NF + HALO, own=NF, e=EF, tile=1024, block=512, S=R.f, W=I.fw, first=0, masked=False
    )
    coarse = SimpleNamespace(
        n=NC, used=3 * NC, tab=512, own=256, e=EC, tile=EC, block=NC, S=R.c, W=I.cw, first=2, masked=True
    )

    def project_own(v, l):
        w, h = v.W.ei, v.S.layers[l].tab[0 : v.n, :]
        v.S.proj[0 : v.n, :] = dot(h, w[l, 128:256, :]).astype(BF)
        v.S.proj[v.tab : v.tab + v.n, :] = dot(h, w[l, 256:384, :]).astype(BF)

    def project_rest(v, l):
        rest = v.S.layers[l].tab[v.n : v.tab, :]
        v.S.proj[v.n : v.tab, :] = dot(rest, v.W.ei[l, 128:256, :]).astype(BF)

    def edge_base(l, h, edges):
        S, w = R.f, I.fw.ei
        S.wide[0:NF, :] = dot(h, w[l, 128:256, :])
        S.wide[NF : 2 * NF, :] = dot(h, w[l, 256:384, :])
        values = S.wide[0 : 2 * NF, :]
        scale = scale_for(column_peak(values))
        S.proj8[0 : 2 * NF, :] = halves(values, scale)

        def one(i, carry):
            rows = chunk(i, fine.tile)
            columns = ((S.cs[rows, :], 0, 0, NF), (S.cr[rows, :], 0, NF, NF))
            z = joined(gather_rows(columns, S.proj8), scale) + dot(edges[rows, :], w[l, 0:128, :])
            S.layers[l].slope[rows, :] = z
            return carry

        lax.fori_loop(0, EF // fine.tile, one, 0)

    def edge_delta(l, rows):
        S = R.f
        received = gather_rows(((S.cs[rows, :], NF, 2 * BLOCKS, HALO),), S.proj8)
        if l == 0:
            return received
        lanes = iota((16, L), 1).astype(I16)
        lanes = jnp.concatenate([lanes] * (fine.tile // 16), axis=0)
        hot = ones_where((R.block_s[rows, :] == lanes) | (R.block_r[rows, :] == lanes)).astype(F8)
        return dot(hot, S.proj8[0 : 2 * BLOCKS, :]) + received

    def forward(v, l, edges):
        S, W, A = v.S, v.W, v.S.layers[l]
        if not v.masked:
            scale = scale_for(column_peak(R.delta[...]))
            S.proj8[0 : 2 * BLOCKS + HALO, :] = halves(R.delta[...], scale)

        def one(i, peak):
            rows = chunk(i, v.tile)
            old = edges[rows, :]
            if v.masked:
                columns = ((S.cs[rows, :], 0, 0, v.tab), (S.cr[rows, :], 0, v.tab, v.own))
                z = gather_rows(columns, S.proj) + dot(old, W.ei[l, 0:128, :])
            else:
                z = A.slope[rows, :] + joined(edge_delta(l, rows), scale)
            gate = jax.nn.sigmoid(z)
            hidden = z * gate
            A.slope[rows, :] = gate * (1.0 + z - hidden)
            hidden = hidden.astype(BF)
            A.hid[rows, :] = hidden
            values, spread_by = normed(dot(hidden, W.eo[l]))
            A.n[rows, :] = values
            A.scale[rows, :] = jnp.broadcast_to(spread_by, values.shape)
            new = (old.astype(F32) + values).astype(BF)
            A.e[rows, :] = new
            return jnp.maximum(peak, column_peak(new.astype(F32)))

        peak = lax.fori_loop(0, v.e // v.tile, one, jnp.zeros((1, L), F32))
        if not v.masked:
            scale = scale_for(peak)

            def split(i, carry):
                rows = chunk(i, v.tile)
                S.e8[rows, :] = halves(A.e[rows, :].astype(F32), scale)
                return carry

            lax.fori_loop(0, v.e // v.tile, split, 0)

        def two(i, carry):
            rows = chunk(i, v.block)
            if v.masked:
                g = scatter_rows(S.rr, A.e, i * v.block, v.block, v.e)
            else:
                g = joined(scatter_rows(S.rr, S.e8, i * v.block, v.block, v.e), scale)
            A.g[rows, :] = g.astype(BF)
            return carry

        lax.fori_loop(0, v.n // v.block, two, 0)
        h = A.tab[0 : v.n, :]
        z = dot(h, W.ni[l, 0:128, :]) + dot(A.g[...], W.ni[l, 128:256, :])
        gate = jax.nn.sigmoid(z)
        hidden = z * gate
        A.slope2[...] = gate * (1.0 + z - hidden)
        hidden = hidden.astype(BF)
        A.hid2[...] = hidden
        values, spread_by = normed(dot(hidden, W.no[l]))
        A.n2[...] = values
        A.scale2[...] = jnp.broadcast_to(spread_by, values.shape)
        new = h.astype(F32) + values
        if v.masked:
            new = new * R.live[...]
        return new.astype(BF)

    def backward(v, l, edges, grad, edge_grad, send_rest, keep_edge, edges_done, parts_done):
        S, W, A = v.S, v.W, v.S.layers[l]
        s, acc, gw = v.first + l, v.S.acc, R.gw
        dn = grad.astype(F32)
        if v.masked:
            dn = dn * R.live[...]
        dy = normed_back(dn, A.n2[...], A.scale2[...]).astype(BF)
        dz = (dot_nt(dy, W.no[l]) * A.slope2[...]).astype(BF)
        S.ndy[...] = dy
        S.ndz[...] = dz
        dg = dot_nt(dz, W.ni[l, 128:256, :])
        if v.masked:
            S.dg[0 : v.n, :] = dg.astype(BF)
        else:
            dg_scale = scale_for(column_peak(dg))
            S.dg8[...] = halves(dg, dg_scale)
        acc[...] = dn + dot_nt(dz, W.ni[l, 0:128, :])

        def one(i, peak):
            rows = chunk(i, v.tile)
            columns = ((S.cr[rows, :], 0, 0, v.own),)
            if v.masked:
                dn = gather_rows(columns, S.dg)
            else:
                dn = joined(gather_rows(columns, S.dg8), dg_scale)
            if edge_grad is not None:
                dn = dn + edge_grad[rows, :].astype(F32)
            dy = normed_back(dn, A.n[rows, :], A.scale[rows, :]).astype(BF)
            dz = (dot_nt(dy, W.eo[l]) * A.slope[rows, :]).astype(BF)
            S.dy[rows, :] = dy
            S.dz[rows, :] = dz
            if keep_edge:
                S.de[rows, :] = dn.astype(BF)
            return jnp.maximum(peak, column_peak(dz.astype(F32)))

        peak = lax.fori_loop(0, v.e // v.tile, one, jnp.zeros((1, L), F32))

        def edge_weights():
            gw[s, 512:640, :] = dot_tn(A.tab[0 : v.n, :], S.ndz[...]).astype(BF)
            gw[s, 640:768, :] = dot_tn(A.g[...], S.ndz[...]).astype(BF)
            gw[s, 768:896, :] = dot_tn(A.hid2[...], S.ndy[...]).astype(BF)
            R.acc_b[...] = jnp.zeros((L, L), F32)
            R.acc_e[...] = jnp.zeros((L, L), F32)

            def add(i, carry):
                rows = chunk(i, v.tile)
                dz = S.dz[rows, :]
                R.acc_b[...] += dot_tn(A.hid[rows, :], S.dy[rows, :])
                R.acc_e[...] += dot_tn(edges[rows, :], dz)
                if keep_edge:
                    S.de[rows, :] = (S.de[rows, :].astype(F32) + dot_nt(dz, W.ei[l, 0:128, :])).astype(BF)
                return carry

            lax.fori_loop(0, v.e // v.tile, add, 0)
            gw[s, 256:384, :] = R.acc_e[...].astype(BF)
            gw[s, 384:512, :] = R.acc_b[...].astype(BF)

        def node_weights():
            gw[s, 0:128, :] = dot_tn(A.tab[0 : v.used, :], S.part[0 : v.used, :]).astype(BF)
            gw[s, 128:256, :] = dot_tn(A.tab[0 : v.n, :], S.other[...]).astype(BF)

        edges_done(edge_weights)
        if v.masked:

            def spread_back(rows_ref, first, count):
                return scatter_rows(rows_ref, S.dz, first, count, v.e).astype(BF)

        else:
            scale = scale_for(peak)

            def split(i, carry):
                rows = chunk(i, v.tile)
                S.e8[rows, :] = halves(S.dz[rows, :].astype(F32), scale)
                return carry

            lax.fori_loop(0, v.e // v.tile, split, 0)

            def spread_back(rows_ref, first, count):
                return joined(scatter_rows(rows_ref, S.e8, first, count, v.e), scale).astype(BF)

        rest = spread_back(S.rs, v.n, v.used - v.n)
        S.part[v.n : v.used, :] = rest
        send_rest(dot_nt(rest, W.ei[l, 128:256, :]).astype(BF))

        def two(i, carry):
            rows = chunk(i, v.block)
            S.part[rows, :] = spread_back(S.rs, i * v.block, v.block)
            S.other[rows, :] = spread_back(S.rr, i * v.block, v.block)
            return carry

        lax.fori_loop(0, v.n // v.block, two, 0)
        parts_done(node_weights)
        acc[...] += dot_nt(S.part[0 : v.n, :], W.ei[l, 128:256, :]) + dot_nt(S.other[...], W.ei[l, 256:384, :])
        return edge_weights, node_weights

    def place_column():
        return R.place[0][...]

    def place_wide():
        return jnp.broadcast_to(R.place[1][0:1, :], (WIDE, L))

    def pool_hot():
        return ones_where((iota((BLOCKS, NF), 1) >> 4) == iota((BLOCKS, NF), 0))

    def grow_hot():
        return ones_where((iota((NF, L), 0) >> 4) == iota((NF, L), 1))[:, 0:BLOCKS]

    def put_hot():
        return ones_where(iota((WIDE, L), 0) == place_wide())[:, 0:BLOCKS]

    def three_places(owner, rank):
        places = []
        for part, shift in ((0, 0), (1, 1), (2, N_COARSE - 1)):
            places.append(((owner + shift) & (N_COARSE - 1)) * PAD + part * CAP + rank)
        return places

    def put_three():
        wide = place_wide()
        down = iota((WIDE, L), 0)
        a, b, d = three_places(wide >> 4, wide & (PAD - 1))
        return ones_where((down == a) | (down == b) | (down == d))[:, 0:BLOCKS]

    def put_flags():
        row = ones_where(iota((WIDE, L), 0) == (place_wide() | (PAD - 1)))[:, 0:BLOCKS]
        lane = ones_where(iota((BLOCKS, L), 1) == (place_column() & (PAD - 1)))
        return dot(row, lane)

    def take_hot():
        return ones_where(jnp.concatenate([place_column()] * 4, axis=1) == iota((BLOCKS, WIDE), 1))

    def take_three():
        place = place_column()
        across = iota((BLOCKS, WIDE), 1)
        a, b, d = (jnp.concatenate([at] * 4, axis=1) for at in three_places(place >> 4, place & (PAD - 1)))
        return ones_where((across == a) | (across == b) | (across == d))

    def slot_of(index):
        within = index & (PAD - 1)
        return jnp.where(within < CAP, (index >> 4) * CAP + within, -1)

    def three_of(index):
        within = index & (PAD - 1)
        part = jnp.where(within >= 2 * CAP, 2, jnp.where(within >= CAP, 1, 0))
        return jnp.where(within < 3 * CAP, part * (NC - CAP) + (index >> 4) * CAP + within, -1)

    def across_hot(rows, places):
        down = iota((rows, 128), 0).astype(I16)
        parts = []
        for k in range(0, WIDE, 128):
            at = places(iota((16, 128), 1) + k).astype(I16)
            parts.append(ones_where(down == jnp.concatenate([at] * (rows // 16), axis=0)))
        return jnp.concatenate(parts, axis=1)

    def apart_hot(places, width):
        at = places(iota((WIDE, 128), 0)).astype(I16)
        lanes = iota((16, 128), 1).astype(I16)
        parts = []
        for k in range(0, width, 128):
            here = jnp.concatenate([lanes + jnp.asarray(k, I16)] * (WIDE // 16), axis=0)
            parts.append(ones_where(at == here))
        return jnp.concatenate(parts, axis=1)

    def flag_places():
        slot = iota((NC, WIDE), 0)
        first = (iota((NC, WIDE), 1) >> 4) * CAP
        last_row = (iota((NC, WIDE), 1) & (PAD - 1)) == PAD - 1
        row = ones_where(last_row & (slot >= first) & (slot < first + CAP))
        count = iota((NC, L), 0).astype(F32)
        within = iota((NC, L), 0) - jnp.floor((count + 0.5) * (1.0 / CAP)).astype(I32) * CAP
        return row, jnp.where(iota((NC, L), 1) == within, 1.0, 0.0)

    def build_hot():
        hot = R.hot
        hot.pool[...] = pool_hot()
        hot.grow[...] = grow_hot()
        hot.three[...] = put_three()
        hot.flags[...] = put_flags()
        hot.put[...] = put_hot()
        hot.take[...] = take_hot()
        hot.take_three[...] = take_three()
        hot.across[...] = across_hot(512, three_of)
        hot.narrow[...] = across_hot(NC, slot_of)
        hot.widen[...] = apart_hot(slot_of, 256)
        hot.apart[...] = apart_hot(three_of, 512)
        hot.flag_row[...], hot.flag_lane[...] = flag_places()

    def halo_pick(tab, k):
        R.hs[k][...] = gather_rows(((R.halo_col[...], 0, 0, NF),), tab).astype(BF)

    def halo_back(k):
        def send(values):
            R.hs[k][...] = values
            halo_start(R.hs[k], R.hr[k - 2], 0, R.hs_sem[k])

        return send

    def halo_add(k):
        halo_wait(R.hs[k], R.hr[k - 2], 0, R.hs_sem[k])

        def one(i, carry):
            rows = chunk(i, 512)
            R.f.acc[rows, :] += scatter_rows(R.halo_row, R.hr[k - 2], i * 512, 512, HALO)
            return carry

        lax.fori_loop(0, NF // 512, one, 0)

    def near_table():
        tab = R.c.layers[1].tab
        own = tab.at[pl.ds(0, NC), :]
        return near_copies(own, tab.at[pl.ds(NC, NC), :], own, tab.at[pl.ds(2 * NC, NC), :], R.near_sem[0])

    def near_grad():
        low, high = pl.ds(0, NC), pl.ds(NC, NC)
        return near_copies(
            R.ns.at[high, :], R.nr.at[low, :], R.ns.at[low, :], R.nr.at[high, :], R.near_sem[1]
        )

    def start(copies):
        for copy in copies:
            copy.start()

    def wait(copies):
        for copy in copies:
            copy.wait()

    later = []

    def nothing(run):
        pass

    def enter():
        greet()
        spread(I.halo, R.halo_col, R.halo_row, HALO // L)
        halo_pick(I.node, 0)
        spread(I.src, R.f.cs, R.f.rs, EF // L, R.block_s)
        spread(I.dst, R.f.cr, R.f.rr, EF // L, R.block_r, BLOCKS)
        edge_base(0, I.node[...], I.edge)
        pl.semaphore_wait(barrier, N_FINE - 1 + N_COARSE - 1)
        halo_start(R.hs[0], R.f.layers[0].tab, NF, R.hs_sem[0])

    def prepare():
        R.f.layers[0].tab[0:NF, :] = I.node[...]
        spread(I.csrc, R.c.cs, R.c.rs, EC // L)
        spread(I.cdst, R.c.cr, R.c.rr, EC // L)
        R.c.layers[1].tab[3 * NC : 512, :] = jnp.zeros((512 - 3 * NC, L), BF)
        R.parts[3 * NC : 512, :] = jnp.zeros((512 - 3 * NC, L), BF)
        R.c.proj[512 + NC : 768, :] = jnp.zeros((256 - NC, L), BF)
        R.c.dg[NC:256, :] = jnp.zeros((256 - NC, L), BF)
        R.delta[0 : 2 * BLOCKS, :] = jnp.zeros((2 * BLOCKS, L), F32)
        owner = jnp.broadcast_to(I.owner[...], (L, BLOCKS)).T
        below = jnp.full((L - BLOCKS, L), -1, I32)
        square = jnp.concatenate([owner, below], axis=0).T
        same = (owner == square[0:BLOCKS, :]) & (iota((BLOCKS, L), 1) < iota((BLOCKS, L), 0))
        rank = lane_sum(jnp.where(same, 1.0, 0.0)).astype(I32)
        place = owner * PAD + rank
        R.place[0][...] = place
        R.place[1][...] = jnp.concatenate([place, below], axis=0).T
        build_hot()

    def received(l):
        rows = R.f.layers[l].tab[NF : NF + HALO, :]
        R.delta[2 * BLOCKS :, :] = dot(rows, I.fw.ei[l, 128:256, :])

    def fine_zero():
        halo_wait(R.hs[0], R.f.layers[0].tab, NF, R.hs_sem[0])
        received(0)
        R.state_one[...] = forward(fine, 0, I.edge)

    def sink():
        pooled = (dot(R.hot.pool[...], R.state_one[...]) * (1.0 / POOL)).astype(BF)
        R.ws[0][...] = (dot(R.hot.three[...], pooled) + R.hot.flags[...]).astype(BF)
        wide_start(0)
        edge_base(1, R.state_one[...], R.f.layers[0].e)
        wide_wait(0)
        arrived = R.wr[0][...]
        R.c.layers[0].tab[...] = dot(R.hot.across[...], arrived).astype(BF)
        row = dot(R.hot.flag_row[...], arrived) * R.hot.flag_lane[...]
        R.live[...] = jnp.broadcast_to(lane_sum(row), (NC, L))

    def coarse_layer(l):
        def run():
            if l == 1:
                start(near_table())
            project_own(coarse, l)
            if l == 1:
                wait(near_table())
            project_rest(coarse, l)
            new = forward(coarse, l, I.cedge if l == 0 else R.c.layers[0].e)
            if l == 0:
                R.c.layers[1].tab[0:NC, :] = new
            else:
                R.ws[1][...] = dot(R.hot.widen[:, 0:NC], new).astype(BF)
                wide_start(1)

        return run

    def rise():
        wide_wait(1)
        picked = dot(R.hot.take[...], R.wr[1][...]).astype(BF)
        R.f.layers[1].tab[0:NF, :] = (R.state_one[...].astype(F32) + dot(R.hot.grow[...], picked)).astype(BF)
        halo_pick(R.f.layers[1].tab, 1)
        halo_start(R.hs[1], R.f.layers[1].tab, NF, R.hs_sem[1])
        w = I.fw.ei
        R.delta[0:BLOCKS, :] = dot(picked, w[1, 128:256, :])
        R.delta[BLOCKS : 2 * BLOCKS, :] = dot(picked, w[1, 256:384, :])
        halo_wait(R.hs[1], R.f.layers[1].tab, NF, R.hs_sem[1])
        received(1)

    def fine_one():
        O.new_state[...] = forward(fine, 1, R.f.layers[0].e)

    def fine_one_back():
        later[:] = backward(
            fine, 1, R.f.layers[0].e, I.cot[...], None, halo_back(2), True, nothing, nothing
        )

    def sink_back():
        halo_add(2)
        grad_two = R.f.acc[...].astype(BF)
        R.grad_two[...] = grad_two
        R.ws[2][...] = dot(R.hot.put[...], dot(R.hot.pool[...], grad_two).astype(BF)).astype(BF)
        wide_start(2)
        for run in later:
            run()
        total[1].one()
        wide_wait(2)
        R.grad_c[...] = dot(R.hot.narrow[...], R.wr[2][...]).astype(BF)

    def coarse_back(l):
        def run():
            def send(values):
                if l == 1:
                    R.ns[...] = values
                    start(near_grad())
                else:
                    R.parts[NC : 3 * NC, :] = values

            edges, edge_grad = (I.cedge, R.c.de) if l == 0 else (R.c.layers[0].e, None)
            weights = backward(
                coarse, l, edges, R.grad_c[...], edge_grad, send, l == 1, nothing, nothing
            )
            if l == 1:
                for run in weights:
                    run()
                total[3].one()
                wait(near_grad())
                total[1].two()
                grad = R.c.acc[...] + R.nr[0:NC, :].astype(F32) + R.nr[NC : 2 * NC, :].astype(F32)
                R.grad_c[...] = grad.astype(BF)
            else:
                R.parts[0:NC, :] = R.c.acc[...].astype(BF)
                R.ws[3][...] = dot(R.hot.apart[...], R.parts[...]).astype(BF)
                wide_start(3)
                for run in weights:
                    run()

        return run

    def rise_back():
        total[2].one()
        total[1].three()
        total[3].two()
        wide_wait(3)
        sunk = (dot(R.hot.take_three[...], R.wr[3][...]).astype(BF).astype(F32) * (1.0 / POOL)).astype(BF)
        R.grad_one[...] = (R.grad_two[...].astype(F32) + dot(R.hot.grow[...], sunk)).astype(BF)

    def fine_zero_back():
        def edges_done(edge_weights):
            edge_weights()
            total[0].one()
            total[2].two()
            total[3].three()

        def parts_done(node_weights):
            node_weights()
            R.late[...] = R.gw[0, 0:LATE, :].astype(F32)
            late.one()

        backward(fine, 0, I.edge, R.grad_one[...], R.f.de, halo_back(3), False, edges_done, parts_done)

    def leave():
        total[0].two()
        total[2].three()
        halo_add(3)
        O.state_grad[...] = R.f.acc[...].astype(BF)
        late.two()
        late.three()
        total[0].three()
        total[1].end()
        total[3].end()
        total[2].end()
        total[0].end()
        late.four()
        O.sums[0, 0:LATE, :] = R.late_sum[...]

    steps = (
        enter, prepare, fine_zero, sink, coarse_layer(0), coarse_layer(1), rise, fine_one, fine_one_back, sink_back,
        coarse_back(1), coarse_back(0), rise_back, fine_zero_back, leave,
    )
    for step in steps[:STEPS]:
        step()


def spread_out(state, grad, sums, *refs):
    outs, sem = refs[:-1], refs[-1]
    pairs = [(state, outs[0]), (grad, outs[1])]
    for s in range(4):
        ei, eo, ni, no = outs[2 + 4 * (s // 2) : 6 + 4 * (s // 2)]
        l = s % 2
        for out, there, here, rows in (
            (ei, 0, 256, 128), (ei, 128, 0, 256), (eo, 0, 384, 128), (ni, 0, 512, 256), (no, 0, 768, 128)
        ):
            pairs.append((sums.at[s, pl.ds(here, rows), :], out.at[l, pl.ds(there, rows), :]))
    copies = [pltpu.make_async_copy(src, dst, sem.at[k]) for k, (src, dst) in enumerate(pairs)]
    for copy in copies:
        copy.start()
    for copy in copies:
        copy.wait()


def body(*arrays):
    arrays = list(arrays)
    for i, rows in ((3, EF // L), (4, EF // L), (7, EC // L), (8, EC // L)):
        arrays[i] = arrays[i].reshape(rows, L)
    arrays[6] = arrays[6].reshape(1, BLOCKS)
    states = [jax.ShapeDtypeStruct((NF, L), BF)] * 2
    vm_spec = pl.BlockSpec(memory_space=pltpu.VMEM)
    any_spec = pl.BlockSpec(memory_space=pl.ANY)
    results = pl.pallas_call(
        kernel,
        out_shape=tuple(states + [jax.ShapeDtypeStruct((4, SET, L), F32)]),
        in_specs=[vm_spec] * len(arrays),
        out_specs=(vm_spec,) * 3,
        scratch_shapes=flat(shapes()),
        compiler_params=pltpu.CompilerParams(
            collective_id=0, has_side_effects=True, vmem_limit_bytes=60 * 2**20
        ),
        cost_estimate=pl.CostEstimate(flops=40 * 10**9, bytes_accessed=8 * 2**20, transcendentals=4 * 10**6),
    )(*arrays)
    outs = list(states)
    for _ in range(2):
        outs += [jax.ShapeDtypeStruct((2, rows, L), F32) for rows in (384, 128, 256, 128)]
    return pl.pallas_call(
        spread_out,
        out_shape=tuple(outs),
        in_specs=[vm_spec] * 3,
        out_specs=(any_spec,) * len(outs),
        scratch_shapes=[pltpu.SemaphoreType.DMA((22,))],
    )(*results)


def solution(mesh):
    rows = P(("fine", "coarse"), None)
    flat = P(("fine", "coarse"))
    placed = (rows, rows, rows, flat, flat, rows, rows, flat, flat, rows) + (P(),) * 8
    return jax.shard_map(
        body, mesh=mesh, in_specs=placed, out_specs=(rows, rows) + (P(),) * 8, check_vma=False
    )
```

```python
from types import SimpleNamespace

import jax
import jax.numpy as jnp
from jax import lax
from jax.experimental import pallas as pl
from jax.experimental.pallas import tpu as pltpu
from jax.sharding import PartitionSpec as P

BF = jnp.bfloat16
F32 = jnp.float32
I16 = jnp.int16
I32 = jnp.int32
F8 = jnp.float8_e4m3fn
MESH = pl.DeviceIdType.MESH

L = 128
NF, EF, HALO = 1024, 4096, 512
NC, EC = 160, 640
BLOCKS, POOL, CAP = 64, 16, 5
PAD = 16
N_FINE, N_COARSE = 4, 32
WIDE = N_COARSE * PAD
SET = 896
LATE = 256
OWNED = 32
EPS = 1e-05


def dot(a, b):
    return jnp.dot(a, b, preferred_element_type=F32)


def dot_nt(a, b):
    return lax.dot_general(a, b, (((1,), (1,)), ((), ())), preferred_element_type=F32)


def dot_tn(a, b):
    return lax.dot_general(a, b, (((0,), (0,)), ((), ())), preferred_element_type=F32)


def iota(shape, dim):
    return lax.broadcasted_iota(I32, shape, dim)


def ones_where(mask):
    return jnp.where(mask, jnp.asarray(1, BF), jnp.asarray(0, BF))


def lane_sum(x):
    return jnp.sum(x, axis=-1, keepdims=True)


def normed(y):
    center = y - lane_sum(y) * (1.0 / L)
    scale = lax.rsqrt(lane_sum(center * center) * (1.0 / L) + EPS)
    return center * scale, scale


def normed_back(dn, n, scale):
    return scale * (dn - lane_sum(dn) * (1.0 / L) - n * (lane_sum(dn * n) * (1.0 / L)))


def hot_columns(column, base, width, dtype):
    count = column.shape[0]
    lanes = iota((16, 128), 1).astype(I16)
    parts = []
    for start in range(0, width, 128):
        places = jnp.concatenate([lanes + jnp.asarray(base + start, I16)] * (count // 16), axis=0)
        parts.append(ones_where(column == places))
    hot = jnp.concatenate(parts, axis=1) if len(parts) > 1 else parts[0]
    return hot.astype(dtype)


def gather_rows(columns, table):
    total = None
    for column, first, base, width in columns:
        for k in range(0, width, 256):
            size = min(256, width - k)
            part = dot(hot_columns(column, first + k, size, table.dtype), table[base + k : base + k + size, :])
            total = part if total is None else total + part
    return total


def scatter_rows(rows_ref, data_ref, first, count, edges):
    down = iota((count, 128), 0).astype(I16)
    shift = jnp.asarray(first, I32).astype(I16)
    total = None
    for k in range(0, edges, 256):
        size = min(256, edges - k)
        parts = []
        for j in range(k // 128, (k + size) // 128):
            row = rows_ref[j] - shift
            parts.append(ones_where(down == jnp.concatenate([row] * (count // 16), axis=0)))
        hot = jnp.concatenate(parts, axis=1) if len(parts) > 1 else parts[0]
        part = dot(hot.astype(data_ref.dtype), data_ref[k : k + size, :])
        total = part if total is None else total + part
    return total


def column_peak(x):
    return jnp.max(jnp.abs(x), axis=0, keepdims=True)


def scale_for(peak):
    return jnp.exp2(7.0 - jnp.floor(jnp.log2(jnp.maximum(peak, 1e-30))))


def halves(x, scale):
    x = x * scale
    high = x.astype(F8)
    low = ((x - high.astype(F32)) * 16.0).astype(F8)
    return jnp.concatenate([high, low], axis=1)


def joined(pair, scale):
    return (pair[:, 0:L] + pair[:, L : 2 * L] * 0.0625) * (1.0 / scale)


def vm(*shape, dtype=F32):
    return pltpu.VMEM(shape, dtype)


def level_shapes(n, tab, own, e):
    def layer():
        return SimpleNamespace(
            tab=vm(tab, L, dtype=BF),
            slope=vm(e, L),
            hid=vm(e, L, dtype=BF),
            n=vm(e, L),
            scale=vm(e, L),
            e=vm(e, L, dtype=BF),
            g=vm(n, L, dtype=BF),
            slope2=vm(n, L),
            hid2=vm(n, L, dtype=BF),
            n2=vm(n, L),
            scale2=vm(n, L),
        )

    return SimpleNamespace(
        cs=vm(e, L, dtype=I16),
        cr=vm(e, L, dtype=I16),
        rs=vm(e // L, 16, L, dtype=I16),
        rr=vm(e // L, 16, L, dtype=I16),
        proj=vm(tab + own, L, dtype=BF),
        wide=vm(2 * n, L),
        proj8=vm(tab + own, 2 * L, dtype=F8),
        dz=vm(e, L, dtype=BF),
        e8=vm(e, 2 * L, dtype=F8),
        dg8=vm(own, 2 * L, dtype=F8),
        de=vm(e, L, dtype=BF),
        dg=vm(own, L, dtype=BF),
        dy=vm(e, L, dtype=BF),
        ndy=vm(n, L, dtype=BF),
        ndz=vm(n, L, dtype=BF),
        part=vm(tab, L, dtype=BF),
        other=vm(n, L, dtype=BF),
        acc=vm(n, L),
        layers=[layer(), layer()],
    )


def shapes():
    dma = pltpu.SemaphoreType.DMA
    return SimpleNamespace(
        f=level_shapes(NF, NF + HALO, NF, EF),
        c=level_shapes(NC, 512, 256, EC),
        state_one=vm(NF, L, dtype=BF),
        live=vm(NC, L),
        acc_b=vm(L, L),
        acc_e=vm(L, L),
        block_s=vm(EF, L, dtype=I16),
        block_r=vm(EF, L, dtype=I16),
        delta=vm(2 * BLOCKS + HALO, L),
        hot=SimpleNamespace(
            pool=vm(BLOCKS, NF, dtype=BF),
            grow=vm(NF, BLOCKS, dtype=BF),
            three=vm(WIDE, BLOCKS, dtype=BF),
            flags=vm(WIDE, L),
            put=vm(WIDE, BLOCKS, dtype=BF),
            take=vm(BLOCKS, WIDE, dtype=BF),
            take_three=vm(BLOCKS, WIDE, dtype=BF),
            across=vm(512, WIDE, dtype=BF),
            narrow=vm(NC, WIDE, dtype=BF),
            widen=vm(WIDE, 256, dtype=BF),
            apart=vm(WIDE, 512, dtype=BF),
            flag_row=vm(NC, WIDE, dtype=BF),
            flag_lane=vm(NC, L),
        ),
        halo_col=vm(HALO, L, dtype=I16),
        halo_row=vm(HALO // L, 16, L, dtype=I16),
        grad_two=vm(NF, L, dtype=BF),
        grad_one=vm(NF, L, dtype=BF),
        grad_c=vm(NC, L, dtype=BF),
        place=[vm(BLOCKS, L, dtype=I32), vm(L, L, dtype=I32)],
        hs=[vm(HALO, L, dtype=BF) for _ in range(4)],
        hr=[vm(HALO, L, dtype=BF) for _ in range(2)],
        ws=[vm(WIDE, L, dtype=BF) for _ in range(4)],
        wr=[vm(WIDE, L, dtype=BF) for _ in range(4)],
        ns=vm(2 * NC, L, dtype=BF),
        nr=vm(2 * NC, L, dtype=BF),
        parts=vm(512, L, dtype=BF),
        gw=vm(4, SET, L, dtype=BF),
        late=vm(LATE, L),
        late_got=vm(LATE, L),
        late_quad=vm(N_FINE, 8, L),
        late_sum=vm(LATE, L),
        got=vm(4, N_COARSE * OWNED, L, dtype=BF),
        quad=vm(4, N_FINE, OWNED, L),
        sums=vm(4, N_COARSE * OWNED, L),
        one_sem=dma((5, 2)),
        two_sem=dma((5, 2, 3)),
        three_sem=dma((5, 2)),
        hs_sem=[dma((2, 3)) for _ in range(4)],
        ws_sem=[dma((2,)) for _ in range(4)],
        near_sem=[dma((2, 2)) for _ in range(2)],
    )


def flat(tree):
    if isinstance(tree, SimpleNamespace):
        return [leaf for part in vars(tree).values() for leaf in flat(part)]
    if isinstance(tree, list):
        return [leaf for part in tree for leaf in flat(part)]
    return [tree]


def rebuilt(tree, leaves):
    if isinstance(tree, SimpleNamespace):
        return SimpleNamespace(**{name: rebuilt(part, leaves) for name, part in vars(tree).items()})
    if isinstance(tree, list):
        return [rebuilt(part, leaves) for part in tree]
    return next(leaves)


def operands():
    def weights():
        return SimpleNamespace(ei=None, eo=None, ni=None, no=None)

    inputs = SimpleNamespace(
        node=None, edge=None, cedge=None, src=None, dst=None, halo=None, owner=None, csrc=None, cdst=None, cot=None,
        fw=weights(), cw=weights(),
    )
    outputs = SimpleNamespace(new_state=None, state_grad=None, sums=None)
    return inputs, outputs


STEPS = None


def kernel(*args):
    leaves = iter(args)
    I, O = (rebuilt(tree, leaves) for tree in operands())
    R = rebuilt(shapes(), leaves)
    f = lax.axis_index("fine")
    c = lax.axis_index("coarse")

    def fine_at(d):
        return lax.rem(f + d + N_FINE, N_FINE)

    def coarse_at(d):
        return lax.rem(c + d + N_COARSE, N_COARSE)

    def chunk(i, size, align=None):
        return pl.ds(pl.multiple_of(i * size, align or size), size)

    def remote(src, dst, send, recv, where):
        return pltpu.make_async_remote_copy(
            src_ref=src, dst_ref=dst, send_sem=send, recv_sem=recv, device_id=where, device_id_type=MESH
        )

    def wait_for(view, sem):
        pltpu.make_async_copy(view, view, sem).wait()

    barrier = pltpu.get_barrier_semaphore()

    def greet():
        for d in range(1, N_FINE):
            pl.semaphore_signal(barrier, inc=1, device_id=(fine_at(d), c), device_id_type=MESH)

        def one(d, carry):
            pl.semaphore_signal(barrier, inc=1, device_id=(f, coarse_at(d)), device_id_type=MESH)
            return carry

        lax.fori_loop(N_COARSE // 2, N_COARSE, one, 0)
        lax.fori_loop(1, N_COARSE // 2, one, 0)

    def spread(src, columns, rows, count, blocks=None, shift=0):
        def one(j, carry):
            wide = jnp.broadcast_to(src[pl.ds(j, 1), :], (L, L))
            rows[j] = wide[:16, :].astype(I16)
            tall = wide.T
            columns[chunk(j, L), :] = tall.astype(I16)
            if blocks is not None:
                blocks[chunk(j, L), :] = jnp.where(tall < NF, (tall >> 4) + shift, -1).astype(I16)
            return carry

        lax.fori_loop(0, count, one, 0, unroll=next(u for u in (8, 5, 4) if count % u == 0))

    def halo_copies(src, dst, base, sem):
        out, back = [], []
        for d in range(1, N_FINE):
            q, at = fine_at(d), fine_at(-d)
            out.append(
                remote(
                    src.at[chunk(q, L), :],
                    dst.at[pl.ds(pl.multiple_of(base + f * L, L), L), :],
                    sem.at[0, d - 1],
                    sem.at[1, d - 1],
                    (q, c),
                )
            )
            back.append((dst.at[pl.ds(pl.multiple_of(base + at * L, L), L), :], sem.at[1, d - 1]))
        return out, back

    def halo_start(src, dst, base, sem):
        for copy in halo_copies(src, dst, base, sem)[0]:
            copy.start()
        dst[pl.ds(pl.multiple_of(base + f * L, L), L), :] = src[chunk(f, L), :]

    def halo_wait(src, dst, base, sem):
        out, back = halo_copies(src, dst, base, sem)
        for copy in out:
            copy.wait_send()
        for view, at in back:
            wait_for(view, at)

    def wide_start(k):
        src, dst, sem = R.ws[k], R.wr[k], R.ws_sem[k]

        def one(d, carry):
            o = coarse_at(d)
            remote(src.at[chunk(o, PAD), :], dst.at[chunk(c, PAD), :], sem.at[0], sem.at[1], (f, o)).start()
            return carry

        lax.fori_loop(N_COARSE // 2, N_COARSE, one, 0)
        lax.fori_loop(1, N_COARSE // 2, one, 0)
        dst[chunk(c, PAD), :] = src[chunk(c, PAD), :]

    def wide_wait(k):
        dst, sem = R.wr[k], R.ws_sem[k]
        wait_for(dst.at[pl.ds(0, WIDE - PAD), :], sem.at[0])
        wait_for(dst.at[pl.ds(0, WIDE - PAD), :], sem.at[1])

    def near_copies(up_src, up_dst, down_src, down_dst, sem):
        return (
            remote(up_src, up_dst, sem.at[0, 0], sem.at[1, 0], (f, coarse_at(1))),
            remote(down_src, down_dst, sem.at[0, 1], sem.at[1, 1], (f, coarse_at(-1))),
        )

    def summing(k, owners, block, src, got, quad, dst):
        sem, group_sem, last_sem = R.one_sem.at[k], R.two_sem.at[k], R.three_sem.at[k]
        mine = chunk(c, block)

        def owner(run):
            run() if owners == N_COARSE else pl.when(c < owners)(run)

        def other(run):
            if owners < N_COARSE:
                pl.when(c >= owners)(run)

        def group():
            return [
                remote(quad.at[f], quad.at[f], group_sem.at[0, d - 1], group_sem.at[1, d - 1], (fine_at(d), c))
                for d in range(1, N_FINE)
            ]

        def one():
            def send(d, carry):
                o = coarse_at(d)

                def go():
                    remote(src.at[chunk(o, block), :], got.at[mine, :], sem.at[0], sem.at[1], (f, o)).start()

                go() if owners == N_COARSE else pl.when(o < owners)(go)
                return carry

            lax.fori_loop(N_COARSE // 2, N_COARSE, send, 0)
            lax.fori_loop(1, N_COARSE // 2, send, 0)

        def two():
            def run():
                got[mine, :] = src[mine, :]
                wait_for(got.at[pl.ds(0, (owners - 1) * block), :], sem.at[0])
                wait_for(got.at[pl.ds(0, (N_COARSE - 1) * block), :], sem.at[1])
                parts = [got[j * block : (j + 1) * block, :].astype(F32) for j in range(N_COARSE)]
                while len(parts) > 1:
                    parts = [parts[j] + parts[j + 1] for j in range(0, len(parts), 2)]
                quad[f] = parts[0]
                for copy in group():
                    copy.start()

            owner(run)
            other(lambda: wait_for(got.at[pl.ds(0, owners * block), :], sem.at[0]))

        def three():
            def run():
                for copy in group():
                    copy.wait()
                dst[mine, :] = (quad[0] + quad[1]) + (quad[2] + quad[3])

                def send(d, carry):
                    o = coarse_at(d)
                    remote(dst.at[mine, :], dst.at[mine, :], last_sem.at[0], last_sem.at[1], (f, o)).start()
                    return carry

                lax.fori_loop(N_COARSE // 2, N_COARSE, send, 0)
                lax.fori_loop(1, N_COARSE // 2, send, 0)

            owner(run)

        def four():
            def run():
                wait_for(dst.at[pl.ds(0, (N_COARSE - 1) * block), :], last_sem.at[0])
                wait_for(dst.at[pl.ds(0, (owners - 1) * block), :], last_sem.at[1])

            owner(run)
            other(lambda: wait_for(dst.at[pl.ds(0, owners * block), :], last_sem.at[1]))

        return SimpleNamespace(one=one, two=two, three=three, four=four)

    def summing_set(s):
        first = LATE if s == 0 else 0
        count = SET - first
        work = summing(
            s, count // OWNED, OWNED, R.gw.at[s, pl.ds(first, count), :], R.got.at[s], R.quad.at[s], R.sums.at[s]
        )

        def end():
            work.four()
            O.sums[s, first:SET, :] = R.sums[s, 0:count, :]

        work.end = end
        return work

    total = [summing_set(s) for s in range(4)]
    late = summing(4, N_COARSE, 8, R.late, R.late_got, R.late_quad, R.late_sum)

    fine = SimpleNamespace(
        n=NF, used=NF + HALO, tab=NF + HALO, own=NF, e=EF, tile=1024, block=512, S=R.f, W=I.fw, first=0, masked=False
    )
    coarse = SimpleNamespace(
        n=NC, used=3 * NC, tab=512, own=256, e=EC, tile=EC, block=NC, S=R.c, W=I.cw, first=2, masked=True
    )

    def project_own(v, l):
        w, h = v.W.ei, v.S.layers[l].tab[0 : v.n, :]
        v.S.proj[0 : v.n, :] = dot(h, w[l, 128:256, :]).astype(BF)
        v.S.proj[v.tab : v.tab + v.n, :] = dot(h, w[l, 256:384, :]).astype(BF)

    def project_rest(v, l):
        rest = v.S.layers[l].tab[v.n : v.tab, :]
        v.S.proj[v.n : v.tab, :] = dot(rest, v.W.ei[l, 128:256, :]).astype(BF)

    def edge_base(l, h, edges):
        S, w = R.f, I.fw.ei
        S.wide[0:NF, :] = dot(h, w[l, 128:256, :])
        S.wide[NF : 2 * NF, :] = dot(h, w[l, 256:384, :])
        values = S.wide[0 : 2 * NF, :]
        scale = scale_for(column_peak(values))
        S.proj8[0 : 2 * NF, :] = halves(values, scale)

        def one(i, carry):
            rows = chunk(i, fine.tile)
            columns = ((S.cs[rows, :], 0, 0, NF), (S.cr[rows, :], 0, NF, NF))
            z = joined(gather_rows(columns, S.proj8), scale) + dot(edges[rows, :], w[l, 0:128, :])
            S.layers[l].slope[rows, :] = z
            return carry

        lax.fori_loop(0, EF // fine.tile, one, 0)

    def edge_delta(l, rows):
        S = R.f
        received = gather_rows(((S.cs[rows, :], NF, 2 * BLOCKS, HALO),), S.proj8)
        if l == 0:
            return received
        lanes = iota((16, L), 1).astype(I16)
        lanes = jnp.concatenate([lanes] * (fine.tile // 16), axis=0)
        hot = ones_where((R.block_s[rows, :] == lanes) | (R.block_r[rows, :] == lanes)).astype(F8)
        return dot(hot, S.proj8[0 : 2 * BLOCKS, :]) + received

    def forward(v, l, edges):
        S, W, A = v.S, v.W, v.S.layers[l]
        if not v.masked:
            scale = scale_for(column_peak(R.delta[...]))
            S.proj8[0 : 2 * BLOCKS + HALO, :] = halves(R.delta[...], scale)

        def one(i, peak):
            rows = chunk(i, v.tile)
            old = edges[rows, :]
            if v.masked:
                columns = ((S.cs[rows, :], 0, 0, v.tab), (S.cr[rows, :], 0, v.tab, v.own))
                z = gather_rows(columns, S.proj) + dot(old, W.ei[l, 0:128, :])
            else:
                z = A.slope[rows, :] + joined(edge_delta(l, rows), scale)
            gate = jax.nn.sigmoid(z)
            hidden = z * gate
            A.slope[rows, :] = gate * (1.0 + z - hidden)
            hidden = hidden.astype(BF)
            A.hid[rows, :] = hidden
            values, spread_by = normed(dot(hidden, W.eo[l]))
            A.n[rows, :] = values
            A.scale[rows, :] = jnp.broadcast_to(spread_by, values.shape)
            new = (old.astype(F32) + values).astype(BF)
            A.e[rows, :] = new
            return jnp.maximum(peak, column_peak(new.astype(F32)))

        peak = lax.fori_loop(0, v.e // v.tile, one, jnp.zeros((1, L), F32))
        if not v.masked:
            scale = scale_for(peak)

            def split(i, carry):
                rows = chunk(i, v.tile)
                S.e8[rows, :] = halves(A.e[rows, :].astype(F32), scale)
                return carry

            lax.fori_loop(0, v.e // v.tile, split, 0)

        def two(i, carry):
            rows = chunk(i, v.block)
            if v.masked:
                g = scatter_rows(S.rr, A.e, i * v.block, v.block, v.e)
            else:
                g = joined(scatter_rows(S.rr, S.e8, i * v.block, v.block, v.e), scale)
            A.g[rows, :] = g.astype(BF)
            return carry

        lax.fori_loop(0, v.n // v.block, two, 0)
        h = A.tab[0 : v.n, :]
        z = dot(h, W.ni[l, 0:128, :]) + dot(A.g[...], W.ni[l, 128:256, :])
        gate = jax.nn.sigmoid(z)
        hidden = z * gate
        A.slope2[...] = gate * (1.0 + z - hidden)
        hidden = hidden.astype(BF)
        A.hid2[...] = hidden
        values, spread_by = normed(dot(hidden, W.no[l]))
        A.n2[...] = values
        A.scale2[...] = jnp.broadcast_to(spread_by, values.shape)
        new = h.astype(F32) + values
        if v.masked:
            new = new * R.live[...]
        return new.astype(BF)

    def backward(v, l, edges, grad, edge_grad, send_rest, keep_edge, edges_done, parts_done):
        S, W, A = v.S, v.W, v.S.layers[l]
        s, acc, gw = v.first + l, v.S.acc, R.gw
        dn = grad.astype(F32)
        if v.masked:
            dn = dn * R.live[...]
        dy = normed_back(dn, A.n2[...], A.scale2[...]).astype(BF)
        dz = (dot_nt(dy, W.no[l]) * A.slope2[...]).astype(BF)
        S.ndy[...] = dy
        S.ndz[...] = dz
        dg = dot_nt(dz, W.ni[l, 128:256, :])
        if v.masked:
            S.dg[0 : v.n, :] = dg.astype(BF)
        else:
            dg_scale = scale_for(column_peak(dg))
            S.dg8[...] = halves(dg, dg_scale)
        acc[...] = dn + dot_nt(dz, W.ni[l, 0:128, :])

        def one(i, peak):
            rows = chunk(i, v.tile)
            columns = ((S.cr[rows, :], 0, 0, v.own),)
            if v.masked:
                dn = gather_rows(columns, S.dg)
            else:
                dn = joined(gather_rows(columns, S.dg8), dg_scale)
            if edge_grad is not None:
                dn = dn + edge_grad[rows, :].astype(F32)
            dy = normed_back(dn, A.n[rows, :], A.scale[rows, :]).astype(BF)
            dz = (dot_nt(dy, W.eo[l]) * A.slope[rows, :]).astype(BF)
            S.dy[rows, :] = dy
            S.dz[rows, :] = dz
            if keep_edge:
                S.de[rows, :] = dn.astype(BF)
            return jnp.maximum(peak, column_peak(dz.astype(F32)))

        peak = lax.fori_loop(0, v.e // v.tile, one, jnp.zeros((1, L), F32))

        def edge_weights():
            gw[s, 512:640, :] = dot_tn(A.tab[0 : v.n, :], S.ndz[...]).astype(BF)
            gw[s, 640:768, :] = dot_tn(A.g[...], S.ndz[...]).astype(BF)
            gw[s, 768:896, :] = dot_tn(A.hid2[...], S.ndy[...]).astype(BF)
            R.acc_b[...] = jnp.zeros((L, L), F32)
            R.acc_e[...] = jnp.zeros((L, L), F32)

            def add(i, carry):
                rows = chunk(i, v.tile)
                dz = S.dz[rows, :]
                R.acc_b[...] += dot_tn(A.hid[rows, :], S.dy[rows, :])
                R.acc_e[...] += dot_tn(edges[rows, :], dz)
                if keep_edge:
                    S.de[rows, :] = (S.de[rows, :].astype(F32) + dot_nt(dz, W.ei[l, 0:128, :])).astype(BF)
                return carry

            lax.fori_loop(0, v.e // v.tile, add, 0)
            gw[s, 256:384, :] = R.acc_e[...].astype(BF)
            gw[s, 384:512, :] = R.acc_b[...].astype(BF)

        def node_weights():
            gw[s, 0:128, :] = dot_tn(A.tab[0 : v.used, :], S.part[0 : v.used, :]).astype(BF)
            gw[s, 128:256, :] = dot_tn(A.tab[0 : v.n, :], S.other[...]).astype(BF)

        edges_done(edge_weights)
        if v.masked:

            def spread_back(rows_ref, first, count):
                return scatter_rows(rows_ref, S.dz, first, count, v.e).astype(BF)

        else:
            scale = scale_for(peak)

            def split(i, carry):
                rows = chunk(i, v.tile)
                S.e8[rows, :] = halves(S.dz[rows, :].astype(F32), scale)
                return carry

            lax.fori_loop(0, v.e // v.tile, split, 0)

            def spread_back(rows_ref, first, count):
                return joined(scatter_rows(rows_ref, S.e8, first, count, v.e), scale).astype(BF)

        rest = spread_back(S.rs, v.n, v.used - v.n)
        S.part[v.n : v.used, :] = rest
        send_rest(dot_nt(rest, W.ei[l, 128:256, :]).astype(BF))

        def two(i, carry):
            rows = chunk(i, v.block)
            S.part[rows, :] = spread_back(S.rs, i * v.block, v.block)
            S.other[rows, :] = spread_back(S.rr, i * v.block, v.block)
            return carry

        lax.fori_loop(0, v.n // v.block, two, 0)
        parts_done(node_weights)
        acc[...] += dot_nt(S.part[0 : v.n, :], W.ei[l, 128:256, :]) + dot_nt(S.other[...], W.ei[l, 256:384, :])
        return edge_weights, node_weights

    def place_column():
        return R.place[0][...]

    def place_wide():
        return jnp.broadcast_to(R.place[1][0:1, :], (WIDE, L))

    def pool_hot():
        return ones_where((iota((BLOCKS, NF), 1) >> 4) == iota((BLOCKS, NF), 0))

    def grow_hot():
        return ones_where((iota((NF, L), 0) >> 4) == iota((NF, L), 1))[:, 0:BLOCKS]

    def put_hot():
        return ones_where(iota((WIDE, L), 0) == place_wide())[:, 0:BLOCKS]

    def three_places(owner, rank):
        places = []
        for part, shift in ((0, 0), (1, 1), (2, N_COARSE - 1)):
            places.append(((owner + shift) & (N_COARSE - 1)) * PAD + part * CAP + rank)
        return places

    def put_three():
        wide = place_wide()
        down = iota((WIDE, L), 0)
        a, b, d = three_places(wide >> 4, wide & (PAD - 1))
        return ones_where((down == a) | (down == b) | (down == d))[:, 0:BLOCKS]

    def put_flags():
        row = ones_where(iota((WIDE, L), 0) == (place_wide() | (PAD - 1)))[:, 0:BLOCKS]
        lane = ones_where(iota((BLOCKS, L), 1) == (place_column() & (PAD - 1)))
        return dot(row, lane)

    def take_hot():
        return ones_where(jnp.concatenate([place_column()] * 4, axis=1) == iota((BLOCKS, WIDE), 1))

    def take_three():
        place = place_column()
        across = iota((BLOCKS, WIDE), 1)
        a, b, d = (jnp.concatenate([at] * 4, axis=1) for at in three_places(place >> 4, place & (PAD - 1)))
        return ones_where((across == a) | (across == b) | (across == d))

    def slot_of(index):
        within = index & (PAD - 1)
        return jnp.where(within < CAP, (index >> 4) * CAP + within, -1)

    def three_of(index):
        within = index & (PAD - 1)
        part = jnp.where(within >= 2 * CAP, 2, jnp.where(within >= CAP, 1, 0))
        return jnp.where(within < 3 * CAP, part * (NC - CAP) + (index >> 4) * CAP + within, -1)

    def across_hot(rows, places):
        down = iota((rows, 128), 0).astype(I16)
        parts = []
        for k in range(0, WIDE, 128):
            at = places(iota((16, 128), 1) + k).astype(I16)
            parts.append(ones_where(down == jnp.concatenate([at] * (rows // 16), axis=0)))
        return jnp.concatenate(parts, axis=1)

    def apart_hot(places, width):
        at = places(iota((WIDE, 128), 0)).astype(I16)
        lanes = iota((16, 128), 1).astype(I16)
        parts = []
        for k in range(0, width, 128):
            here = jnp.concatenate([lanes + jnp.asarray(k, I16)] * (WIDE // 16), axis=0)
            parts.append(ones_where(at == here))
        return jnp.concatenate(parts, axis=1)

    def flag_places():
        slot = iota((NC, WIDE), 0)
        first = (iota((NC, WIDE), 1) >> 4) * CAP
        last_row = (iota((NC, WIDE), 1) & (PAD - 1)) == PAD - 1
        row = ones_where(last_row & (slot >= first) & (slot < first + CAP))
        count = iota((NC, L), 0).astype(F32)
        within = iota((NC, L), 0) - jnp.floor((count + 0.5) * (1.0 / CAP)).astype(I32) * CAP
        return row, jnp.where(iota((NC, L), 1) == within, 1.0, 0.0)

    def build_hot():
        hot = R.hot
        hot.pool[...] = pool_hot()
        hot.grow[...] = grow_hot()
        hot.three[...] = put_three()
        hot.flags[...] = put_flags()
        hot.put[...] = put_hot()
        hot.take[...] = take_hot()
        hot.take_three[...] = take_three()
        hot.across[...] = across_hot(512, three_of)
        hot.narrow[...] = across_hot(NC, slot_of)
        hot.widen[...] = apart_hot(slot_of, 256)
        hot.apart[...] = apart_hot(three_of, 512)
        hot.flag_row[...], hot.flag_lane[...] = flag_places()

    def halo_pick(tab, k):
        R.hs[k][...] = gather_rows(((R.halo_col[...], 0, 0, NF),), tab).astype(BF)

    def halo_back(k):
        def send(values):
            R.hs[k][...] = values
            halo_start(R.hs[k], R.hr[k - 2], 0, R.hs_sem[k])

        return send

    def halo_add(k):
        halo_wait(R.hs[k], R.hr[k - 2], 0, R.hs_sem[k])

        def one(i, carry):
            rows = chunk(i, 512)
            R.f.acc[rows, :] += scatter_rows(R.halo_row, R.hr[k - 2], i * 512, 512, HALO)
            return carry

        lax.fori_loop(0, NF // 512, one, 0)

    def near_table():
        tab = R.c.layers[1].tab
        own = tab.at[pl.ds(0, NC), :]
        return near_copies(own, tab.at[pl.ds(NC, NC), :], own, tab.at[pl.ds(2 * NC, NC), :], R.near_sem[0])

    def near_grad():
        low, high = pl.ds(0, NC), pl.ds(NC, NC)
        return near_copies(
            R.ns.at[high, :], R.nr.at[low, :], R.ns.at[low, :], R.nr.at[high, :], R.near_sem[1]
        )

    def start(copies):
        for copy in copies:
            copy.start()

    def wait(copies):
        for copy in copies:
            copy.wait()

    later = []

    def nothing(run):
        pass

    def enter():
        greet()
        spread(I.halo, R.halo_col, R.halo_row, HALO // L)
        halo_pick(I.node, 0)
        spread(I.src, R.f.cs, R.f.rs, EF // L, R.block_s)
        spread(I.dst, R.f.cr, R.f.rr, EF // L, R.block_r, BLOCKS)
        edge_base(0, I.node[...], I.edge)
        pl.semaphore_wait(barrier, N_FINE - 1 + N_COARSE - 1)
        halo_start(R.hs[0], R.f.layers[0].tab, NF, R.hs_sem[0])

    def prepare():
        R.f.layers[0].tab[0:NF, :] = I.node[...]
        spread(I.csrc, R.c.cs, R.c.rs, EC // L)
        spread(I.cdst, R.c.cr, R.c.rr, EC // L)
        R.c.layers[1].tab[3 * NC : 512, :] = jnp.zeros((512 - 3 * NC, L), BF)
        R.parts[3 * NC : 512, :] = jnp.zeros((512 - 3 * NC, L), BF)
        R.c.proj[512 + NC : 768, :] = jnp.zeros((256 - NC, L), BF)
        R.c.dg[NC:256, :] = jnp.zeros((256 - NC, L), BF)
        R.delta[0 : 2 * BLOCKS, :] = jnp.zeros((2 * BLOCKS, L), F32)
        owner = jnp.broadcast_to(I.owner[...], (L, BLOCKS)).T
        below = jnp.full((L - BLOCKS, L), -1, I32)
        square = jnp.concatenate([owner, below], axis=0).T
        same = (owner == square[0:BLOCKS, :]) & (iota((BLOCKS, L), 1) < iota((BLOCKS, L), 0))
        rank = lane_sum(jnp.where(same, 1.0, 0.0)).astype(I32)
        place = owner * PAD + rank
        R.place[0][...] = place
        R.place[1][...] = jnp.concatenate([place, below], axis=0).T
        build_hot()

    def received(l):
        rows = R.f.layers[l].tab[NF : NF + HALO, :]
        R.delta[2 * BLOCKS :, :] = dot(rows, I.fw.ei[l, 128:256, :])

    def fine_zero():
        halo_wait(R.hs[0], R.f.layers[0].tab, NF, R.hs_sem[0])
        received(0)
        R.state_one[...] = forward(fine, 0, I.edge)

    def sink():
        pooled = (dot(R.hot.pool[...], R.state_one[...]) * (1.0 / POOL)).astype(BF)
        R.ws[0][...] = (dot(R.hot.three[...], pooled) + R.hot.flags[...]).astype(BF)
        wide_start(0)
        edge_base(1, R.state_one[...], R.f.layers[0].e)
        wide_wait(0)
        arrived = R.wr[0][...]
        R.c.layers[0].tab[...] = dot(R.hot.across[...], arrived).astype(BF)
        row = dot(R.hot.flag_row[...], arrived) * R.hot.flag_lane[...]
        R.live[...] = jnp.broadcast_to(lane_sum(row), (NC, L))

    def coarse_layer(l):
        def run():
            if l == 1:
                start(near_table())
            project_own(coarse, l)
            if l == 1:
                wait(near_table())
            project_rest(coarse, l)
            new = forward(coarse, l, I.cedge if l == 0 else R.c.layers[0].e)
            if l == 0:
                R.c.layers[1].tab[0:NC, :] = new
            else:
                R.ws[1][...] = dot(R.hot.widen[:, 0:NC], new).astype(BF)
                wide_start(1)

        return run

    def rise():
        wide_wait(1)
        picked = dot(R.hot.take[...], R.wr[1][...]).astype(BF)
        R.f.layers[1].tab[0:NF, :] = (R.state_one[...].astype(F32) + dot(R.hot.grow[...], picked)).astype(BF)
        halo_pick(R.f.layers[1].tab, 1)
        halo_start(R.hs[1], R.f.layers[1].tab, NF, R.hs_sem[1])
        w = I.fw.ei
        R.delta[0:BLOCKS, :] = dot(picked, w[1, 128:256, :])
        R.delta[BLOCKS : 2 * BLOCKS, :] = dot(picked, w[1, 256:384, :])
        halo_wait(R.hs[1], R.f.layers[1].tab, NF, R.hs_sem[1])
        received(1)

    def fine_one():
        O.new_state[...] = forward(fine, 1, R.f.layers[0].e)

    def fine_one_back():
        later[:] = backward(
            fine, 1, R.f.layers[0].e, I.cot[...], None, halo_back(2), True, nothing, nothing
        )

    def sink_back():
        halo_add(2)
        grad_two = R.f.acc[...].astype(BF)
        R.grad_two[...] = grad_two
        R.ws[2][...] = dot(R.hot.put[...], dot(R.hot.pool[...], grad_two).astype(BF)).astype(BF)
        wide_start(2)
        for run in later:
            run()
        total[1].one()
        wide_wait(2)
        R.grad_c[...] = dot(R.hot.narrow[...], R.wr[2][...]).astype(BF)

    def coarse_back(l):
        def run():
            def send(values):
                if l == 1:
                    R.ns[...] = values
                    start(near_grad())
                else:
                    R.parts[NC : 3 * NC, :] = values

            edges, edge_grad = (I.cedge, R.c.de) if l == 0 else (R.c.layers[0].e, None)
            weights = backward(
                coarse, l, edges, R.grad_c[...], edge_grad, send, l == 1, nothing, nothing
            )
            if l == 1:
                for run in weights:
                    run()
                total[3].one()
                wait(near_grad())
                total[1].two()
                grad = R.c.acc[...] + R.nr[0:NC, :].astype(F32) + R.nr[NC : 2 * NC, :].astype(F32)
                R.grad_c[...] = grad.astype(BF)
            else:
                R.parts[0:NC, :] = R.c.acc[...].astype(BF)
                R.ws[3][...] = dot(R.hot.apart[...], R.parts[...]).astype(BF)
                wide_start(3)
                for run in weights:
                    run()

        return run

    def rise_back():
        total[2].one()
        total[1].three()
        total[3].two()
        wide_wait(3)
        sunk = (dot(R.hot.take_three[...], R.wr[3][...]).astype(BF).astype(F32) * (1.0 / POOL)).astype(BF)
        R.grad_one[...] = (R.grad_two[...].astype(F32) + dot(R.hot.grow[...], sunk)).astype(BF)

    def fine_zero_back():
        def edges_done(edge_weights):
            edge_weights()
            total[0].one()
            total[2].two()
            total[3].three()

        def parts_done(node_weights):
            node_weights()
            R.late[...] = R.gw[0, 0:LATE, :].astype(F32)
            late.one()

        backward(fine, 0, I.edge, R.grad_one[...], R.f.de, halo_back(3), False, edges_done, parts_done)

    def leave():
        total[0].two()
        total[2].three()
        halo_add(3)
        O.state_grad[...] = R.f.acc[...].astype(BF)
        total[0].three()
        late.two()
        total[1].end()
        late.three()
        total[3].end()
        total[2].end()
        total[0].end()
        late.four()
        O.sums[0, 0:LATE, :] = R.late_sum[...]

    steps = (
        enter, prepare, fine_zero, sink, coarse_layer(0), coarse_layer(1), rise, fine_one, fine_one_back, sink_back,
        coarse_back(1), coarse_back(0), rise_back, fine_zero_back, leave,
    )
    for step in steps[:STEPS]:
        step()


def spread_out(state, grad, sums, *refs):
    outs, sem = refs[:-1], refs[-1]
    pairs = [(state, outs[0]), (grad, outs[1])]
    for s in range(4):
        ei, eo, ni, no = outs[2 + 4 * (s // 2) : 6 + 4 * (s // 2)]
        l = s % 2
        for out, there, here, rows in (
            (ei, 0, 256, 128), (ei, 128, 0, 256), (eo, 0, 384, 128), (ni, 0, 512, 256), (no, 0, 768, 128)
        ):
            pairs.append((sums.at[s, pl.ds(here, rows), :], out.at[l, pl.ds(there, rows), :]))
    copies = [pltpu.make_async_copy(src, dst, sem.at[k]) for k, (src, dst) in enumerate(pairs)]
    for copy in copies:
        copy.start()
    for copy in copies:
        copy.wait()


def body(*arrays):
    arrays = list(arrays)
    for i, rows in ((3, EF // L), (4, EF // L), (7, EC // L), (8, EC // L)):
        arrays[i] = arrays[i].reshape(rows, L)
    arrays[6] = arrays[6].reshape(1, BLOCKS)
    states = [jax.ShapeDtypeStruct((NF, L), BF)] * 2
    vm_spec = pl.BlockSpec(memory_space=pltpu.VMEM)
    any_spec = pl.BlockSpec(memory_space=pl.ANY)
    results = pl.pallas_call(
        kernel,
        out_shape=tuple(states + [jax.ShapeDtypeStruct((4, SET, L), F32)]),
        in_specs=[vm_spec] * len(arrays),
        out_specs=(vm_spec,) * 3,
        scratch_shapes=flat(shapes()),
        compiler_params=pltpu.CompilerParams(
            collective_id=0, has_side_effects=True, vmem_limit_bytes=60 * 2**20
        ),
        cost_estimate=pl.CostEstimate(flops=40 * 10**9, bytes_accessed=8 * 2**20, transcendentals=4 * 10**6),
    )(*arrays)
    outs = list(states)
    for _ in range(2):
        outs += [jax.ShapeDtypeStruct((2, rows, L), F32) for rows in (384, 128, 256, 128)]
    return pl.pallas_call(
        spread_out,
        out_shape=tuple(outs),
        in_specs=[vm_spec] * 3,
        out_specs=(any_spec,) * len(outs),
        scratch_shapes=[pltpu.SemaphoreType.DMA((22,))],
    )(*results)


def solution(mesh):
    rows = P(("fine", "coarse"), None)
    flat = P(("fine", "coarse"))
    placed = (rows, rows, rows, flat, flat, rows, rows, flat, flat, rows) + (P(),) * 8
    return jax.shard_map(
        body, mesh=mesh, in_specs=placed, out_specs=(rows, rows) + (P(),) * 8, check_vma=False
    )
```
